128 devices in a mesh: seq: 32 (over z_lo, y, x), dp: 4 (over z_hi, core).
Axes of the slice: x: 4, y: 4, z: 4 (z_hi: 2, z_lo: 2; z = z_hi * 2 + z_lo), core: 2. Of those that a mesh axis runs over, the one named last changes fastest.
Arguments:
- tokens: bfloat16 [4, 16384, 2240], P('dp', 'seq'), may hold values from -100 to 100
- modulation: float32 [4, 2, 2240], P('dp'), may hold values from -2.5 to 2.5
- weight: bfloat16 [2240, 3360], P('seq', 'dp'), may hold values from -0.375 to 0.375
- cotangent: bfloat16 [4, 16384, 1120], P('dp', 'seq'), may hold values from -6 to 6
Outputs:
- attention: bfloat16 [4, 16384, 1120], P('dp', 'seq')
- grad_tokens: bfloat16 [4, 16384, 2240], P('dp', 'seq')
- grad_weight: float32 [2240, 3360], P('seq', 'dp')
- grad_modulation: float32 [4, 2, 2240], P('dp')
The draws below stay inside these ranges and needn't reach their ends.
All inputs are finite; a program needn't handle non-finite values.
Results may differ from the reference program's by a relative error of at most 0.015.
Values may be sent and summed in bfloat16 or wider, within the bound.
No kernel may reach another device: no remote copies, remote signals or barrier semaphores. Data moves between devices by JAX's collectives and lax.ppermute only.
A program may use at most 128 MiB of HBM per device.

```python
import math
import jax
import jax.numpy as jnp
from jax import lax

D = 2240
HEADS = 35
HDIM = 32
TOK_DEV = 512
LEN = 16384
CLIPS = 4
N_SEQ = 32


def draw_tokens(key, part):
    key = jax.random.fold_in(key, 11)
    first = jax.random.fold_in(key, 0)
    second = jax.random.fold_in(key, 1)
    third = jax.random.fold_in(key, 2)
    fifth = jax.random.fold_in(key, 4)
    sixth = jax.random.fold_in(key, 5)
    seventh = jax.random.fold_in(key, 6)
    blocks = LEN // TOK_DEV
    position = jnp.arange(LEN, dtype=jnp.float32) / LEN
    ramp = (0.6 + 1.4 * position)[None, :, None]
    freq = jax.random.randint(fifth, (CLIPS, 1, 1), 1, 4).astype(jnp.float32)
    phase = jax.random.uniform(sixth, (CLIPS, 1, 1), jnp.float32, 0.0, 1.0)
    smooth = jnp.cos(2.0 * math.pi * (freq * position[None, :, None] + phase))
    common = jnp.clip(jax.random.normal(seventh, (CLIPS, 1, D), jnp.float32), -4.0, 4.0)
    directions = jnp.clip(jax.random.normal(first, (CLIPS, blocks, D), jnp.float32), -4.0, 4.0)
    rough = 0.25 * jnp.clip(jax.random.normal(second, (CLIPS, LEN, 1), jnp.float32), -4.0, 4.0)
    noise = jnp.clip(jax.random.normal(third, (CLIPS, LEN, D), jnp.float32), -4.0, 4.0)
    amplitude = ramp * (1.6 + 0.5 * smooth + rough)
    per_token = jnp.repeat(directions, TOK_DEV, axis=1) + common
    values = jnp.clip(amplitude * per_token + noise, -96.0, 96.0)
    return values.astype(jnp.bfloat16)


def level_of(rng, extent, cuts, least, high):
    def one(dim, blocks):
        draws = jax.random.uniform(jax.random.fold_in(jax.random.fold_in(rng, 6), dim), (blocks,), jnp.float32, least / len(cuts), high / len(cuts))
        return jnp.repeat(jnp.exp(draws), extent[dim] // blocks).reshape((-1,) + (1,) * (len(extent) - dim - 1))

    level = one(*cuts[0])
    for cut in cuts[1:]:
        level = level * one(*cut)
    return level


def gaussian(key, extent, spread, reach, pieces=(), kind=jnp.bfloat16):
    factor_of = level_of(key, extent, pieces, -0.22, 0.18) if pieces else 1.0
    drawn = jax.random.normal(key, extent, jnp.float32) * spread * factor_of
    return jnp.minimum(jnp.maximum(drawn, -reach), reach).astype(kind)


def setup_inputs(seed: int = 0) -> dict:
    arg_keys = jax.random.split(jax.random.key(seed), 5)
    tokens = draw_tokens(jax.random.fold_in(arg_keys[4], 71), 0)
    modulation = gaussian(arg_keys[1], (CLIPS, 2, D), 0.5, 2.5, ((0, 4),), jnp.float32)
    weight = gaussian(arg_keys[2], (D, 3 * HEADS * HDIM), (D // 9) ** -0.5, 0.375, ((0, 32), (1, 4)))
    cotangent = gaussian(arg_keys[3], (CLIPS, LEN, HEADS * HDIM), 1.0, 6.0, ((0, 4), (1, 32)))
    return {"tokens": tokens, "modulation": modulation, "weight": weight, "cotangent": cotangent}


HIGH = lax.Precision.HIGHEST

def modulate(values_in, mods):
    values = values_in.astype(jnp.float32)
    inverse = lax.rsqrt(lax.optimization_barrier(jnp.mean(values * values, axis=-1, keepdims=True)) + 1e-06)
    normed = values * inverse
    hidden = (normed * (1.0 + mods[1]) + mods[0]).astype(jnp.bfloat16)
    return (inverse, normed, hidden)

def feature(values_in):
    values = values_in.astype(jnp.float32)
    lower = jnp.exp(jnp.minimum(values, 0.0))
    return (jnp.where(values > 0, values + 1.0, lower), jnp.where(values > 0, 1.0, lower))

def clip_pass(clip_tokens, mods, clip_cot, weight):
    count = clip_tokens.shape[0]
    inverse, normed, hidden = modulate(clip_tokens, mods)
    qkv = jnp.dot(hidden, weight, preferred_element_type=jnp.float32).astype(jnp.bfloat16)
    heads = qkv.reshape(count, 3, HEADS, HDIM)
    query, keys, values = (heads[:, 0], heads[:, 1], heads[:, 2])
    key_pos, key_slope = feature(keys)
    values32 = values.astype(jnp.float32)
    state = jnp.einsum('the,thf->hef', key_pos, values32, precision=HIGH)
    key_total = lax.optimization_barrier(jnp.sum(key_pos, axis=0))
    query_pos, query_slope = feature(query)
    numer = jnp.einsum('the,hef->thf', query_pos, state, precision=HIGH)
    denom = jnp.einsum('the,he->th', query_pos, key_total, precision=HIGH) + 1.0
    quotient = numer / denom[..., None]
    attention = quotient.reshape(count, HEADS * HDIM).astype(jnp.bfloat16)
    grad_out = clip_cot.astype(jnp.float32).reshape(count, HEADS, HDIM)
    grad_numer = grad_out / denom[..., None]
    grad_denom = -lax.optimization_barrier(jnp.sum(grad_out * quotient, axis=-1)) / denom
    state_grad = jnp.einsum('the,thf->hef', query_pos, grad_numer, precision=HIGH)
    total_grad = jnp.einsum('the,th->he', query_pos, grad_denom, precision=HIGH)
    grad_query = jnp.einsum('thf,hef->the', grad_numer, state, precision=HIGH) + grad_denom[..., None] * key_total
    grad_query = query_slope * grad_query
    grad_keys = jnp.einsum('thf,hef->the', values32, state_grad, precision=HIGH) + total_grad
    grad_keys = key_slope * grad_keys
    grad_values = jnp.einsum('the,hef->thf', key_pos, state_grad, precision=HIGH)
    grad_qkv = jnp.stack([grad_query, grad_keys, grad_values], axis=1).reshape(count, -1).astype(jnp.bfloat16)
    grad_hidden = lax.dot_general(grad_qkv, weight, (((1,), (1,)), ((), ())), preferred_element_type=jnp.float32)
    mod_grad = jnp.stack([lax.optimization_barrier(jnp.sum(grad_hidden, axis=0)), lax.optimization_barrier(jnp.sum(grad_hidden * normed, axis=0))])
    mod_grad = mod_grad * (1.0 / math.sqrt(LEN))
    grad_normed = grad_hidden * (1.0 + mods[1])
    grad_tokens = inverse * (grad_normed - normed * lax.optimization_barrier(jnp.mean(grad_normed * normed, axis=-1, keepdims=True)))
    hidden_blocks = hidden.reshape(N_SEQ, TOK_DEV, D)
    grad_blocks = grad_qkv.reshape(N_SEQ, TOK_DEV, -1)

    def block_step(total, pair):
        term = lax.dot_general(pair[0], pair[1], (((0,), (0,)), ((), ())), preferred_element_type=jnp.float32)
        rounded = lax.optimization_barrier(term.astype(jnp.bfloat16))
        return (total + rounded.astype(jnp.float32), None)
    start = jnp.zeros((D, 3 * HEADS * HDIM), jnp.float32)
    weight_grad, unused = lax.scan(block_step, start, (hidden_blocks, grad_blocks))
    return (attention, grad_tokens.astype(jnp.bfloat16), weight_grad, mod_grad)

def reference(tokens, modulation, weight, cotangent):
    attention_list = []
    grad_list = []
    mod_list = []
    weight_grad = jnp.zeros((D, 3 * HEADS * HDIM), jnp.float32)
    for clip in range(CLIPS):
        attention, grad_tokens, clip_weight_grad, mod_grad = clip_pass(tokens[clip], modulation[clip], cotangent[clip], weight)
        attention_list.append(attention)
        grad_list.append(grad_tokens)
        mod_list.append(mod_grad)
        weight_grad = weight_grad + clip_weight_grad
    weight_grad = weight_grad * (1.0 / math.sqrt(CLIPS * LEN))
    return (jnp.stack(attention_list), jnp.stack(grad_list), weight_grad, jnp.stack(mod_list))
```

```python
import math

import jax
import jax.numpy as jnp
from jax import lax
from jax.sharding import PartitionSpec as P

HDIM = 32
HIGH = lax.Precision.HIGHEST
AXES = ("seq", "dp")
ROWS = 70
UNIT = 144
COLS = 840


def place(index):
    seq, dp = divmod(index, 4)
    z_lo, rest = divmod(seq, 16)
    y, x = divmod(rest, 4)
    z_hi, core = divmod(dp, 2)
    return x, y, z_hi * 2 + z_lo, core


def index_of(x, y, z, core):
    x, y, z = x % 4, y % 4, z % 4
    return ((z % 2) * 16 + y * 4 + x) * 4 + (z // 2) * 2 + core


def route(kind, offset):
    pairs = []
    for index in range(128):
        x, y, z, core = place(index)
        if kind == "z":
            target = index_of(x, y, z + offset, core)
        elif kind == "z_lo":
            target = index_of(x, y, z ^ 1, core)
        elif kind == "core":
            target = index_of(x, y, z, 1 - core)
        elif (kind == "last") == (core == 0):
            target = index_of(x + offset, y, z, core)
        else:
            target = index_of(x, y + offset, z, core)
        pairs.append((index, target))
    return pairs


def send(value, kind, offset=0):
    return lax.ppermute(value, AXES, route(kind, offset))


def ring_gather(block, half, kind):
    ahead = send(block, kind, -1)
    behind = send(block, kind, 1)
    far_first = send(ahead[:half], kind, -1)
    far_second = send(behind[half:], kind, 1)
    return block, ahead, far_first, far_second, behind


def add(left, right):
    return (left.astype(jnp.float32) + right.astype(jnp.float32)).astype(jnp.bfloat16)


def ring_scatter(shards, half, kind):
    far_first = send(shards[2][:half], kind, 1)
    far_second = send(shards[2][half:], kind, -1)
    ahead = jnp.concatenate([add(shards[1][:half], far_first), shards[1][half:]])
    behind = jnp.concatenate([shards[3][:half], add(shards[3][half:], far_second)])
    from_behind = send(ahead, kind, 1)
    from_ahead = send(behind, kind, -1)
    total = shards[0].astype(jnp.float32) + from_behind.astype(jnp.float32) + from_ahead.astype(jnp.float32)
    return total.astype(jnp.bfloat16)


def seq_sum(value):
    for kind in ("last", "middle"):
        far = send(value, kind, 2)
        ahead = send(value, kind, -1)
        behind = send(value, kind, 1)
        value = (value + far) + (ahead + behind)
    return value + send(value, "z_lo")


def gather_weight(weight, z):
    relative = [weight, send(weight, "z", -1), send(weight, "z", -2), send(weight, "z", 1)]
    relative = jnp.stack(relative + relative[:3])
    blocks = lax.dynamic_slice_in_dim(relative, lax.rem(4 - z, 4), 4, axis=0)
    unit = jnp.concatenate(
        [
            jnp.concatenate([blocks[0], blocks[1]], axis=0),
            jnp.concatenate([blocks[2], blocks[3]], axis=0),
        ],
        axis=1,
    )
    unit = jnp.pad(unit, ((0, UNIT - 2 * ROWS), (0, 0)))
    own, ahead, far_first, far_second, behind = ring_gather(unit, UNIT // 2, "middle")
    group = jnp.stack([own, ahead, jnp.concatenate([far_first, far_second]), behind])
    pieces = ring_gather(group, 2, "last")
    others = [send(piece, "core") for piece in pieces]
    mine = jnp.concatenate(pieces).reshape(16 * UNIT, 2 * COLS)
    other = jnp.concatenate(others).reshape(4, 4, UNIT, 2 * COLS)
    other = other.transpose(1, 0, 2, 3).reshape(16 * UNIT, 2 * COLS)
    return mine, other


def scatter_weight(mine, other, z):
    shape = (4, 4, UNIT, 2 * COLS)
    received = send(other, "core").reshape(shape)
    mine = mine.reshape(shape)
    shards = [add(mine[j], received[:, j]) for j in range(4)]
    group = ring_scatter(shards, 2, "last")
    unit = ring_scatter([group[j] for j in range(4)], UNIT // 2, "middle")
    blocks = jnp.stack(
        [
            unit[:ROWS, :COLS],
            unit[ROWS : 2 * ROWS, :COLS],
            unit[:ROWS, COLS:],
            unit[ROWS : 2 * ROWS, COLS:],
        ]
    )
    relative = lax.dynamic_slice_in_dim(jnp.concatenate([blocks, blocks[:3]]), z, 4, axis=0)
    ahead = send(relative[1], "z", 1)
    far = send(relative[2], "z", 2)
    behind = send(relative[3], "z", -1)
    return (relative[0].astype(jnp.float32) + far.astype(jnp.float32)) + (
        ahead.astype(jnp.float32) + behind.astype(jnp.float32)
    )


def arrival_order(x, y, core, features):
    row = lax.broadcasted_iota(jnp.int32, (1, 16 * UNIT), 1)
    last, middle, inner = row // (4 * UNIT), (row // UNIT) % 4, row % UNIT
    at_x = lax.rem(x + jnp.where(core == 0, last, middle), 4)
    at_y = lax.rem(y + jnp.where(core == 0, middle, last), 4)
    z_lo = inner // ROWS
    feature_index = (z_lo * 16 + at_y * 4 + at_x) * ROWS + inner % ROWS
    feature_index = jnp.where(inner < 2 * ROWS, feature_index, -1)
    return (lax.broadcasted_iota(jnp.int32, (features, 1), 0) == feature_index).astype(jnp.bfloat16)


def feature(values_in):
    values = values_in.astype(jnp.float32)
    lower = jnp.exp(jnp.minimum(values, 0.0))
    return (jnp.where(values > 0, values + 1.0, lower), jnp.where(values > 0, 1.0, lower))


def pack(state, total):
    flat = jnp.concatenate([state.reshape(-1), total.reshape(-1)])
    return jnp.pad(flat, (0, -flat.shape[0] % 1024)).reshape(-1, 128)


def unpack(packed, heads):
    flat = packed.reshape(-1)
    cut = heads * HDIM * HDIM
    return flat[:cut].reshape(heads, HDIM, HDIM), flat[cut : cut + heads * HDIM].reshape(heads, HDIM)


def body(tokens, modulation, weight, cotangent):
    seq, dp = lax.axis_index("seq"), lax.axis_index("dp")
    x, y = lax.rem(seq, 4), lax.rem(seq // 4, 4)
    z, core = (dp // 2) * 2 + seq // 16, lax.rem(dp, 2)
    count, features = tokens.shape[1:]
    clip_length = count * lax.axis_size("seq")
    all_length = clip_length * lax.axis_size("dp")

    mine, other = gather_weight(weight, z)

    order = arrival_order(x, y, core, features)
    local = jnp.dot(tokens[0], order, preferred_element_type=jnp.float32)
    mods = jnp.dot(modulation[0], order.astype(jnp.float32), precision=HIGH)
    inverse = lax.rsqrt(jnp.sum(local * local, axis=-1, keepdims=True) * (1.0 / features) + 1e-06)
    normed = local * inverse
    hidden = (normed * (1.0 + mods[1]) + mods[0]).astype(jnp.bfloat16)

    qkv_mine = jnp.dot(hidden, mine, preferred_element_type=jnp.float32).astype(jnp.bfloat16)
    qkv_other = jnp.dot(hidden, other, preferred_element_type=jnp.float32).astype(jnp.bfloat16)
    even = jnp.where(core == 0, qkv_mine, qkv_other)
    odd = jnp.where(core == 0, qkv_other, qkv_mine)
    qkv = jnp.concatenate([even[:, :COLS], odd[:, :COLS], even[:, COLS:], odd[:, COLS:]], axis=1)

    head_count = qkv.shape[1] // (3 * HDIM)
    heads = qkv.reshape(count, 3, head_count, HDIM)
    query, keys, values = (heads[:, 0], heads[:, 1], heads[:, 2])
    key_pos, key_slope = feature(keys)
    values32 = values.astype(jnp.float32)
    state_local = jnp.einsum("the,thf->hef", key_pos, values32, precision=HIGH)
    total_local = jnp.sum(key_pos, axis=0)
    state, key_total = unpack(seq_sum(pack(state_local, total_local)), head_count)
    query_pos, query_slope = feature(query)
    numer = jnp.einsum("the,hef->thf", query_pos, state, precision=HIGH)
    denom = jnp.einsum("the,he->th", query_pos, key_total, precision=HIGH) + 1.0
    quotient = numer / denom[..., None]
    attention = quotient.reshape(count, head_count * HDIM).astype(jnp.bfloat16)
    grad_out = cotangent[0].astype(jnp.float32).reshape(count, head_count, HDIM)
    grad_numer = grad_out / denom[..., None]
    grad_denom = -jnp.sum(grad_out * quotient, axis=-1) / denom
    state_grad_local = jnp.einsum("the,thf->hef", query_pos, grad_numer, precision=HIGH)
    total_grad_local = jnp.einsum("the,th->he", query_pos, grad_denom, precision=HIGH)
    state_grad, total_grad = unpack(seq_sum(pack(state_grad_local, total_grad_local)), head_count)
    grad_query = (
        jnp.einsum("thf,hef->the", grad_numer, state, precision=HIGH)
        + grad_denom[..., None] * key_total
    )
    grad_query = query_slope * grad_query
    grad_keys = jnp.einsum("thf,hef->the", values32, state_grad, precision=HIGH) + total_grad
    grad_keys = key_slope * grad_keys
    grad_values = jnp.einsum("the,hef->thf", key_pos, state_grad, precision=HIGH)
    grad_qkv = (
        jnp.stack([grad_query, grad_keys, grad_values], axis=1)
        .reshape(count, -1)
        .astype(jnp.bfloat16)
    )
    even = jnp.concatenate([grad_qkv[:, :COLS], grad_qkv[:, 2 * COLS : 3 * COLS]], axis=1)
    odd = jnp.concatenate([grad_qkv[:, COLS : 2 * COLS], grad_qkv[:, 3 * COLS :]], axis=1)
    grad_mine = jnp.where(core == 0, even, odd)
    grad_other = jnp.where(core == 0, odd, even)

    def weight_term(grad):
        term = lax.dot_general(hidden, grad, (((0,), (0,)), ((), ())), preferred_element_type=jnp.float32)
        return term.astype(jnp.bfloat16)

    term_other = weight_term(grad_other)
    term_mine = weight_term(grad_mine)
    weight_grad = scatter_weight(term_mine, term_other, z) * (1.0 / math.sqrt(all_length))

    def back(grad, rows):
        return lax.dot_general(grad, rows, (((1,), (1,)), ((), ())), preferred_element_type=jnp.float32)

    grad_hidden = back(grad_mine, mine) + back(grad_other, other)
    mod_local = jnp.stack([jnp.sum(grad_hidden, axis=0), jnp.sum(grad_hidden * normed, axis=0)])
    mod_local = lax.dot_general(
        mod_local, order.astype(jnp.float32), (((1,), (1,)), ((), ())), precision=HIGH
    )
    mod_grad = seq_sum(mod_local) * (1.0 / math.sqrt(clip_length))
    grad_normed = grad_hidden * (1.0 + mods[1])
    mean = jnp.sum(grad_normed * normed, axis=-1, keepdims=True) * (1.0 / features)
    grad_tokens = (inverse * (grad_normed - normed * mean)).astype(jnp.bfloat16)
    grad_tokens = lax.dot_general(
        grad_tokens, order, (((1,), (1,)), ((), ())), preferred_element_type=jnp.float32
    ).astype(jnp.bfloat16)
    return (attention[None], grad_tokens[None], weight_grad, mod_grad[None])


def solution(mesh):
    return jax.shard_map(
        body,
        mesh=mesh,
        in_specs=(P("dp", "seq", None), P("dp", None, None), P("seq", "dp"), P("dp", "seq", None)),
        out_specs=(P("dp", "seq", None), P("dp", "seq", None), P("seq", "dp"), P("dp", None, None)),
        check_vma=False,
    )
```

```python
import math

import jax
import jax.numpy as jnp
from jax import lax
from jax.sharding import PartitionSpec as P

HDIM = 32
HIGH = lax.Precision.HIGHEST
AXES = ("seq", "dp")
ROWS = 70
UNIT = 144
COLS = 840
HALF = 576


def place(index):
    seq, dp = divmod(index, 4)
    z_lo, rest = divmod(seq, 16)
    y, x = divmod(rest, 4)
    z_hi, core = divmod(dp, 2)
    return x, y, z_hi * 2 + z_lo, core


def index_of(x, y, z, core):
    x, y, z = x % 4, y % 4, z % 4
    return ((z % 2) * 16 + y * 4 + x) * 4 + (z // 2) * 2 + core


def route(kind, offset):
    pairs = []
    for index in range(128):
        x, y, z, core = place(index)
        if kind == "z":
            target = index_of(x, y, z + offset, core)
        elif kind == "z_lo":
            target = index_of(x, y, z ^ 1, core)
        elif kind == "core":
            target = index_of(x, y, z, 1 - core)
        elif (kind == "last") == (core == 0):
            target = index_of(x + offset, y, z, core)
        else:
            target = index_of(x, y + offset, z, core)
        pairs.append((index, target))
    return pairs


def send(value, kind, offset=0):
    return lax.ppermute(value, AXES, route(kind, offset))


def ring_gather(block, half, kind):
    ahead = send(block, kind, -1)
    behind = send(block, kind, 1)
    far_first = send(ahead[:half], kind, -1)
    far_second = send(behind[half:], kind, 1)
    return block, ahead, far_first, far_second, behind


def ring_gather_halves(block, half, kind):
    first, second = block[:half], block[half:]
    ahead_first = send(first, kind, -1)
    behind_second = send(second, kind, 1)
    ahead_second = send(second, kind, -1)
    behind_first = send(first, kind, 1)
    far_first = send(ahead_first, kind, -1)
    far_second = send(behind_second, kind, 1)
    return block, ahead_first, ahead_second, far_first, far_second, behind_first, behind_second


def add(left, right):
    return (left.astype(jnp.float32) + right.astype(jnp.float32)).astype(jnp.bfloat16)


def ring_scatter(shards, half, kind):
    far_first = send(shards[2][:half], kind, 1)
    far_second = send(shards[2][half:], kind, -1)
    plain_ahead = send(shards[1][half:], kind, 1)
    plain_behind = send(shards[3][:half], kind, -1)
    summed_ahead = send(add(shards[1][:half], far_first), kind, 1)
    summed_behind = send(add(shards[3][half:], far_second), kind, -1)
    own = shards[0].astype(jnp.float32)
    first = own[:half] + summed_ahead.astype(jnp.float32) + plain_behind.astype(jnp.float32)
    second = own[half:] + plain_ahead.astype(jnp.float32) + summed_behind.astype(jnp.float32)
    return jnp.concatenate([first, second]).astype(jnp.bfloat16)


def seq_sum(value):
    for kind in ("last", "middle"):
        far = send(value, kind, 2)
        ahead = send(value, kind, -1)
        behind = send(value, kind, 1)
        value = (value + far) + (ahead + behind)
    return value + send(value, "z_lo")


def pick(core, on_zero, on_one):
    return jnp.where(core == 0, on_zero, on_one)


def head_half(array, core, other=False):
    width = array.shape[-1]
    low, high = array[..., :HALF], array[..., width - HALF :]
    return pick(core, high, low) if other else pick(core, low, high)


def head_join(mine, other, core):
    return jnp.concatenate([pick(core, mine, other), pick(core, other, mine)[..., HDIM:]], axis=-1)


def gather_units(weight, z, core):
    relative = [weight, send(weight, "z", -1), send(weight, "z", -2), send(weight, "z", 1)]
    relative = jnp.stack(relative + relative[:3])
    blocks = lax.dynamic_slice_in_dim(relative, lax.rem(4 - z, 4), 4, axis=0)
    others = send(blocks, "core")
    even, odd = pick(core, blocks, others), pick(core, others, blocks)
    columns = jnp.concatenate([even[:2], odd[:2], even[2:], odd[2:]], axis=2)
    columns = columns.reshape(2 * ROWS, 4 * COLS)
    columns = jnp.pad(columns, ((0, UNIT - 2 * ROWS), (0, 0)))
    third = 4 * COLS // 3
    query, keys, values = (head_half(columns[:, i * third : (i + 1) * third], core) for i in range(3))
    return jnp.concatenate([keys, values], axis=1), query


def gather_rows(unit, width):
    own, ahead, far_first, far_second, behind = ring_gather(unit, UNIT // 2, "middle")
    group = jnp.stack([own, ahead, jnp.concatenate([far_first, far_second]), behind])
    pieces = ring_gather_halves(group, 2, "last")
    return jnp.concatenate(pieces).reshape(16 * UNIT, width)


def scatter_rows(term):
    shards = term.reshape(4, 4, UNIT, term.shape[1])
    group = ring_scatter([shards[j] for j in range(4)], 2, "last")
    return ring_scatter([group[j] for j in range(4)], UNIT // 2, "middle")


def scatter_units(query, pair, z, core):
    other_query, other_pair = send(query, "core"), send(pair, "core")
    columns = jnp.concatenate(
        [
            head_join(query, other_query, core),
            head_join(pair[:, :HALF], other_pair[:, :HALF], core),
            head_join(pair[:, HALF:], other_pair[:, HALF:], core),
        ],
        axis=1,
    )
    low = pick(core, columns[:, :COLS], columns[:, COLS : 2 * COLS])
    high = pick(core, columns[:, 2 * COLS : 3 * COLS], columns[:, 3 * COLS :])
    blocks = jnp.stack([low[:ROWS], low[ROWS : 2 * ROWS], high[:ROWS], high[ROWS : 2 * ROWS]])
    relative = lax.dynamic_slice_in_dim(jnp.concatenate([blocks, blocks[:3]]), z, 4, axis=0)
    ahead = send(relative[1], "z", 1)
    far = send(relative[2], "z", 2)
    behind = send(relative[3], "z", -1)
    return (relative[0].astype(jnp.float32) + far.astype(jnp.float32)) + (
        ahead.astype(jnp.float32) + behind.astype(jnp.float32)
    )


def arrival_order(x, y, core, features):
    row = lax.broadcasted_iota(jnp.int32, (1, 16 * UNIT), 1)
    last, middle, inner = row // (4 * UNIT), (row // UNIT) % 4, row % UNIT
    at_x = lax.rem(x + jnp.where(core == 0, last, middle), 4)
    at_y = lax.rem(y + jnp.where(core == 0, middle, last), 4)
    z_lo = inner // ROWS
    feature_index = (z_lo * 16 + at_y * 4 + at_x) * ROWS + inner % ROWS
    feature_index = jnp.where(inner < 2 * ROWS, feature_index, -1)
    return (lax.broadcasted_iota(jnp.int32, (features, 1), 0) == feature_index).astype(jnp.bfloat16)


def feature(values_in):
    values = values_in.astype(jnp.float32)
    lower = jnp.exp(jnp.minimum(values, 0.0))
    return (jnp.where(values > 0, values + 1.0, lower), jnp.where(values > 0, 1.0, lower))


def pack(state, total):
    flat = jnp.concatenate([state.reshape(-1), total.reshape(-1)])
    return jnp.pad(flat, (0, -flat.shape[0] % 1024)).reshape(-1, 128)


def unpack(packed):
    flat = packed.reshape(-1)
    heads = HALF // HDIM
    cut = 2 * heads * HDIM * HDIM
    state = flat[:cut].reshape(2, heads, HDIM, HDIM)
    return state, flat[cut : cut + 2 * heads * HDIM].reshape(2, heads, HDIM)


def body(tokens, modulation, weight, cotangent):
    seq, dp = lax.axis_index("seq"), lax.axis_index("dp")
    x, y = lax.rem(seq, 4), lax.rem(seq // 4, 4)
    z, core = (dp // 2) * 2 + seq // 16, lax.rem(dp, 2)
    count, features = tokens.shape[1:]
    clip_length = count * lax.axis_size("seq")
    all_length = clip_length * lax.axis_size("dp")

    unit_pair, unit_query = gather_units(weight, z, core)
    rows_pair = gather_rows(unit_pair, 2 * HALF)
    rows_query = gather_rows(unit_query, HALF)

    order = arrival_order(x, y, core, features)
    both = jnp.concatenate([tokens, send(tokens, "core")])
    both_mods = jnp.concatenate([modulation, send(modulation, "core")])
    grad_out = cotangent[0]
    grad_out = jnp.stack(
        [head_half(grad_out, core), send(head_half(grad_out, core, other=True), "core")]
    )

    local = jnp.dot(both.reshape(2 * count, features), order, preferred_element_type=jnp.float32)
    local = local.reshape(2, count, 16 * UNIT)
    mods = jnp.dot(both_mods.reshape(4, features), order.astype(jnp.float32), precision=HIGH)
    mods = mods.reshape(2, 2, 1, 16 * UNIT)
    inverse = lax.rsqrt(jnp.sum(local * local, axis=-1, keepdims=True) * (1.0 / features) + 1e-06)
    hidden = (local * inverse * (1.0 + mods[:, 1]) + mods[:, 0]).astype(jnp.bfloat16)
    hidden = hidden.reshape(2 * count, 16 * UNIT)

    def heads_of(array):
        return array.reshape(2, count, HALF // HDIM, HDIM)

    pair = jnp.dot(hidden, rows_pair, preferred_element_type=jnp.float32).astype(jnp.bfloat16)
    key_pos, key_slope = feature(heads_of(pair[:, :HALF]))
    values32 = heads_of(pair[:, HALF:]).astype(jnp.float32)
    state_local = jnp.einsum("bthe,bthf->bhef", key_pos, values32, precision=HIGH)
    total_local = jnp.sum(key_pos, axis=1)
    state, key_total = unpack(seq_sum(pack(state_local, total_local)))

    query = jnp.dot(hidden, rows_query, preferred_element_type=jnp.float32).astype(jnp.bfloat16)
    query_pos, query_slope = feature(heads_of(query))
    numer = jnp.einsum("bthe,bhef->bthf", query_pos, state, precision=HIGH)
    denom = jnp.einsum("bthe,bhe->bth", query_pos, key_total, precision=HIGH) + 1.0
    quotient = numer / denom[..., None]
    attention = quotient.reshape(2, count, HALF).astype(jnp.bfloat16)
    attention = head_join(attention[0], send(attention[1], "core"), core)
    grad_out = heads_of(grad_out.astype(jnp.float32))
    grad_numer = grad_out / denom[..., None]
    grad_denom = -jnp.sum(grad_out * quotient, axis=-1) / denom
    state_grad_local = jnp.einsum("bthe,bthf->bhef", query_pos, grad_numer, precision=HIGH)
    total_grad_local = jnp.einsum("bthe,bth->bhe", query_pos, grad_denom, precision=HIGH)
    state_grad, total_grad = unpack(seq_sum(pack(state_grad_local, total_grad_local)))
    once = (lax.broadcasted_iota(jnp.int32, (1, HALF), 1) >= HDIM) | (core == 0)

    def joined(array):
        return jnp.where(once, array.reshape(2 * count, HALF), 0.0).astype(jnp.bfloat16)

    def weight_term(grad):
        term = lax.dot_general(hidden, grad, (((0,), (0,)), ((), ())), preferred_element_type=jnp.float32)
        return term.astype(jnp.bfloat16)

    def back(grad, rows):
        return lax.dot_general(grad, rows, (((1,), (1,)), ((), ())), preferred_element_type=jnp.float32)

    grad_query = (
        jnp.einsum("bthf,bhef->bthe", grad_numer, state, precision=HIGH)
        + grad_denom[..., None] * key_total[:, None]
    )
    grad_query = joined(query_slope * grad_query)
    part_query = scatter_rows(weight_term(grad_query))
    grad_keys = jnp.einsum("bthf,bhef->bthe", values32, state_grad, precision=HIGH)
    grad_keys = key_slope * (grad_keys + total_grad[:, None])
    grad_values = jnp.einsum("bthe,bhef->bthf", key_pos, state_grad, precision=HIGH)
    grad_pair = jnp.concatenate([joined(grad_keys), joined(grad_values)], axis=1)
    part_pair = scatter_rows(weight_term(grad_pair))
    weight_grad = scatter_units(part_query, part_pair, z, core) * (1.0 / math.sqrt(all_length))

    partial = (back(grad_query, rows_query) + back(grad_pair, rows_pair)).astype(jnp.bfloat16)
    partial = back(partial, order).astype(jnp.bfloat16).reshape(2, count, features)
    grad_hidden = partial[0].astype(jnp.float32) + send(partial[1], "core").astype(jnp.float32)
    values = tokens[0].astype(jnp.float32)
    inverse = lax.rsqrt(jnp.mean(values * values, axis=-1, keepdims=True) + 1e-06)
    normed = values * inverse
    mod_local = jnp.stack([jnp.sum(grad_hidden, axis=0), jnp.sum(grad_hidden * normed, axis=0)])
    mod_grad = seq_sum(mod_local) * (1.0 / math.sqrt(clip_length))
    grad_normed = grad_hidden * (1.0 + modulation[0, 1])
    mean = jnp.mean(grad_normed * normed, axis=-1, keepdims=True)
    grad_tokens = (inverse * (grad_normed - normed * mean)).astype(jnp.bfloat16)
    return (attention[None], grad_tokens[None], weight_grad, mod_grad[None])


def solution(mesh):
    return jax.shard_map(
        body,
        mesh=mesh,
        in_specs=(P("dp", "seq", None), P("dp", None, None), P("seq", "dp"), P("dp", "seq", None)),
        out_specs=(P("dp", "seq", None), P("dp", "seq", None), P("seq", "dp"), P("dp", None, None)),
        check_vma=False,
    )
```

```python
import functools
import math

import jax
import jax.numpy as jnp
from jax import lax
from jax.experimental import pallas as pl
from jax.experimental.pallas import tpu as pltpu
from jax.sharding import PartitionSpec as P

HDIM = 32
AXES = ("seq", "dp")
ROWS = 70
UNIT = 144
COLS = 840
HALF = 576
GROUP = 4 * UNIT
ALL = 16 * UNIT
LANES = 128
PACK = 40
F32, BF16 = jnp.float32, jnp.bfloat16
WHOLE = pl.BlockSpec(memory_space=pltpu.VMEM)
ANYWHERE = pl.BlockSpec(memory_space=pl.ANY)
PARAMS = pltpu.CompilerParams(vmem_limit_bytes=56 * 1024 * 1024)


def place(index):
    seq, dp = divmod(index, 4)
    z_lo, rest = divmod(seq, 16)
    y, x = divmod(rest, 4)
    z_hi, core = divmod(dp, 2)
    return x, y, z_hi * 2 + z_lo, core


def index_of(x, y, z, core):
    x, y, z = x % 4, y % 4, z % 4
    return ((z % 2) * 16 + y * 4 + x) * 4 + (z // 2) * 2 + core


def route(kind, offset):
    pairs = []
    for index in range(128):
        x, y, z, core = place(index)
        if kind == "z":
            target = index_of(x, y, z + offset, core)
        elif kind == "z_lo":
            target = index_of(x, y, z ^ 1, core)
        elif kind == "core":
            target = index_of(x, y, z, 1 - core)
        elif (kind == "last") == (core == 0):
            target = index_of(x + offset, y, z, core)
        else:
            target = index_of(x, y + offset, z, core)
        pairs.append((index, target))
    return pairs


def send(value, kind, offset=0):
    return lax.ppermute(value, AXES, route(kind, offset))


def ring_gather(block, kind):
    half = block.shape[0] // 2
    ahead = send(block, kind, -1)
    behind = send(block, kind, 1)
    far_first = send(ahead[:half], kind, -1)
    far_second = send(behind[half:], kind, 1)
    return block, ahead, far_first, far_second, behind


def ring_gather_halves(block, kind):
    half = block.shape[0] // 2
    first, second = block[:half], block[half:]
    ahead_first = send(first, kind, -1)
    behind_second = send(second, kind, 1)
    ahead_second = send(second, kind, -1)
    behind_first = send(first, kind, 1)
    far_first = send(ahead_first, kind, -1)
    far_second = send(behind_second, kind, 1)
    return block, ahead_first, ahead_second, far_first, far_second, behind_first, behind_second


def add(left, right):
    return (left.astype(F32) + right.astype(F32)).astype(BF16)


def ring_scatter(own, ahead, far, behind, kind):
    far_first = send(far[0], kind, 1)
    far_second = send(far[1], kind, -1)
    plain_ahead = send(ahead[1], kind, 1)
    plain_behind = send(behind[0], kind, -1)
    summed_ahead = send(add(ahead[0], far_first), kind, 1)
    summed_behind = send(add(behind[1], far_second), kind, -1)
    first = own[0].astype(F32) + summed_ahead.astype(F32) + plain_behind.astype(F32)
    second = own[1].astype(F32) + plain_ahead.astype(F32) + summed_behind.astype(F32)
    return jnp.concatenate([first, second]).astype(BF16)


def ring_scatter_joined(own, ahead, far, behind, kind):
    half = own.shape[0] // 2
    far_first = send(far[:half], kind, 1)
    far_second = send(far[half:], kind, -1)
    ahead = jnp.concatenate([add(ahead[:half], far_first), ahead[half:]])
    behind = jnp.concatenate([behind[:half], add(behind[half:], far_second)])
    from_behind = send(ahead, kind, 1)
    from_ahead = send(behind, kind, -1)
    return (own.astype(F32) + from_behind.astype(F32) + from_ahead.astype(F32)).astype(BF16)


def seq_sum(value):
    for kind in ("last", "middle"):
        far = send(value, kind, 2)
        ahead = send(value, kind, -1)
        behind = send(value, kind, 1)
        value = (value + far) + (ahead + behind)
    return value + send(value, "z_lo")


def pick(core, on_zero, on_one):
    return jnp.where(core == 0, on_zero, on_one)


def head_half(array, core, other=False):
    width = array.shape[-1]
    low, high = array[..., :HALF], array[..., width - HALF :]
    return pick(core, high, low) if other else pick(core, low, high)


def head_join(mine, other, core):
    return jnp.concatenate([pick(core, mine, other), pick(core, other, mine)[..., HDIM:]], axis=-1)


def interleave(keys, values):
    parts = []
    for start in range(0, HALF, LANES):
        parts += [keys[:, start : start + LANES], values[:, start : start + LANES]]
    return jnp.concatenate(parts, axis=1)


def separate(pair):
    keys, values = [], []
    for start in range(0, HALF, LANES):
        width = min(LANES, HALF - start)
        keys.append(pair[:, 2 * start : 2 * start + width])
        values.append(pair[:, 2 * start + width : 2 * start + 2 * width])
    return jnp.concatenate(keys, axis=1), jnp.concatenate(values, axis=1)


def gather_units(weight, z, core):
    relative = [weight, send(weight, "z", -1), send(weight, "z", -2), send(weight, "z", 1)]
    relative = jnp.stack(relative + relative[:3])
    blocks = lax.dynamic_slice_in_dim(relative, lax.rem(4 - z, 4), 4, axis=0)
    others = send(blocks, "core")
    even, odd = pick(core, blocks, others), pick(core, others, blocks)
    columns = jnp.concatenate([even[:2], odd[:2], even[2:], odd[2:]], axis=2)
    columns = columns.reshape(2 * ROWS, 4 * COLS)
    columns = jnp.pad(columns, ((0, UNIT - 2 * ROWS), (0, 0)))
    third = 4 * COLS // 3
    query, keys, values = (head_half(columns[:, i * third : (i + 1) * third], core) for i in range(3))
    return interleave(keys, values), query


def gather_middle(unit):
    own, ahead, far_first, far_second, behind = ring_gather(unit, "middle")
    return jnp.concatenate([own, ahead, far_first, far_second, behind])


def scatter_units(query, pair, z, core):
    other_query, other_pair = send(query, "core"), send(pair, "core")
    keys, values = separate(pair)
    other_keys, other_values = separate(other_pair)
    columns = jnp.concatenate(
        [
            head_join(query, other_query, core),
            head_join(keys, other_keys, core),
            head_join(values, other_values, core),
        ],
        axis=1,
    )
    low = pick(core, columns[:, :COLS], columns[:, COLS : 2 * COLS])
    high = pick(core, columns[:, 2 * COLS : 3 * COLS], columns[:, 3 * COLS :])
    blocks = jnp.stack([low[:ROWS], low[ROWS : 2 * ROWS], high[:ROWS], high[ROWS : 2 * ROWS]])
    relative = lax.dynamic_slice_in_dim(jnp.concatenate([blocks, blocks[:3]]), z, 4, axis=0)
    ahead = send(relative[1], "z", 1)
    far = send(relative[2], "z", 2)
    behind = send(relative[3], "z", -1)
    return (relative[0].astype(F32) + far.astype(F32)) + (ahead.astype(F32) + behind.astype(F32))


def arrival_order(x, y, core, features):
    row = lax.broadcasted_iota(jnp.int32, (1, ALL), 1)
    last, middle, inner = row // GROUP, (row // UNIT) % 4, row % UNIT
    at_x = lax.rem(x + jnp.where(core == 0, last, middle), 4)
    at_y = lax.rem(y + jnp.where(core == 0, middle, last), 4)
    z_lo = inner // ROWS
    feature_index = (z_lo * 16 + at_y * 4 + at_x) * ROWS + inner % ROWS
    feature_index = jnp.where(inner < 2 * ROWS, feature_index, -1)
    return (lax.broadcasted_iota(jnp.int32, (features, 1), 0) == feature_index).astype(BF16)


def cost(flops, moved):
    return pl.CostEstimate(flops=int(flops), bytes_accessed=int(moved), transcendentals=0)


def split(value):
    high = value.astype(BF16)
    return high, (value - high.astype(F32)).astype(BF16)


def dot(left, right, dims=((1,), (0,))):
    return lax.dot_general(left, right, (dims, ((), ())), preferred_element_type=F32)


def dot_wide(left, right, dims=((1,), (0,))):
    left_high, left_low = split(left)
    right_high, right_low = split(right)
    return dot(left_high, right_high, dims) + (
        dot(left_low, right_high, dims) + dot(left_high, right_low, dims)
    )


def dot_left(left, right, dims=((1,), (0,))):
    high, low = split(left)
    return dot(high, right, dims) + dot(low, right, dims)


def dot_right(left, right, dims=((1,), (0,))):
    high, low = split(right)
    return dot(left, high, dims) + dot(left, low, dims)


def feature(values):
    lower = jnp.exp(jnp.minimum(values, 0.0))
    return jnp.where(values > 0, values + 1.0, lower), jnp.where(values > 0, 1.0, lower)


def same_head(rows, cols):
    row = lax.broadcasted_iota(jnp.int32, (rows, cols), 0) // HDIM
    return row == lax.broadcasted_iota(jnp.int32, (rows, cols), 1) // HDIM


def diagonal(product):
    width = product.shape[1]
    kept = jnp.where(same_head(width, width), product, 0.0)
    total = kept[:HDIM]
    for start in range(HDIM, width, HDIM):
        total = total + kept[start : start + HDIM]
    return total


def block_diagonal(blocks):
    width = blocks.shape[1]
    tiled = jnp.concatenate([blocks] * (width // HDIM), axis=0)
    return jnp.where(same_head(width, width), tiled, 0.0)


def groups():
    return [(start, min(LANES, HALF - start)) for start in range(0, HALF, LANES)]


def hidden_kernel(tokens_ref, mods_ref, order_ref, out_ref, turned_ref):
    tokens = tokens_ref[...]
    wide = tokens.astype(F32)
    inverse = lax.rsqrt(jnp.mean(wide * wide, axis=-1, keepdims=True) + 1e-06)
    mods = mods_ref[0]
    high = mods.astype(BF16).astype(F32)
    middle = (mods - high).astype(BF16).astype(F32)
    parts = jnp.concatenate([high, middle, mods - high - middle], axis=0).astype(BF16)
    parts = dot(parts, order_ref[...])
    shift = parts[0:1] + parts[2:3] + parts[4:5]
    scale = parts[1:2] + parts[3:4] + parts[5:6]
    local = dot(tokens, order_ref[...])
    hidden = local * inverse * (1.0 + scale) + shift
    out_ref[...] = hidden.astype(BF16)
    turned_ref[...] = hidden.T.astype(BF16)


def make_hidden(both, mods, order):
    count, features = both.shape
    block = 256
    return pl.pallas_call(
        hidden_kernel,
        grid=(count // block,),
        out_shape=(
            jax.ShapeDtypeStruct((count, ALL), BF16),
            jax.ShapeDtypeStruct((ALL, count), BF16),
        ),
        in_specs=[
            pl.BlockSpec((block, features), lambda i: (i, 0)),
            pl.BlockSpec((1, 2, features), lambda i: (i // (count // block // 2), 0, 0)),
            pl.BlockSpec((features, ALL), lambda i: (0, 0)),
        ],
        out_specs=(
            pl.BlockSpec((block, ALL), lambda i: (i, 0)),
            pl.BlockSpec((ALL, block), lambda i: (0, i)),
        ),
        compiler_params=PARAMS,
        cost_estimate=cost(2 * count * features * ALL, 2 * features * ALL + 6 * count * ALL),
        name="hidden",
    )(both, mods, order)


def load_rows(pieces, rows_ref, sems):
    copies, start = [], 0
    for number, piece in enumerate(pieces):
        target = rows_ref.at[pl.ds(start, piece.shape[0]), :]
        copies.append(pltpu.make_async_copy(piece, target, sems.at[number]))
        start += piece.shape[0]
    for copy in copies:
        copy.start()
    for copy in copies:
        copy.wait()


def pair_kernel(hidden_ref, *refs):
    pieces, (pair_ref, rows_ref, state_ref, sems) = refs[:-4], refs[-4:]
    load_rows(pieces, rows_ref, sems)
    count = hidden_ref.shape[0] // 2
    state_ref[...] = jnp.zeros_like(state_ref)
    for start, width in groups():
        columns = slice(2 * start, 2 * start + 2 * width)
        for clip in range(2):
            tokens = slice(clip * count, (clip + 1) * count)
            pair = dot(hidden_ref[tokens, :], rows_ref[:, columns]).astype(BF16)
            pair_ref[tokens, columns] = pair
            keys, _ = feature(pair[:, :width].astype(F32))
            product = dot_left(keys, pair[:, width:], ((0,), (0,)))
            base = clip * PACK
            state_ref[base : base + HDIM, start : start + width] = diagonal(product)
            total = jnp.sum(keys, axis=0, keepdims=True)
            state_ref[base + HDIM : base + HDIM + 1, start : start + width] = total


def query_kernel(hidden_ref, *refs):
    pieces, (query_ref, rows_ref, sems) = refs[:-3], refs[-3:]
    load_rows(pieces, rows_ref, sems)
    count = hidden_ref.shape[0] // 2
    for start, width in ((0, 256), (256, 256), (512, 64)):
        for clip in range(2):
            tokens = slice(clip * count, (clip + 1) * count)
            part = dot(hidden_ref[tokens, :], rows_ref[:, start : start + width])
            query_ref[tokens, start : start + width] = part.astype(BF16)


def project(kernel, hidden, pieces, extra):
    count, width = hidden.shape[0], pieces[0].shape[1]
    return pl.pallas_call(
        kernel,
        out_shape=(
            jax.ShapeDtypeStruct((count, width), BF16),
            jax.ShapeDtypeStruct((ALL, width), BF16),
            *extra,
        ),
        in_specs=[WHOLE] + [ANYWHERE] * len(pieces),
        out_specs=(WHOLE,) * (2 + len(extra)),
        scratch_shapes=[pltpu.SemaphoreType.DMA((len(pieces),))],
        compiler_params=PARAMS,
        cost_estimate=cost(2 * count * width * ALL, 2 * (count * width + ALL * width + count * ALL)),
        name=kernel.__name__,
    )(hidden, *pieces)


def middle_kernel(query_ref, grad_ref, state_ref, attention_ref, grad_query_ref, state_grad_ref):
    count = query_ref.shape[0] // 2
    state_grad_ref[...] = jnp.zeros_like(state_grad_ref)
    for start, width in groups():
        columns = slice(start, start + width)
        ones = same_head(width, width).astype(BF16)
        for clip in range(2):
            tokens = slice(clip * count, (clip + 1) * count)
            base = clip * PACK
            state = block_diagonal(state_ref[base : base + HDIM, columns])
            total = state_ref[base + HDIM : base + HDIM + 1, columns]
            query, slope = feature(query_ref[tokens, columns].astype(F32))
            grad = grad_ref[tokens, columns].astype(F32)
            numer = dot_wide(query, state)
            inverse = 1.0 / (dot_left(query * total, ones) + 1.0)
            quotient = numer * inverse
            attention_ref[tokens, columns] = quotient.astype(BF16)
            grad_numer = grad * inverse
            grad_denom = -dot_left(grad * quotient, ones) * inverse
            product = dot_wide(query, grad_numer, ((0,), (0,)))
            state_grad_ref[base : base + HDIM, columns] = diagonal(product)
            total_grad = jnp.sum(query * grad_denom, axis=0, keepdims=True)
            state_grad_ref[base + HDIM : base + HDIM + 1, columns] = total_grad
            back = dot_wide(grad_numer, state, ((1,), (1,))) + grad_denom * total
            grad_query_ref[tokens, columns] = (slope * back).astype(BF16)


def make_middle(query, grad, state):
    count = query.shape[0]
    return pl.pallas_call(
        middle_kernel,
        out_shape=(
            jax.ShapeDtypeStruct((count, HALF), BF16),
            jax.ShapeDtypeStruct((count, HALF), BF16),
            jax.ShapeDtypeStruct((2 * PACK, HALF), F32),
        ),
        in_specs=[WHOLE] * 3,
        out_specs=(WHOLE,) * 3,
        compiler_params=PARAMS,
        cost_estimate=cost(1e10, 8 * count * HALF),
        name="attention",
    )(query, grad, state)


def pair_grad_kernel(pair_ref, state_grad_ref, out_ref):
    count = pair_ref.shape[0] // 2
    for start, width in groups():
        columns = slice(2 * start, 2 * start + 2 * width)
        for clip in range(2):
            tokens = slice(clip * count, (clip + 1) * count)
            base = clip * PACK
            state_grad = block_diagonal(state_grad_ref[base : base + HDIM, start : start + width])
            total_grad = state_grad_ref[base + HDIM : base + HDIM + 1, start : start + width]
            pair = pair_ref[tokens, columns]
            keys, slope = feature(pair[:, :width].astype(F32))
            grad_keys = dot_right(pair[:, width:], state_grad, ((1,), (1,))) + total_grad
            grad_values = dot_wide(keys, state_grad)
            joined = jnp.concatenate([slope * grad_keys, grad_values], axis=1)
            out_ref[tokens, columns] = joined.astype(BF16)


def make_pair_grad(pair, state_grad):
    return pl.pallas_call(
        pair_grad_kernel,
        out_shape=jax.ShapeDtypeStruct(pair.shape, BF16),
        in_specs=[WHOLE] * 2,
        out_specs=WHOLE,
        compiler_params=PARAMS,
        cost_estimate=cost(5e9, 4 * pair.size),
        name="pair_grad",
    )(pair, state_grad)


def terms_kernel(blocks, grad_ref, *refs):
    for number in range(blocks):
        refs[blocks + number][...] = dot(refs[number][...], grad_ref[...]).astype(BF16)


def weight_terms(turned, grad, blocks, rows):
    count, width = grad.shape
    return pl.pallas_call(
        functools.partial(terms_kernel, len(blocks)),
        grid=(1,),
        out_shape=(jax.ShapeDtypeStruct((rows, width), BF16),) * len(blocks),
        in_specs=[pl.BlockSpec((count, width), lambda i: (0, 0))]
        + [pl.BlockSpec((rows, count), lambda i, b=block: (b, 0)) for block in blocks],
        out_specs=(pl.BlockSpec((rows, width), lambda i: (0, 0)),) * len(blocks),
        compiler_params=PARAMS,
        cost_estimate=cost(
            2 * len(blocks) * rows * count * width, 2 * len(blocks) * rows * (count + width)
        ),
        name="weight_terms",
    )(grad, *([turned] * len(blocks)))


def back_kernel(query_ref, pair_ref, rows_query_ref, rows_pair_ref, order_ref, out_ref):
    last = ((1,), (1,))
    partial = dot(query_ref[...], rows_query_ref[...], last)
    partial = partial + dot(pair_ref[...], rows_pair_ref[...], last)
    out_ref[...] = dot(partial.astype(BF16), order_ref[...], last).astype(BF16)


def back_project(grad_query, grad_pair, rows_query, rows_pair, order, clip):
    count, features = grad_query.shape[0] // 2, order.shape[0]
    block = 256
    steps = count // block
    return pl.pallas_call(
        back_kernel,
        grid=(steps,),
        out_shape=jax.ShapeDtypeStruct((count, features), BF16),
        in_specs=[
            pl.BlockSpec((block, HALF), lambda i: (i + clip * steps, 0)),
            pl.BlockSpec((block, 2 * HALF), lambda i: (i + clip * steps, 0)),
            pl.BlockSpec((ALL, HALF), lambda i: (0, 0)),
            pl.BlockSpec((ALL, 2 * HALF), lambda i: (0, 0)),
            pl.BlockSpec((features, ALL), lambda i: (0, 0)),
        ],
        out_specs=pl.BlockSpec((block, features), lambda i: (i, 0)),
        compiler_params=PARAMS,
        cost_estimate=cost(2 * count * ALL * (3 * HALF + features), 2 * ALL * (3 * HALF + features)),
        name="back_project",
    )(grad_query, grad_pair, rows_query, rows_pair, order)


def body(tokens, modulation, weight, cotangent):
    seq, dp = lax.axis_index("seq"), lax.axis_index("dp")
    x, y = lax.rem(seq, 4), lax.rem(seq // 4, 4)
    z, core = (dp // 2) * 2 + seq // 16, lax.rem(dp, 2)
    count, features = tokens.shape[1:]
    clip_length = count * lax.axis_size("seq")
    all_length = clip_length * lax.axis_size("dp")
    state_shape = jax.ShapeDtypeStruct((2 * PACK, HALF), F32)

    order = arrival_order(x, y, core, features)
    both = jnp.concatenate([tokens[0], send(tokens[0], "core")])
    both_mods = jnp.concatenate([modulation, send(modulation, "core")])
    grad_out = cotangent[0]
    grad_out = jnp.concatenate(
        [head_half(grad_out, core), send(head_half(grad_out, core, other=True), "core")]
    )
    hidden, turned = make_hidden(both, both_mods, order)

    unit_pair, unit_query = gather_units(weight, z, core)
    group_pair = gather_middle(unit_pair)
    group_pair, hidden = lax.optimization_barrier((group_pair, hidden))
    pieces_pair = ring_gather_halves(group_pair, "last")
    group_query = gather_middle(unit_query)
    group_query, pieces_pair = lax.optimization_barrier((group_query, pieces_pair))
    pieces_query = ring_gather(group_query, "last")

    pair, rows_pair, state = project(pair_kernel, hidden, pieces_pair, (state_shape,))
    state = seq_sum(state)
    query, rows_query = project(query_kernel, hidden, pieces_query, ())
    attention, grad_query, state_grad = make_middle(query, grad_out, state)
    attention = head_join(attention[:count], send(attention[count:], "core"), core)
    state_grad = seq_sum(state_grad)

    once = (lax.broadcasted_iota(jnp.int32, (1, HALF), 1) >= HDIM) | (core == 0)
    once_pair = interleave(once, once)
    grad_query = jnp.where(once, grad_query, 0.0).astype(BF16)
    terms = weight_terms(turned, grad_query, (2, 1, 3, 0), GROUP)
    group = ring_scatter_joined(terms[3], terms[1], terms[0], terms[2], "last")
    part_query = ring_scatter_joined(*jnp.split(group, 4), "middle")

    grad_pair = jnp.where(once_pair, make_pair_grad(pair, state_grad), 0.0).astype(BF16)
    soon = weight_terms(turned, grad_pair, (4, 5, 3, 6), GROUP // 2)
    later = weight_terms(turned, grad_pair, (2, 7, 0, 1), GROUP // 2)
    group = ring_scatter(
        later[2:], (later[0], soon[2]), soon[:2], (soon[3], later[1]), "last"
    )
    part_pair = ring_scatter_joined(*jnp.split(group, 4), "middle")
    weight_grad = scatter_units(part_query, part_pair, z, core) * (1.0 / math.sqrt(all_length))

    args = (grad_query, grad_pair, rows_query, rows_pair, order)
    received = send(back_project(*args, 1), "core")
    grad_hidden = back_project(*args, 0).astype(F32) + received.astype(F32)
    values = tokens[0].astype(F32)
    inverse = lax.rsqrt(jnp.mean(values * values, axis=-1, keepdims=True) + 1e-06)
    normed = values * inverse
    mod_local = jnp.stack([jnp.sum(grad_hidden, axis=0), jnp.sum(grad_hidden * normed, axis=0)])
    mod_grad = seq_sum(mod_local) * (1.0 / math.sqrt(clip_length))
    grad_normed = grad_hidden * (1.0 + modulation[0, 1])
    mean = jnp.mean(grad_normed * normed, axis=-1, keepdims=True)
    grad_tokens = (inverse * (grad_normed - normed * mean)).astype(BF16)
    return (attention[None], grad_tokens[None], weight_grad, mod_grad[None])


def solution(mesh):
    return jax.shard_map(
        body,
        mesh=mesh,
        in_specs=(P("dp", "seq", None), P("dp", None, None), P("seq", "dp"), P("dp", "seq", None)),
        out_specs=(P("dp", "seq", None), P("dp", "seq", None), P("seq", "dp"), P("dp", None, None)),
        check_vma=False,
    )
```

```python
import functools
import math

import jax
import jax.numpy as jnp
from jax import lax
from jax.experimental import pallas as pl
from jax.experimental.pallas import tpu as pltpu
from jax.sharding import PartitionSpec as P

HDIM = 32
AXES = ("seq", "dp")
ROWS = 70
UNIT = 144
COLS = 840
HALF = 576
GROUP = 4 * UNIT
ALL = 16 * UNIT
LANES = 128
PACK = 72
NEAR = 3 * GROUP
F32, BF16 = jnp.float32, jnp.bfloat16
WHOLE = pl.BlockSpec(memory_space=pltpu.VMEM)
ANYWHERE = pl.BlockSpec(memory_space=pl.ANY)
PARAMS = pltpu.CompilerParams(vmem_limit_bytes=56 * 1024 * 1024)


def place(index):
    seq, dp = divmod(index, 4)
    z_lo, rest = divmod(seq, 16)
    y, x = divmod(rest, 4)
    z_hi, core = divmod(dp, 2)
    return x, y, z_hi * 2 + z_lo, core


def index_of(x, y, z, core):
    x, y, z = x % 4, y % 4, z % 4
    return ((z % 2) * 16 + y * 4 + x) * 4 + (z // 2) * 2 + core


def route(kind, offset):
    pairs = []
    for index in range(128):
        x, y, z, core = place(index)
        if kind == "z":
            target = index_of(x, y, z + offset, core)
        elif kind == "z_lo":
            target = index_of(x, y, z ^ 1, core)
        elif kind == "z_hi":
            target = index_of(x, y, z ^ 2, core)
        elif kind == "z_hi_core":
            target = index_of(x, y, z ^ 2, 1 - core)
        elif kind == "core":
            target = index_of(x, y, z, 1 - core)
        elif (kind == "last") == (core == 0):
            target = index_of(x + offset, y, z, core)
        else:
            target = index_of(x, y + offset, z, core)
        pairs.append((index, target))
    return pairs


def send(value, kind, offset=0):
    return lax.ppermute(value, AXES, route(kind, offset))


def together(*values):
    return lax.optimization_barrier(values)


def ring_gather(block, kind):
    half = block.shape[0] // 2
    ahead = send(block, kind, -1)
    behind = send(block, kind, 1)
    far_first = send(ahead[:half], kind, -1)
    far_second = send(behind[half:], kind, 1)
    return jnp.concatenate([block, ahead, far_first, far_second, behind])


def add(left, right):
    return (left.astype(F32) + right.astype(F32)).astype(BF16)


def ring_scatter(own, ahead, far, behind, kind):
    half = own.shape[0] // 2
    far_first = send(far[:half], kind, 1)
    far_second = send(far[half:], kind, -1)
    ahead = jnp.concatenate([add(ahead[:half], far_first), ahead[half:]])
    behind = jnp.concatenate([behind[:half], add(behind[half:], far_second)])
    from_behind = send(ahead, kind, 1)
    from_ahead = send(behind, kind, -1)
    return (own.astype(F32) + from_behind.astype(F32) + from_ahead.astype(F32)).astype(BF16)


def exchange(value, kind):
    return send(value, kind, 2), send(value, kind, -1), send(value, kind, 1)


def ring_sum(value, parts):
    far, ahead, behind = parts
    return (value + far) + (ahead + behind)


def pick(core, on_zero, on_one):
    return jnp.where(core == 0, on_zero, on_one)


def head_half(array, core, axis, other=False):
    size = array.shape[axis]
    low = lax.slice_in_dim(array, 0, HALF, axis=axis)
    high = lax.slice_in_dim(array, size - HALF, size, axis=axis)
    return pick(core, high, low) if other else pick(core, low, high)


def head_join(mine, other, core, axis):
    second = lax.slice_in_dim(pick(core, other, mine), HDIM, HALF, axis=axis)
    return jnp.concatenate([pick(core, mine, other), second], axis=axis)


def gather_units(weight, z_lo, core):
    blocks = lax.all_gather(weight, "dp")
    columns = jnp.concatenate([blocks[i] for i in range(4)], axis=1)
    third = 4 * COLS // 3
    query, keys, values = (
        head_half(columns[:, i * third : (i + 1) * third], core, 1) for i in range(3)
    )
    mine = jnp.concatenate([keys, values, query], axis=1)
    other = send(mine, "z_lo")
    unit = jnp.concatenate([pick(z_lo, mine, other), pick(z_lo, other, mine)])
    return jnp.pad(unit, ((0, UNIT - 2 * ROWS), (0, 0)))


def finish_weight(keys_values, query, z_lo, dp, core):
    unit = jnp.concatenate([query, keys_values], axis=1)
    first, second = unit[:ROWS], unit[ROWS : 2 * ROWS]
    mine = add(pick(z_lo, first, second), send(pick(z_lo, second, first), "z_lo"))
    zero = jnp.zeros((ROWS, HALF), BF16)
    columns = jnp.concatenate(
        [head_join(mine[:, i * HALF : (i + 1) * HALF], zero, core, 1) for i in range(3)], axis=1
    )
    blocks = jnp.stack([columns[:, i * COLS : (i + 1) * COLS] for i in range(4)])

    def block(flip):
        return lax.dynamic_index_in_dim(blocks, dp ^ flip, 0, keepdims=False)

    by_z = send(block(2), "z_hi")
    by_both = send(block(3), "z_hi_core")
    by_core = send(block(1), "core")
    return (block(0).astype(F32) + by_core.astype(F32)) + (by_z.astype(F32) + by_both.astype(F32))


def cost(flops, moved):
    return pl.CostEstimate(flops=int(flops), bytes_accessed=int(moved), transcendentals=0)


def split(value):
    high = value.astype(BF16)
    return high, (value - high.astype(F32)).astype(BF16)


def dot(left, right, dims=((1,), (0,))):
    return lax.dot_general(left, right, (dims, ((), ())), preferred_element_type=F32)


def dot_wide(left, right, dims=((1,), (0,))):
    left_high, left_low = split(left)
    right_high, right_low = split(right)
    return dot(left_high, right_high, dims) + (
        dot(left_low, right_high, dims) + dot(left_high, right_low, dims)
    )


def dot_left(left, right, dims=((1,), (0,))):
    high, low = split(left)
    return dot(high, right, dims) + dot(low, right, dims)


def dot_right(left, right, dims=((1,), (0,))):
    high, low = split(right)
    return dot(left, high, dims) + dot(left, low, dims)


def feature(values):
    lower = jnp.exp(jnp.minimum(values, 0.0))
    return jnp.where(values > 0, values + 1.0, lower), jnp.where(values > 0, 1.0, lower)


def same_head(size):
    row = lax.broadcasted_iota(jnp.int32, (size, size), 0) // HDIM
    return row == lax.broadcasted_iota(jnp.int32, (size, size), 1) // HDIM


def diagonal(product):
    width = product.shape[1]
    kept = jnp.where(same_head(width), product, 0.0)
    total = kept[:HDIM]
    for start in range(HDIM, width, HDIM):
        total = total + kept[start : start + HDIM]
    return total


def block_diagonal(blocks):
    width = blocks.shape[1]
    tiled = jnp.concatenate([blocks] * (width // HDIM), axis=0)
    return jnp.where(same_head(width), tiled, 0.0)


def column(row):
    width = row.shape[1]
    index = lax.broadcasted_iota(jnp.int32, (width, width), 0)
    same = index == lax.broadcasted_iota(jnp.int32, (width, width), 1)
    return jnp.sum(jnp.where(same, row, 0.0), axis=1, keepdims=True)


def token_sum(array):
    ones = jnp.ones((16, array.shape[1]), BF16)
    return dot_right(ones, array, ((1,), (1,)))[:1]


def groups():
    return [(start, min(LANES, HALF - start)) for start in range(0, HALF, LANES)]


def unit_rows(starts_ref, number):
    return pl.ds(pl.multiple_of(starts_ref[number], 16), UNIT)


def hidden_kernel(starts_ref, tokens_ref, mods_ref, *refs):
    out_ref, wide_ref = refs[-2:]
    features, count = tokens_ref.shape
    chunk = 112
    total = jnp.zeros((1, count), F32)
    for start in range(0, features, chunk):
        values = tokens_ref[start : start + chunk, :].astype(F32)
        total = total + jnp.sum(values * values, axis=0, keepdims=True)
    inverse = lax.rsqrt(total * (1.0 / features) + 1e-06)
    for start in range(0, features, chunk):
        rows = slice(start, start + chunk)
        values = tokens_ref[rows, :].astype(F32) * inverse
        wide_ref[rows, :] = values * (1.0 + mods_ref[rows, 1:2]) + mods_ref[rows, 0:1]
    for number in range(16):
        low, high = number * ROWS, (16 + number) * ROWS
        parts = [
            wide_ref[low : low + ROWS, :],
            wide_ref[high : high + ROWS, :],
            jnp.zeros((UNIT - 2 * ROWS, count), F32),
        ]
        out_ref[unit_rows(starts_ref, number), :] = jnp.concatenate(parts).astype(BF16)


def make_hidden(starts, tokens, mods, clip, before=None):
    features, count = tokens.shape
    extra = [] if before is None else [before]
    return pl.pallas_call(
        hidden_kernel,
        grid=(1,),
        out_shape=jax.ShapeDtypeStruct((ALL, 2 * count), BF16),
        in_specs=[
            pl.BlockSpec(memory_space=pltpu.SMEM),
            pl.BlockSpec((features, count), lambda i: (0, 0)),
            pl.BlockSpec((features, 2), lambda i: (0, 0)),
        ]
        + [ANYWHERE] * len(extra),
        out_specs=pl.BlockSpec((ALL, count), lambda i: (0, clip)),
        scratch_shapes=[pltpu.VMEM((features, count), F32)],
        input_output_aliases={3: 0} if extra else {},
        compiler_params=PARAMS,
        cost_estimate=cost(3e9, 6 * count * ALL),
        name="hidden",
    )(starts, tokens, mods, *extra)


def state_kernel(pair_ref, state_ref):
    count = pair_ref.shape[1] // 2
    state_ref[2 * HDIM :, :] = jnp.zeros((PACK - 2 * HDIM, HALF), F32)
    for start, width in groups():
        columns = slice(start, start + width)
        for clip in range(2):
            tokens = slice(clip * count, (clip + 1) * count)
            keys, _ = feature(pair_ref[columns, tokens].astype(F32))
            values = pair_ref[HALF + start : HALF + start + width, tokens]
            product = dot_left(keys, values, ((1,), (1,)))
            state_ref[clip * HDIM : (clip + 1) * HDIM, columns] = diagonal(product)
            state_ref[2 * HDIM + clip : 2 * HDIM + clip + 1, columns] = token_sum(keys)


def make_state(pair):
    return pl.pallas_call(
        state_kernel,
        out_shape=jax.ShapeDtypeStruct((PACK, HALF), F32),
        in_specs=[WHOLE],
        out_specs=WHOLE,
        compiler_params=PARAMS,
        cost_estimate=cost(2e9, 2 * pair.size),
        name="state",
    )(pair)


def once(start, width, keep):
    row = lax.broadcasted_iota(jnp.int32, (width, 1), 0) + start
    return jnp.where(row < HDIM, keep, 1.0)


def middle_kernel(
    keep_ref, query_ref, grad_ref, state_ref, attention_ref, grad_query_ref, state_grad_ref
):
    count = query_ref.shape[1] // 2
    state_grad_ref[2 * HDIM :, :] = jnp.zeros((PACK - 2 * HDIM, HALF), F32)
    keep = keep_ref[0]
    for start, width in groups():
        rows = slice(start, start + width)
        ones = same_head(width).astype(BF16)
        for clip in range(2):
            tokens = slice(clip * count, (clip + 1) * count)
            mine = slice(clip * HDIM, (clip + 1) * HDIM)
            sums = slice(2 * HDIM + clip, 2 * HDIM + clip + 1)
            state = block_diagonal(state_ref[mine, rows])
            total = state_ref[sums, rows]
            total_column = column(total)
            query, slope = feature(query_ref[rows, tokens].astype(F32))
            grad = grad_ref[rows, tokens].astype(F32)
            numer = dot_wide(state, query, ((0,), (0,)))
            inverse = 1.0 / (dot_right(ones, query * total_column) + 1.0)
            quotient = numer * inverse
            attention_ref[rows, tokens] = quotient.astype(BF16)
            grad_numer = grad * inverse
            grad_denom = -dot_right(ones, grad * quotient) * inverse
            product = dot_wide(query, grad_numer, ((1,), (1,)))
            state_grad_ref[mine, rows] = diagonal(product)
            state_grad_ref[sums, rows] = token_sum(query * grad_denom)
            back = dot_wide(state, grad_numer) + grad_denom * total_column
            back = slope * back * once(start, width, keep)
            grad_query_ref[rows, tokens] = back.astype(BF16)


def make_middle(keep, query, grad, state):
    count = query.shape[1]
    return pl.pallas_call(
        middle_kernel,
        out_shape=(
            jax.ShapeDtypeStruct((HALF, count), BF16),
            jax.ShapeDtypeStruct((HALF, count), BF16),
            jax.ShapeDtypeStruct((PACK, HALF), F32),
        ),
        in_specs=[pl.BlockSpec(memory_space=pltpu.SMEM)] + [WHOLE] * 3,
        out_specs=(WHOLE,) * 3,
        compiler_params=PARAMS,
        cost_estimate=cost(8e9, 8 * count * HALF),
        name="attention",
    )(keep, query, grad, state)


def pair_grad_kernel(keep_ref, pair_ref, state_grad_ref, out_ref):
    count = pair_ref.shape[1] // 2
    keep = keep_ref[0]
    for start, width in groups():
        rows = slice(start, start + width)
        value_rows = slice(HALF + start, HALF + start + width)
        factor = once(start, width, keep)
        for clip in range(2):
            tokens = slice(clip * count, (clip + 1) * count)
            sums = slice(2 * HDIM + clip, 2 * HDIM + clip + 1)
            state_grad = block_diagonal(state_grad_ref[clip * HDIM : (clip + 1) * HDIM, rows])
            total_grad = column(state_grad_ref[sums, rows])
            keys, slope = feature(pair_ref[rows, tokens].astype(F32))
            grad_keys = dot_left(state_grad, pair_ref[value_rows, tokens]) + total_grad
            grad_values = dot_wide(state_grad, keys, ((0,), (0,)))
            out_ref[rows, tokens] = (slope * grad_keys * factor).astype(BF16)
            out_ref[value_rows, tokens] = (grad_values * factor).astype(BF16)


def make_pair_grad(keep, pair, state_grad):
    return pl.pallas_call(
        pair_grad_kernel,
        out_shape=jax.ShapeDtypeStruct(pair.shape, BF16),
        in_specs=[pl.BlockSpec(memory_space=pltpu.SMEM)] + [WHOLE] * 2,
        out_specs=WHOLE,
        compiler_params=PARAMS,
        cost_estimate=cost(5e9, 4 * pair.size),
        name="pair_grad",
    )(keep, pair, state_grad)


def terms_kernel(blocks, grad_ref, *refs):
    for number in range(blocks):
        part = dot(refs[number][...], grad_ref[...], ((1,), (1,)))
        refs[blocks + number][...] = part.astype(BF16)


def weight_terms(hidden, grad, blocks, rows):
    width, count = grad.shape
    return pl.pallas_call(
        functools.partial(terms_kernel, len(blocks)),
        grid=(1,),
        out_shape=(jax.ShapeDtypeStruct((rows, width), BF16),) * len(blocks),
        in_specs=[pl.BlockSpec((width, count), lambda i: (0, 0))]
        + [pl.BlockSpec((rows, count), lambda i, b=block: (b, 0)) for block in blocks],
        out_specs=(pl.BlockSpec((rows, width), lambda i: (0, 0)),) * len(blocks),
        compiler_params=PARAMS,
        cost_estimate=cost(
            2 * len(blocks) * rows * count * width, 2 * len(blocks) * rows * (count + width)
        ),
        name="weight_terms",
    )(grad, *([hidden] * len(blocks)))


def restore_kernel(starts_ref, near_ref, far_ref, out_ref, wide_ref, plain_ref):
    for start in range(0, NEAR, UNIT):
        wide_ref[start : start + UNIT, :] = near_ref[start : start + UNIT, :].astype(F32)
    for start in range(0, GROUP, UNIT):
        wide_ref[NEAR + start : NEAR + start + UNIT, :] = far_ref[start : start + UNIT, :].astype(F32)
    for number in range(16):
        low, high = number * ROWS, (16 + number) * ROWS
        unit = wide_ref[unit_rows(starts_ref, number), :]
        plain_ref[low : low + ROWS, :] = unit[:ROWS]
        plain_ref[high : high + ROWS, :] = unit[ROWS : 2 * ROWS]
    chunk = 112
    for start in range(0, 32 * ROWS, chunk):
        out_ref[start : start + chunk, :] = plain_ref[start : start + chunk, :].astype(BF16)


def restore(starts, near, far, clip):
    count = near.shape[1] // 2
    return pl.pallas_call(
        restore_kernel,
        grid=(1,),
        out_shape=jax.ShapeDtypeStruct((32 * ROWS, count), BF16),
        in_specs=[
            pl.BlockSpec(memory_space=pltpu.SMEM),
            pl.BlockSpec((NEAR, count), lambda i: (0, clip)),
            pl.BlockSpec((GROUP, count), lambda i: (0, clip)),
        ],
        out_specs=pl.BlockSpec((32 * ROWS, count), lambda i: (0, 0)),
        scratch_shapes=[pltpu.VMEM((ALL, count), F32), pltpu.VMEM((32 * ROWS, count), F32)],
        compiler_params=PARAMS,
        cost_estimate=cost(3e9, 6 * count * ALL),
        name="restore",
    )(starts, near, far)


def unit_starts(x, y, core):
    starts = []
    for at_y in range(4):
        for at_x in range(4):
            step_x, step_y = lax.rem(at_x - x + 4, 4), lax.rem(at_y - y + 4, 4)
            outer, inner = pick(core, step_x, step_y), pick(core, step_y, step_x)
            outer = jnp.where(outer == 2, 3, jnp.where(outer == 3, 2, outer))
            starts.append((outer * 4 + inner) * UNIT)
    return jnp.stack(starts).astype(jnp.int32)


def body(tokens, modulation, weight, cotangent):
    seq, dp = lax.axis_index("seq"), lax.axis_index("dp")
    x, y, z_lo = lax.rem(seq, 4), lax.rem(seq // 4, 4), seq // 16
    core = lax.rem(dp, 2)
    count, features = tokens.shape[1:]
    clip_length = count * lax.axis_size("seq")
    all_length = clip_length * lax.axis_size("dp")
    keep = jnp.where(core == 0, 1.0, 0.0).astype(F32).reshape(1)
    first, last = ((0,), (0,)), ((1,), (1,))

    tokens_own = tokens[0].T
    tokens_other = send(tokens_own, "core")
    mods_own = modulation[0].T
    mods_other = send(modulation[0], "core").T
    grad_out = cotangent[0].T
    grad_out = jnp.concatenate(
        [head_half(grad_out, core, 0), send(head_half(grad_out, core, 0, other=True), "core")], axis=1
    )
    starts = unit_starts(x, y, core)

    group = ring_gather(gather_units(weight, z_lo, core), "middle")
    pair_group, query_group = group[:, : 2 * HALF], group[:, 2 * HALF :]
    half = GROUP // 2
    ahead_first = send(pair_group[:half], "last", -1)
    behind_second = send(pair_group[half:], "last", 1)
    ahead_second = send(pair_group[half:], "last", -1)
    behind_first = send(pair_group[:half], "last", 1)
    hidden = make_hidden(starts, tokens_own, mods_own, 0)
    ahead_first, behind_second, hidden = together(ahead_first, behind_second, hidden)
    far_first = send(ahead_first, "last", -1)
    far_second = send(behind_second, "last", 1)
    hidden = make_hidden(starts, tokens_other, mods_other, 1, hidden)
    ahead_second, behind_first, hidden, query_group = together(
        ahead_second, behind_first, hidden, query_group
    )
    query_ahead = send(query_group, "last", -1)
    query_behind = send(query_group, "last", 1)
    near_pair = jnp.concatenate(
        [pair_group, ahead_first, ahead_second, behind_first, behind_second]
    )
    pair = dot(near_pair, hidden[:NEAR], first)
    far_first, far_second, pair = together(far_first, far_second, pair)
    far_pair = jnp.concatenate([far_first, far_second])
    pair = (pair + dot(far_pair, hidden[NEAR:], first)).astype(BF16)
    state = make_state(pair)

    parts = exchange(state, "last")
    query_ahead, query_behind, state = together(query_ahead, query_behind, state)
    query_far_first = send(query_ahead[:half], "last", -1)
    query_far_second = send(query_behind[half:], "last", 1)
    near_query = jnp.concatenate([query_group, query_ahead, query_behind])
    query = dot(near_query, hidden[:NEAR], first)
    *parts, query = together(*parts, query)
    state = ring_sum(state, parts)
    parts = exchange(state, "middle")
    far_query = jnp.concatenate([query_far_first, query_far_second])
    query = (query + dot(far_query, hidden[NEAR:], first)).astype(BF16)
    *parts, query = together(*parts, query)
    state = ring_sum(state, parts)
    state = state + send(state, "z_lo")

    attention, grad_query, state_grad = make_middle(keep, query, grad_out, state)
    attention = head_join(attention[:, :count], send(attention[:, count:], "core"), core, 0)

    parts = exchange(state_grad, "last")
    terms = weight_terms(hidden, grad_query, (3, 1, 2, 0), GROUP)
    *parts, terms = together(*parts, terms)
    state_grad = ring_sum(state_grad, parts)
    parts = exchange(state_grad, "middle")
    near_back = dot(near_query, grad_query)
    far_back = dot(far_query, grad_query)
    *parts, near_back, far_back = together(*parts, near_back, far_back)
    state_grad = ring_sum(state_grad, parts)
    state_grad = state_grad + send(state_grad, "z_lo")
    query_part = ring_scatter(terms[3], terms[1], terms[0], terms[2], "last")
    query_part = ring_scatter(*jnp.split(query_part, 4), "middle")

    grad_pair = make_pair_grad(keep, pair, state_grad)
    soon = weight_terms(hidden, grad_pair, (6, 7, 3, 4), half)
    far_first = send(soon[0], "last", 1)
    far_second = send(soon[1], "last", -1)
    plain_ahead = send(soon[2], "last", 1)
    plain_behind = send(soon[3], "last", -1)
    grad_pair, _ = together(grad_pair, soon[0])
    later = weight_terms(hidden, grad_pair, (2, 5, 0, 1), half)
    far_first, far_second, later = together(far_first, far_second, later)
    summed_ahead = send(add(later[0], far_first), "last", 1)
    summed_behind = send(add(later[1], far_second), "last", -1)
    grad_pair, _ = together(grad_pair, later[2])
    near_back = (near_back + dot(near_pair, grad_pair)).astype(BF16)
    far_back = (far_back + dot(far_pair, grad_pair)).astype(BF16)
    plain_ahead, plain_behind, summed_ahead, summed_behind, near_back, far_back = together(
        plain_ahead, plain_behind, summed_ahead, summed_behind, near_back, far_back
    )
    pair_part = jnp.concatenate(
        [
            later[2].astype(F32) + summed_ahead.astype(F32) + plain_behind.astype(F32),
            later[3].astype(F32) + plain_ahead.astype(F32) + summed_behind.astype(F32),
        ]
    ).astype(BF16)
    pair_part = ring_scatter(*jnp.split(pair_part, 4), "middle")
    weight_grad = finish_weight(pair_part, query_part, z_lo, dp, core)
    weight_grad = weight_grad * (1.0 / math.sqrt(all_length))

    received = send(restore(starts, near_back, far_back, 1), "core")
    grad_hidden = restore(starts, near_back, far_back, 0)
    grad_hidden = grad_hidden.astype(F32) + received.astype(F32)
    values = tokens_own.astype(F32)
    inverse = lax.rsqrt(jnp.mean(values * values, axis=0, keepdims=True) + 1e-06)
    normed = values * inverse
    mod_grad = jnp.stack([jnp.sum(grad_hidden, axis=1), jnp.sum(grad_hidden * normed, axis=1)])
    for kind in ("last", "middle"):
        mod_grad = ring_sum(mod_grad, exchange(mod_grad, kind))
    mod_grad = (mod_grad + send(mod_grad, "z_lo")) * (1.0 / math.sqrt(clip_length))
    grad_normed = grad_hidden * (1.0 + mods_own[:, 1:2])
    mean = jnp.mean(grad_normed * normed, axis=0, keepdims=True)
    grad_tokens = (inverse * (grad_normed - normed * mean)).astype(BF16)
    return (attention.T[None], grad_tokens.T[None], weight_grad, mod_grad[None])


def solution(mesh):
    return jax.shard_map(
        body,
        mesh=mesh,
        in_specs=(P("dp", "seq", None), P("dp", None, None), P("seq", "dp"), P("dp", "seq", None)),
        out_specs=(P("dp", "seq", None), P("dp", "seq", None), P("seq", "dp"), P("dp", None, None)),
        check_vma=False,
    )
```

```python
import functools
import math

import jax
import jax.numpy as jnp
from jax import lax
from jax.experimental import pallas as pl
from jax.experimental.pallas import tpu as pltpu
from jax.sharding import PartitionSpec as P

HDIM = 32
AXES = ("seq", "dp")
ROWS = 70
UNIT = 144
COLS = 840
HALF = 576
GROUP = 4 * UNIT
ALL = 16 * UNIT
LANES = 128
PACK = 72
NEAR = 3 * GROUP
F32, BF16 = jnp.float32, jnp.bfloat16
WHOLE = pl.BlockSpec(memory_space=pltpu.VMEM)
ANYWHERE = pl.BlockSpec(memory_space=pl.ANY)


def place(index):
    seq, dp = divmod(index, 4)
    z_lo, rest = divmod(seq, 16)
    y, x = divmod(rest, 4)
    z_hi, core = divmod(dp, 2)
    return x, y, z_hi * 2 + z_lo, core


def index_of(x, y, z, core):
    x, y, z = x % 4, y % 4, z % 4
    return ((z % 2) * 16 + y * 4 + x) * 4 + (z // 2) * 2 + core


def route(kind, offset):
    pairs = []
    for index in range(128):
        x, y, z, core = place(index)
        if kind == "z":
            target = index_of(x, y, z + offset, core)
        elif kind == "z_lo":
            target = index_of(x, y, z ^ 1, core)
        elif kind == "z_hi":
            target = index_of(x, y, z ^ 2, core)
        elif kind == "z_hi_core":
            target = index_of(x, y, z ^ 2, 1 - core)
        elif kind == "core":
            target = index_of(x, y, z, 1 - core)
        elif (kind == "last") == (core == 0):
            target = index_of(x + offset, y, z, core)
        else:
            target = index_of(x, y + offset, z, core)
        pairs.append((index, target))
    return pairs


def send(value, kind, offset=0):
    return lax.ppermute(value, AXES, route(kind, offset))


def together(*values):
    return lax.optimization_barrier(values)


def ring_gather(block, kind):
    half = block.shape[0] // 2
    ahead = send(block, kind, -1)
    behind = send(block, kind, 1)
    far_first = send(ahead[:half], kind, -1)
    far_second = send(behind[half:], kind, 1)
    return jnp.concatenate([block, ahead, far_first, far_second, behind])


def add(left, right):
    return (left.astype(F32) + right.astype(F32)).astype(BF16)


def exchange(value, kind):
    return send(value, kind, 2), send(value, kind, -1), send(value, kind, 1)


def ring_sum(value, parts):
    far, ahead, behind = parts
    return (value + far) + (ahead + behind)


def pick(core, on_zero, on_one):
    return jnp.where(core == 0, on_zero, on_one)


def head_half(array, core, axis, other=False):
    size = array.shape[axis]
    low = lax.slice_in_dim(array, 0, HALF, axis=axis)
    high = lax.slice_in_dim(array, size - HALF, size, axis=axis)
    return pick(core, high, low) if other else pick(core, low, high)


def head_join(mine, other, core, axis):
    second = lax.slice_in_dim(pick(core, other, mine), HDIM, HALF, axis=axis)
    return jnp.concatenate([pick(core, mine, other), second], axis=axis)


def gather_units(weight, z_lo, core):
    blocks = lax.all_gather(weight, "dp")
    columns = jnp.concatenate([blocks[i] for i in range(4)], axis=1)
    third = 4 * COLS // 3
    query, keys, values = (
        head_half(columns[:, i * third : (i + 1) * third], core, 1) for i in range(3)
    )
    mine = jnp.concatenate([keys, values, query], axis=1)
    other = send(mine, "z_lo")
    unit = jnp.concatenate([pick(z_lo, mine, other), pick(z_lo, other, mine)])
    return jnp.pad(unit, ((0, UNIT - 2 * ROWS), (0, 0)))


def finish_weight(unit, z_lo, dp, core):
    first, second = unit[:ROWS], unit[ROWS : 2 * ROWS]
    mine = add(pick(z_lo, first, second), send(pick(z_lo, second, first), "z_lo"))
    zero = jnp.zeros((ROWS, HALF), BF16)
    columns = jnp.concatenate(
        [head_join(mine[:, i * HALF : (i + 1) * HALF], zero, core, 1) for i in (2, 0, 1)], axis=1
    )
    blocks = jnp.stack([columns[:, i * COLS : (i + 1) * COLS] for i in range(4)])

    def block(flip):
        return lax.dynamic_index_in_dim(blocks, dp ^ flip, 0, keepdims=False)

    by_z = send(block(2), "z_hi")
    by_both = send(block(3), "z_hi_core")
    by_core = send(block(1), "core")
    return (block(0).astype(F32) + by_core.astype(F32)) + (by_z.astype(F32) + by_both.astype(F32))


def params(mebibytes):
    return pltpu.CompilerParams(vmem_limit_bytes=mebibytes * 1024 * 1024)


NO_COST = pl.CostEstimate(flops=0, bytes_accessed=0, transcendentals=0)


def split(value):
    high = value.astype(BF16)
    return high, (value - high.astype(F32)).astype(BF16)


def dot(left, right, dims=((1,), (0,))):
    return lax.dot_general(left, right, (dims, ((), ())), preferred_element_type=F32)


def dot_wide(left, right, dims=((1,), (0,))):
    left_high, left_low = split(left)
    right_high, right_low = split(right)
    return dot(left_high, right_high, dims) + (
        dot(left_low, right_high, dims) + dot(left_high, right_low, dims)
    )


def dot_left(left, right, dims=((1,), (0,))):
    high, low = split(left)
    return dot(high, right, dims) + dot(low, right, dims)


def dot_right(left, right, dims=((1,), (0,))):
    high, low = split(right)
    return dot(left, high, dims) + dot(left, low, dims)


def feature(values):
    lower = jnp.exp(jnp.minimum(values, 0.0))
    return jnp.where(values > 0, values + 1.0, lower), jnp.where(values > 0, 1.0, lower)


def same_head(size):
    row = lax.broadcasted_iota(jnp.int32, (size, size), 0) // HDIM
    return row == lax.broadcasted_iota(jnp.int32, (size, size), 1) // HDIM


def diagonal(product):
    width = product.shape[1]
    kept = jnp.where(same_head(width), product, 0.0)
    total = kept[:HDIM]
    for start in range(HDIM, width, HDIM):
        total = total + kept[start : start + HDIM]
    return total


def block_diagonal(blocks):
    width = blocks.shape[1]
    tiled = jnp.concatenate([blocks] * (width // HDIM), axis=0)
    return jnp.where(same_head(width), tiled, 0.0)


def column(row):
    width = row.shape[1]
    index = lax.broadcasted_iota(jnp.int32, (width, width), 0)
    same = index == lax.broadcasted_iota(jnp.int32, (width, width), 1)
    return jnp.sum(jnp.where(same, row, 0.0), axis=1, keepdims=True)


def token_sum(array):
    ones = jnp.ones((16, array.shape[1]), BF16)
    return dot_right(ones, array, ((1,), (1,)))[:1]


def groups():
    return [(start, min(LANES, HALF - start)) for start in range(0, HALF, LANES)]


def unit_rows(starts_ref, number):
    return pl.ds(pl.multiple_of(starts_ref[number], 16), UNIT)


def hidden_kernel(starts_ref, tokens_ref, mods_ref, *refs):
    out_ref, wide_ref = refs[-2:]
    features, count = tokens_ref.shape
    chunk = 112
    total = jnp.zeros((1, count), F32)
    for start in range(0, features, chunk):
        values = tokens_ref[start : start + chunk, :].astype(F32)
        total = total + jnp.sum(values * values, axis=0, keepdims=True)
    inverse = lax.rsqrt(total * (1.0 / features) + 1e-06)
    for start in range(0, features, chunk):
        rows = slice(start, start + chunk)
        values = tokens_ref[rows, :].astype(F32) * inverse
        wide_ref[rows, :] = values * (1.0 + mods_ref[rows, 1:2]) + mods_ref[rows, 0:1]
    for number in range(16):
        low, high = number * ROWS, (16 + number) * ROWS
        parts = [
            wide_ref[low : low + ROWS, :],
            wide_ref[high : high + ROWS, :],
            jnp.zeros((UNIT - 2 * ROWS, count), F32),
        ]
        out_ref[unit_rows(starts_ref, number), :] = jnp.concatenate(parts).astype(BF16)


def make_hidden(starts, tokens, mods, clip, before=None):
    features, count = tokens.shape
    extra = [] if before is None else [before]
    return pl.pallas_call(
        hidden_kernel,
        grid=(1,),
        out_shape=jax.ShapeDtypeStruct((ALL, 2 * count), BF16),
        in_specs=[
            pl.BlockSpec(memory_space=pltpu.SMEM),
            pl.BlockSpec((features, count), lambda i: (0, 0)),
            pl.BlockSpec((features, 2), lambda i: (0, 0)),
        ]
        + [ANYWHERE] * len(extra),
        out_specs=pl.BlockSpec((ALL, count), lambda i: (0, clip)),
        scratch_shapes=[pltpu.VMEM((features, count), F32)],
        input_output_aliases={3: 0} if extra else {},
        compiler_params=params(24),
        cost_estimate=NO_COST,
        name="hidden",
    )(starts, tokens, mods, *extra)


def chunks(width):
    size = 384 if width % 384 == 0 else 256
    return [slice(start, min(start + size, width)) for start in range(0, width, size)]


def halves(count):
    return [slice(0, count // 2), slice(count // 2, count)]


FIRST, LAST = ((0,), (0,)), ((1,), (1,))


def near_kernel(hidden_ref, own_ref, ahead_ref, behind_ref, out_ref):
    for rows in chunks(out_ref.shape[0]):
        for tokens in halves(out_ref.shape[1]):
            total = dot(own_ref[:, rows], hidden_ref[:GROUP, tokens], FIRST)
            total += dot(ahead_ref[:, rows], hidden_ref[GROUP : 2 * GROUP, tokens], FIRST)
            total += dot(behind_ref[:, rows], hidden_ref[2 * GROUP :, tokens], FIRST)
            out_ref[rows, tokens] = total


def project_near(hidden, pieces):
    width, count = pieces[0].shape[1], hidden.shape[1]
    return pl.pallas_call(
        near_kernel,
        grid=(1,),
        out_shape=jax.ShapeDtypeStruct((width, count), F32),
        in_specs=[pl.BlockSpec((NEAR, count), lambda i: (0, 0))]
        + [pl.BlockSpec((GROUP, width), lambda i: (0, 0))] * 3,
        out_specs=pl.BlockSpec((width, count), lambda i: (0, 0)),
        compiler_params=params(40),
        cost_estimate=NO_COST,
        name="project_near",
    )(hidden, *pieces)


def far_kernel(hidden_ref, near_ref, first_ref, second_ref, out_ref, *state_refs):
    half = GROUP // 2
    width, count = out_ref.shape
    for rows in chunks(width):
        for tokens in halves(count):
            total = near_ref[rows, tokens]
            total += dot(first_ref[:, rows], hidden_ref[:half, tokens], FIRST)
            total += dot(second_ref[:, rows], hidden_ref[half:, tokens], FIRST)
            out_ref[rows, tokens] = total.astype(BF16)
    for state_ref in state_refs:
        state_ref[2 * HDIM :, :] = jnp.zeros((PACK - 2 * HDIM, HALF), F32)
        for start, size in groups():
            columns = slice(start, start + size)
            for clip, tokens in enumerate(halves(count)):
                keys, _ = feature(out_ref[columns, tokens].astype(F32))
                values = out_ref[HALF + start : HALF + start + size, tokens]
                product = dot_left(keys, values, LAST)
                state_ref[clip * HDIM : (clip + 1) * HDIM, columns] = diagonal(product)
                state_ref[2 * HDIM + clip : 2 * HDIM + clip + 1, columns] = token_sum(keys)


def project_far(hidden, near, first, second, with_state):
    width, count = near.shape
    shapes = [jax.ShapeDtypeStruct((width, count), BF16)]
    if with_state:
        shapes.append(jax.ShapeDtypeStruct((PACK, HALF), F32))
    return pl.pallas_call(
        far_kernel,
        grid=(1,),
        out_shape=shapes,
        in_specs=[
            pl.BlockSpec((GROUP, count), lambda i: (3, 0)),
            pl.BlockSpec((width, count), lambda i: (0, 0)),
        ]
        + [pl.BlockSpec((GROUP // 2, width), lambda i: (0, 0))] * 2,
        out_specs=[pl.BlockSpec(shape.shape, lambda i: (0, 0)) for shape in shapes],
        compiler_params=params(40),
        cost_estimate=NO_COST,
        name="project_far",
    )(hidden, near, first, second)


def once(start, width, keep):
    row = lax.broadcasted_iota(jnp.int32, (width, 1), 0) + start
    return jnp.where(row < HDIM, keep, 1.0)


def middle_kernel(
    keep_ref, query_ref, grad_ref, state_ref, attention_ref, grad_query_ref, state_grad_ref
):
    count = query_ref.shape[1] // 2
    state_grad_ref[2 * HDIM :, :] = jnp.zeros((PACK - 2 * HDIM, HALF), F32)
    keep = keep_ref[0]
    for start, width in groups():
        rows = slice(start, start + width)
        ones = same_head(width).astype(BF16)
        for clip in range(2):
            tokens = slice(clip * count, (clip + 1) * count)
            mine = slice(clip * HDIM, (clip + 1) * HDIM)
            sums = slice(2 * HDIM + clip, 2 * HDIM + clip + 1)
            state = block_diagonal(state_ref[mine, rows])
            total = state_ref[sums, rows]
            total_column = column(total)
            query, slope = feature(query_ref[rows, tokens].astype(F32))
            grad = grad_ref[rows, tokens].astype(F32)
            numer = dot_wide(state, query, ((0,), (0,)))
            inverse = 1.0 / (dot_right(ones, query * total_column) + 1.0)
            quotient = numer * inverse
            attention_ref[rows, tokens] = quotient.astype(BF16)
            grad_numer = grad * inverse
            grad_denom = -dot_right(ones, grad * quotient) * inverse
            product = dot_wide(query, grad_numer, ((1,), (1,)))
            state_grad_ref[mine, rows] = diagonal(product)
            state_grad_ref[sums, rows] = token_sum(query * grad_denom)
            back = dot_wide(state, grad_numer) + grad_denom * total_column
            back = slope * back * once(start, width, keep)
            grad_query_ref[rows, tokens] = back.astype(BF16)


def make_middle(keep, query, grad, state):
    count = query.shape[1]
    return pl.pallas_call(
        middle_kernel,
        out_shape=(
            jax.ShapeDtypeStruct((HALF, count), BF16),
            jax.ShapeDtypeStruct((HALF, count), BF16),
            jax.ShapeDtypeStruct((PACK, HALF), F32),
        ),
        in_specs=[pl.BlockSpec(memory_space=pltpu.SMEM)] + [WHOLE] * 3,
        out_specs=(WHOLE,) * 3,
        compiler_params=params(24),
        cost_estimate=NO_COST,
        name="attention",
    )(keep, query, grad, state)


def pair_grad_kernel(keep_ref, pair_ref, state_grad_ref, out_ref):
    count = pair_ref.shape[1] // 2
    keep = keep_ref[0]
    for start, width in groups():
        rows = slice(start, start + width)
        value_rows = slice(HALF + start, HALF + start + width)
        factor = once(start, width, keep)
        for clip in range(2):
            tokens = slice(clip * count, (clip + 1) * count)
            sums = slice(2 * HDIM + clip, 2 * HDIM + clip + 1)
            state_grad = block_diagonal(state_grad_ref[clip * HDIM : (clip + 1) * HDIM, rows])
            total_grad = column(state_grad_ref[sums, rows])
            keys, slope = feature(pair_ref[rows, tokens].astype(F32))
            grad_keys = dot_left(state_grad, pair_ref[value_rows, tokens]) + total_grad
            grad_values = dot_wide(state_grad, keys, ((0,), (0,)))
            out_ref[rows, tokens] = (slope * grad_keys * factor).astype(BF16)
            out_ref[value_rows, tokens] = (grad_values * factor).astype(BF16)


def make_pair_grad(keep, pair, state_grad):
    return pl.pallas_call(
        pair_grad_kernel,
        out_shape=jax.ShapeDtypeStruct(pair.shape, BF16),
        in_specs=[pl.BlockSpec(memory_space=pltpu.SMEM)] + [WHOLE] * 2,
        out_specs=WHOLE,
        compiler_params=params(24),
        cost_estimate=NO_COST,
        name="pair_grad",
    )(keep, pair, state_grad)


def terms_kernel(blocks, grad_ref, *refs):
    for number in range(blocks):
        part = dot(refs[number][...], grad_ref[...], ((1,), (1,)))
        refs[blocks + number][...] = part.astype(BF16)


def weight_terms(hidden, grad, blocks, rows):
    width, count = grad.shape
    return pl.pallas_call(
        functools.partial(terms_kernel, len(blocks)),
        grid=(1,),
        out_shape=(jax.ShapeDtypeStruct((rows, width), BF16),) * len(blocks),
        in_specs=[pl.BlockSpec((width, count), lambda i: (0, 0))]
        + [pl.BlockSpec((rows, count), lambda i, b=block: (b, 0)) for block in blocks],
        out_specs=(pl.BlockSpec((rows, width), lambda i: (0, 0)),) * len(blocks),
        compiler_params=params(32),
        cost_estimate=NO_COST,
        name="weight_terms",
    )(grad, *([hidden] * len(blocks)))


def back_kernel(starts_ref, query_ref, pair_ref, *refs):
    pieces, (out_ref, wide_ref, plain_ref) = refs[:-3], refs[-3:]
    base = 0
    for query_rows, pair_rows in zip(pieces[:5], pieces[5:], strict=True):
        for start in range(0, query_rows.shape[0], 288):
            rows = slice(start, start + 288)
            part = dot(query_rows[rows, :], query_ref[...]) + dot(pair_rows[rows, :], pair_ref[...])
            wide_ref[base : base + 288, :] = part
            base += 288
    for number in range(16):
        low, high = number * ROWS, (16 + number) * ROWS
        unit = wide_ref[unit_rows(starts_ref, number), :]
        plain_ref[low : low + ROWS, :] = unit[:ROWS]
        plain_ref[high : high + ROWS, :] = unit[ROWS : 2 * ROWS]
    chunk = 112
    for start in range(0, 32 * ROWS, chunk):
        out_ref[start : start + chunk, :] = plain_ref[start : start + chunk, :].astype(BF16)


def back_project(starts, grad_query, grad_pair, query_pieces, pair_pieces, clip):
    count = grad_query.shape[1] // 2
    pieces = [*query_pieces, *pair_pieces]
    return pl.pallas_call(
        back_kernel,
        grid=(1,),
        out_shape=jax.ShapeDtypeStruct((32 * ROWS, count), BF16),
        in_specs=[
            pl.BlockSpec(memory_space=pltpu.SMEM),
            pl.BlockSpec((HALF, count), lambda i: (0, clip)),
            pl.BlockSpec((2 * HALF, count), lambda i: (0, clip)),
        ]
        + [pl.BlockSpec(piece.shape, lambda i: (0, 0)) for piece in pieces],
        out_specs=pl.BlockSpec((32 * ROWS, count), lambda i: (0, 0)),
        scratch_shapes=[pltpu.VMEM((ALL, count), F32), pltpu.VMEM((32 * ROWS, count), F32)],
        compiler_params=params(50),
        cost_estimate=NO_COST,
        name="back_project",
    )(starts, grad_query, grad_pair, *pieces)


def unit_starts(x, y, core):
    starts = []
    for at_y in range(4):
        for at_x in range(4):
            step_x, step_y = lax.rem(at_x - x + 4, 4), lax.rem(at_y - y + 4, 4)
            outer, inner = pick(core, step_x, step_y), pick(core, step_y, step_x)
            outer = jnp.where(outer == 2, 3, jnp.where(outer == 3, 2, outer))
            starts.append((outer * 4 + inner) * UNIT)
    return jnp.stack(starts).astype(jnp.int32)


def body(tokens, modulation, weight, cotangent):
    seq, dp = lax.axis_index("seq"), lax.axis_index("dp")
    x, y, z_lo = lax.rem(seq, 4), lax.rem(seq // 4, 4), seq // 16
    core = lax.rem(dp, 2)
    count, features = tokens.shape[1:]
    clip_length = count * lax.axis_size("seq")
    all_length = clip_length * lax.axis_size("dp")
    keep = jnp.where(core == 0, 1.0, 0.0).astype(F32).reshape(1)

    tokens_own = tokens[0].T
    tokens_other = send(tokens_own, "core")
    mods_own = modulation[0].T
    mods_other = send(modulation[0], "core").T
    grad_out = cotangent[0].T
    grad_out = jnp.concatenate(
        [head_half(grad_out, core, 0), send(head_half(grad_out, core, 0, other=True), "core")], axis=1
    )
    starts = unit_starts(x, y, core)

    group = ring_gather(gather_units(weight, z_lo, core), "middle")
    pair_group, query_group = group[:, : 2 * HALF], group[:, 2 * HALF :]
    half = GROUP // 2
    pair_ahead = send(pair_group, "last", -1)
    pair_behind = send(pair_group, "last", 1)
    hidden = make_hidden(starts, tokens_own, mods_own, 0)
    hidden = make_hidden(starts, tokens_other, mods_other, 1, hidden)
    pair_ahead, pair_behind, hidden = together(pair_ahead, pair_behind, hidden)
    pair_far_first = send(pair_ahead[:half], "last", -1)
    pair_far_second = send(pair_behind[half:], "last", 1)
    pair = project_near(hidden, (pair_group, pair_ahead, pair_behind))
    pair_far_first, pair_far_second, pair, query_group = together(
        pair_far_first, pair_far_second, pair, query_group
    )
    query_ahead = send(query_group, "last", -1)
    query_behind = send(query_group, "last", 1)
    pair, state = project_far(hidden, pair, pair_far_first, pair_far_second, True)

    parts = exchange(state, "last")
    *parts, query_ahead, query_behind = together(*parts, query_ahead, query_behind)
    state = ring_sum(state, parts)
    parts = exchange(state, "middle")
    query_far_first = send(query_ahead[:half], "last", -1)
    query_far_second = send(query_behind[half:], "last", 1)
    query = project_near(hidden, (query_group, query_ahead, query_behind))
    *parts, query, query_far_first, query_far_second = together(
        *parts, query, query_far_first, query_far_second
    )
    state = ring_sum(state, parts)
    part = send(state, "z_lo")
    (query,) = project_far(hidden, query, query_far_first, query_far_second, False)
    part, query = together(part, query)
    state = state + part

    attention, grad_query, state_grad = make_middle(keep, query, grad_out, state)
    parts = exchange(state_grad, "last")
    terms = weight_terms(hidden, grad_query, (3, 1, 2, 0), GROUP)
    *parts, terms = together(*parts, terms)
    state_grad = ring_sum(state_grad, parts)
    parts = exchange(state_grad, "middle")
    far_first = send(terms[0][:half], "last", 1)
    far_second = send(terms[0][half:], "last", -1)
    *parts, far_first, far_second = together(*parts, far_first, far_second)
    state_grad = ring_sum(state_grad, parts)
    part = send(state_grad, "z_lo")
    query_ahead_term = jnp.concatenate([add(terms[1][:half], far_first), terms[1][half:]])
    query_behind_term = jnp.concatenate([terms[2][:half], add(terms[2][half:], far_second)])
    part, query_ahead_term, query_behind_term = together(part, query_ahead_term, query_behind_term)
    state_grad = state_grad + part
    query_from_behind = send(query_ahead_term, "last", 1)
    query_from_ahead = send(query_behind_term, "last", -1)

    grad_pair = make_pair_grad(keep, pair, state_grad)
    soon = weight_terms(hidden, grad_pair, (6, 7, 3, 4), half)
    query_from_behind, query_from_ahead, soon = together(query_from_behind, query_from_ahead, soon)
    far_first = send(soon[0], "last", 1)
    far_second = send(soon[1], "last", -1)
    plain_ahead = send(soon[2], "last", 1)
    plain_behind = send(soon[3], "last", -1)
    grad_pair, attention, _ = together(grad_pair, attention, soon[0])
    later = weight_terms(hidden, grad_pair, (2, 5, 0, 1), half)
    far_first, far_second, later = together(far_first, far_second, later)
    summed_ahead = send(add(later[0], far_first), "last", 1)
    summed_behind = send(add(later[1], far_second), "last", -1)
    attention = head_join(attention[:, :count], send(attention[:, count:], "core"), core, 0)
    grad_pair, _ = together(grad_pair, later[2])
    back_args = (
        starts,
        grad_query,
        grad_pair,
        (query_group, query_ahead, query_behind, query_far_first, query_far_second),
        (pair_group, pair_ahead, pair_behind, pair_far_first, pair_far_second),
    )
    received = back_project(*back_args, 1)
    query_part = (
        terms[3].astype(F32) + query_from_behind.astype(F32) + query_from_ahead.astype(F32)
    ).astype(BF16)
    plain_ahead, plain_behind, summed_ahead, summed_behind, received, query_part = together(
        plain_ahead, plain_behind, summed_ahead, summed_behind, received, query_part
    )
    pair_part = jnp.concatenate(
        [
            later[2].astype(F32) + summed_ahead.astype(F32) + plain_behind.astype(F32),
            later[3].astype(F32) + plain_ahead.astype(F32) + summed_behind.astype(F32),
        ]
    ).astype(BF16)
    shards = jnp.split(jnp.concatenate([pair_part, query_part], axis=1), 4)
    far_first = send(shards[2][: UNIT // 2], "middle", 1)
    far_second = send(shards[2][UNIT // 2 :], "middle", -1)
    received = send(received, "core")
    grad_pair, _ = together(grad_pair, shards[2])
    grad_hidden = back_project(starts, grad_query, grad_pair, *back_args[3:], 0)
    far_first, far_second, grad_hidden = together(far_first, far_second, grad_hidden)
    ahead = jnp.concatenate([add(shards[1][: UNIT // 2], far_first), shards[1][UNIT // 2 :]])
    behind = jnp.concatenate([shards[3][: UNIT // 2], add(shards[3][UNIT // 2 :], far_second)])
    from_behind = send(ahead, "middle", 1)
    from_ahead = send(behind, "middle", -1)
    unit = (shards[0].astype(F32) + from_behind.astype(F32) + from_ahead.astype(F32)).astype(BF16)
    weight_grad = finish_weight(unit, z_lo, dp, core)
    weight_grad = weight_grad * (1.0 / math.sqrt(all_length))

    grad_hidden = grad_hidden.astype(F32) + received.astype(F32)
    values = tokens_own.astype(F32)
    inverse = lax.rsqrt(jnp.mean(values * values, axis=0, keepdims=True) + 1e-06)
    normed = values * inverse
    mod_grad = jnp.stack([jnp.sum(grad_hidden, axis=1), jnp.sum(grad_hidden * normed, axis=1)])
    for kind in ("last", "middle"):
        mod_grad = ring_sum(mod_grad, exchange(mod_grad, kind))
    mod_grad = (mod_grad + send(mod_grad, "z_lo")) * (1.0 / math.sqrt(clip_length))
    grad_normed = grad_hidden * (1.0 + mods_own[:, 1:2])
    mean = jnp.mean(grad_normed * normed, axis=0, keepdims=True)
    grad_tokens = (inverse * (grad_normed - normed * mean)).astype(BF16)
    return (attention.T[None], grad_tokens.T[None], weight_grad, mod_grad[None])


def solution(mesh):
    return jax.shard_map(
        body,
        mesh=mesh,
        in_specs=(P("dp", "seq", None), P("dp", None, None), P("seq", "dp"), P("dp", "seq", None)),
        out_specs=(P("dp", "seq", None), P("dp", "seq", None), P("seq", "dp"), P("dp", None, None)),
        check_vma=False,
    )
```

```python
import functools
import math

import jax
import jax.numpy as jnp
from jax import lax
from jax.experimental import pallas as pl
from jax.experimental.pallas import tpu as pltpu
from jax.sharding import PartitionSpec as P

HDIM = 32
AXES = ("seq", "dp")
ROWS = 70
UNIT = 144
COLS = 840
HALF = 576
GROUP = 4 * UNIT
ALL = 16 * UNIT
LANES = 128
PACK = 72
NEAR = 3 * GROUP
F32, BF16 = jnp.float32, jnp.bfloat16
WHOLE = pl.BlockSpec(memory_space=pltpu.VMEM)
ANYWHERE = pl.BlockSpec(memory_space=pl.ANY)


def place(index):
    seq, dp = divmod(index, 4)
    z_lo, rest = divmod(seq, 16)
    y, x = divmod(rest, 4)
    z_hi, core = divmod(dp, 2)
    return x, y, z_hi * 2 + z_lo, core


def index_of(x, y, z, core):
    x, y, z = x % 4, y % 4, z % 4
    return ((z % 2) * 16 + y * 4 + x) * 4 + (z // 2) * 2 + core


def route(kind, offset):
    pairs = []
    for index in range(128):
        x, y, z, core = place(index)
        if kind == "z":
            target = index_of(x, y, z + offset, core)
        elif kind == "z_lo":
            target = index_of(x, y, z ^ 1, core)
        elif kind == "z_hi":
            target = index_of(x, y, z ^ 2, core)
        elif kind == "z_hi_core":
            target = index_of(x, y, z ^ 2, 1 - core)
        elif kind == "core":
            target = index_of(x, y, z, 1 - core)
        elif (kind == "last") == (core == 0):
            target = index_of(x + offset, y, z, core)
        else:
            target = index_of(x, y + offset, z, core)
        pairs.append((index, target))
    return pairs


def send(value, kind, offset=0):
    return lax.ppermute(value, AXES, route(kind, offset))


def together(*values):
    return lax.optimization_barrier(values)


def add(left, right):
    return (left.astype(F32) + right.astype(F32)).astype(BF16)


def exchange(value, kind):
    return send(value, kind, 2), send(value, kind, -1), send(value, kind, 1)


def ring_sum(value, parts):
    far, ahead, behind = (part.astype(F32) for part in parts)
    return (value + far) + (ahead + behind)


def pick(core, on_zero, on_one):
    return jnp.where(core == 0, on_zero, on_one)


def head_half(array, core, axis, other=False):
    size = array.shape[axis]
    low = lax.slice_in_dim(array, 0, HALF, axis=axis)
    high = lax.slice_in_dim(array, size - HALF, size, axis=axis)
    return pick(core, high, low) if other else pick(core, low, high)


def head_join(mine, other, core, axis):
    second = lax.slice_in_dim(pick(core, other, mine), HDIM, HALF, axis=axis)
    return jnp.concatenate([pick(core, mine, other), second], axis=axis)


def gather_units(weight, z_lo, core, extra):
    blocks, extra = together(lax.all_gather(weight, "dp"), extra)
    columns = jnp.concatenate([blocks[i] for i in range(4)], axis=1)
    third = 4 * COLS // 3
    query, keys, values = (
        head_half(columns[:, i * third : (i + 1) * third], core, 1) for i in range(3)
    )
    mine = jnp.concatenate([keys, values, query], axis=1)
    other = send(mine, "z_lo")
    unit = jnp.concatenate([pick(z_lo, mine, other), pick(z_lo, other, mine)])
    return jnp.pad(unit, ((0, UNIT - 2 * ROWS), (0, 0))), extra


def finish_weight(unit, z_lo, dp, core):
    first, second = unit[:ROWS], unit[ROWS : 2 * ROWS]
    mine = add(pick(z_lo, first, second), send(pick(z_lo, second, first), "z_lo"))
    zero = jnp.zeros((ROWS, HALF), BF16)
    columns = jnp.concatenate(
        [head_join(mine[:, i * HALF : (i + 1) * HALF], zero, core, 1) for i in (2, 0, 1)], axis=1
    )
    blocks = jnp.stack([columns[:, i * COLS : (i + 1) * COLS] for i in range(4)])

    def block(flip):
        return lax.dynamic_index_in_dim(blocks, dp ^ flip, 0, keepdims=False)

    by_z = send(block(2), "z_hi")
    by_both = send(block(3), "z_hi_core")
    by_core = send(block(1), "core")
    return (block(0).astype(F32) + by_core.astype(F32)) + (by_z.astype(F32) + by_both.astype(F32))


def params(mebibytes):
    return pltpu.CompilerParams(vmem_limit_bytes=mebibytes * 1024 * 1024)


NO_COST = pl.CostEstimate(flops=0, bytes_accessed=0, transcendentals=0)


def split(value):
    high = value.astype(BF16)
    return high, (value - high.astype(F32)).astype(BF16)


def dot(left, right, dims=((1,), (0,))):
    return lax.dot_general(left, right, (dims, ((), ())), preferred_element_type=F32)


def dot_wide(left, right, dims=((1,), (0,))):
    left_high, left_low = split(left)
    right_high, right_low = split(right)
    return dot(left_high, right_high, dims) + (
        dot(left_low, right_high, dims) + dot(left_high, right_low, dims)
    )


def dot_left(left, right, dims=((1,), (0,))):
    high, low = split(left)
    return dot(high, right, dims) + dot(low, right, dims)


def dot_right(left, right, dims=((1,), (0,))):
    high, low = split(right)
    return dot(left, high, dims) + dot(left, low, dims)


def feature(values):
    lower = jnp.exp(jnp.minimum(values, 0.0))
    return jnp.where(values > 0, values + 1.0, lower), jnp.where(values > 0, 1.0, lower)


def same_head(size):
    row = lax.broadcasted_iota(jnp.int32, (size, size), 0) // HDIM
    return row == lax.broadcasted_iota(jnp.int32, (size, size), 1) // HDIM


def diagonal(product):
    width = product.shape[1]
    kept = jnp.where(same_head(width), product, 0.0)
    total = kept[:HDIM]
    for start in range(HDIM, width, HDIM):
        total = total + kept[start : start + HDIM]
    return total


def block_diagonal(blocks):
    width = blocks.shape[1]
    tiled = jnp.concatenate([blocks] * (width // HDIM), axis=0)
    return jnp.where(same_head(width), tiled, 0.0)


def column(row):
    width = row.shape[1]
    index = lax.broadcasted_iota(jnp.int32, (width, width), 0)
    same = index == lax.broadcasted_iota(jnp.int32, (width, width), 1)
    return jnp.sum(jnp.where(same, row, 0.0), axis=1, keepdims=True)


def token_sum(array):
    ones = jnp.ones((16, array.shape[1]), BF16)
    return dot_right(ones, array, ((1,), (1,)))[:1]


def groups():
    return [(start, min(LANES, HALF - start)) for start in range(0, HALF, LANES)]


def unit_rows(starts_ref, number):
    return pl.ds(pl.multiple_of(starts_ref[number], 16), UNIT)


def hidden_kernel(starts_ref, *refs):
    out_ref, wide_ref = refs[-2:]
    chunk = 112
    for clip in range(2):
        tokens_ref, mods_ref = refs[2 * clip : 2 * clip + 2]
        features, count = tokens_ref.shape
        total = jnp.zeros((1, count), F32)
        for start in range(0, features, chunk):
            values = tokens_ref[start : start + chunk, :].astype(F32)
            total = total + jnp.sum(values * values, axis=0, keepdims=True)
        inverse = lax.rsqrt(total * (1.0 / features) + 1e-06)
        for start in range(0, features, chunk):
            rows = slice(start, start + chunk)
            values = tokens_ref[rows, :].astype(F32) * inverse
            wide_ref[rows, :] = values * (1.0 + mods_ref[rows, 1:2]) + mods_ref[rows, 0:1]
        for number in range(16):
            low, high = number * ROWS, (16 + number) * ROWS
            parts = [
                wide_ref[low : low + ROWS, :],
                wide_ref[high : high + ROWS, :],
                jnp.zeros((UNIT - 2 * ROWS, count), F32),
            ]
            tokens = slice(clip * count, (clip + 1) * count)
            out_ref[unit_rows(starts_ref, number), tokens] = jnp.concatenate(parts).astype(BF16)


def make_hidden(starts, *arrays):
    features, count = arrays[0].shape
    return pl.pallas_call(
        hidden_kernel,
        out_shape=jax.ShapeDtypeStruct((ALL, 2 * count), BF16),
        in_specs=[pl.BlockSpec(memory_space=pltpu.SMEM)] + [WHOLE] * 4,
        out_specs=WHOLE,
        scratch_shapes=[pltpu.VMEM((features, count), F32)],
        compiler_params=params(24),
        cost_estimate=NO_COST,
        name="hidden",
    )(starts, *arrays)


def chunks(width):
    size = 384 if width % 384 == 0 else 256
    return [slice(start, min(start + size, width)) for start in range(0, width, size)]


def halves(count):
    return [slice(0, count // 2), slice(count // 2, count)]


FIRST, LAST = ((0,), (0,)), ((1,), (1,))


def near_kernel(numbers, hidden_ref, *refs):
    out_ref = refs[-1]
    for rows in chunks(out_ref.shape[0]):
        for tokens in halves(out_ref.shape[1]):
            total = refs[len(numbers)][rows, tokens] if len(refs) > len(numbers) + 1 else 0.0
            for number, piece_ref in zip(numbers, refs, strict=False):
                depth = piece_ref.shape[0]
                part = hidden_ref[number * depth : (number + 1) * depth, tokens]
                total = total + dot(piece_ref[:, rows], part, FIRST)
            out_ref[rows, tokens] = total


def project_near(hidden, pieces, numbers, before=()):
    width, count = pieces[0].shape[1], hidden.shape[1]
    return pl.pallas_call(
        functools.partial(near_kernel, numbers),
        out_shape=jax.ShapeDtypeStruct((width, count), F32),
        in_specs=[WHOLE] * (1 + len(pieces) + len(before)),
        out_specs=WHOLE,
        compiler_params=params(24),
        cost_estimate=NO_COST,
        name="project_near",
    )(hidden, *pieces, *before)


def far_kernel(hidden_ref, near_ref, first_ref, second_ref, out_ref, *state_refs):
    half = GROUP // 2
    width, count = out_ref.shape
    for rows in chunks(width):
        for tokens in halves(count):
            total = near_ref[rows, tokens]
            total += dot(first_ref[:, rows], hidden_ref[NEAR : NEAR + half, tokens], FIRST)
            total += dot(second_ref[:, rows], hidden_ref[NEAR + half :, tokens], FIRST)
            out_ref[rows, tokens] = total.astype(BF16)
    for state_ref in state_refs:
        state_ref[2 * HDIM :, :] = jnp.zeros((PACK - 2 * HDIM, HALF), F32)
        for start, size in groups():
            columns = slice(start, start + size)
            for clip, tokens in enumerate(halves(count)):
                keys, _ = feature(out_ref[columns, tokens].astype(F32))
                values = out_ref[HALF + start : HALF + start + size, tokens]
                product = dot_left(keys, values, LAST)
                state_ref[clip * HDIM : (clip + 1) * HDIM, columns] = diagonal(product)
                state_ref[2 * HDIM + clip : 2 * HDIM + clip + 1, columns] = token_sum(keys)


def project_far(hidden, near, first, second, with_state):
    width, count = near.shape
    shapes = [jax.ShapeDtypeStruct((width, count), BF16)]
    if with_state:
        shapes.append(jax.ShapeDtypeStruct((PACK, HALF), F32))
    return pl.pallas_call(
        far_kernel,
        out_shape=shapes,
        in_specs=[WHOLE] * 4,
        out_specs=[WHOLE] * len(shapes),
        compiler_params=params(24),
        cost_estimate=NO_COST,
        name="project_far",
    )(hidden, near, first, second)


def once(start, width, keep):
    row = lax.broadcasted_iota(jnp.int32, (width, 1), 0) + start
    return jnp.where(row < HDIM, keep, 1.0)


def middle_kernel(
    keep_ref, query_ref, grad_ref, state_ref, attention_ref, grad_query_ref, state_grad_ref
):
    count = query_ref.shape[1] // 2
    state_grad_ref[2 * HDIM :, :] = jnp.zeros((PACK - 2 * HDIM, HALF), F32)
    keep = keep_ref[0]
    for start, width in groups():
        rows = slice(start, start + width)
        ones = same_head(width).astype(BF16)
        for clip in range(2):
            tokens = slice(clip * count, (clip + 1) * count)
            mine = slice(clip * HDIM, (clip + 1) * HDIM)
            sums = slice(2 * HDIM + clip, 2 * HDIM + clip + 1)
            state = block_diagonal(state_ref[mine, rows])
            total = state_ref[sums, rows]
            total_column = column(total)
            query, slope = feature(query_ref[rows, tokens].astype(F32))
            grad = grad_ref[rows, tokens].astype(F32)
            numer = dot_wide(state, query, ((0,), (0,)))
            inverse = 1.0 / (dot_right(ones, query * total_column) + 1.0)
            quotient = numer * inverse
            attention_ref[rows, tokens] = quotient.astype(BF16)
            grad_numer = grad * inverse
            grad_denom = -dot_right(ones, grad * quotient) * inverse
            product = dot_wide(query, grad_numer, ((1,), (1,)))
            state_grad_ref[mine, rows] = diagonal(product)
            state_grad_ref[sums, rows] = token_sum(query * grad_denom)
            back = dot_wide(state, grad_numer) + grad_denom * total_column
            back = slope * back * once(start, width, keep)
            grad_query_ref[rows, tokens] = back.astype(BF16)


def make_middle(keep, query, grad, state):
    count = query.shape[1]
    return pl.pallas_call(
        middle_kernel,
        out_shape=(
            jax.ShapeDtypeStruct((HALF, count), BF16),
            jax.ShapeDtypeStruct((HALF, count), BF16),
            jax.ShapeDtypeStruct((PACK, HALF), F32),
        ),
        in_specs=[pl.BlockSpec(memory_space=pltpu.SMEM)] + [WHOLE] * 3,
        out_specs=(WHOLE,) * 3,
        compiler_params=params(24),
        cost_estimate=NO_COST,
        name="attention",
    )(keep, query, grad, state)


def pair_grad_kernel(keep_ref, pair_ref, state_grad_ref, out_ref):
    count = pair_ref.shape[1] // 2
    keep = keep_ref[0]
    for start, width in groups():
        rows = slice(start, start + width)
        value_rows = slice(HALF + start, HALF + start + width)
        factor = once(start, width, keep)
        for clip in range(2):
            tokens = slice(clip * count, (clip + 1) * count)
            sums = slice(2 * HDIM + clip, 2 * HDIM + clip + 1)
            state_grad = block_diagonal(state_grad_ref[clip * HDIM : (clip + 1) * HDIM, rows])
            total_grad = column(state_grad_ref[sums, rows])
            keys, slope = feature(pair_ref[rows, tokens].astype(F32))
            grad_keys = dot_left(state_grad, pair_ref[value_rows, tokens]) + total_grad
            grad_values = dot_wide(state_grad, keys, ((0,), (0,)))
            out_ref[rows, tokens] = (slope * grad_keys * factor).astype(BF16)
            out_ref[value_rows, tokens] = (grad_values * factor).astype(BF16)


def make_pair_grad(keep, pair, state_grad):
    return pl.pallas_call(
        pair_grad_kernel,
        out_shape=jax.ShapeDtypeStruct(pair.shape, BF16),
        in_specs=[pl.BlockSpec(memory_space=pltpu.SMEM)] + [WHOLE] * 2,
        out_specs=WHOLE,
        compiler_params=params(24),
        cost_estimate=NO_COST,
        name="pair_grad",
    )(keep, pair, state_grad)


def terms_kernel(blocks, grad_ref, hidden_ref, *outs):
    for number, out_ref in zip(blocks, outs, strict=True):
        rows = slice(number * out_ref.shape[0], (number + 1) * out_ref.shape[0])
        out_ref[...] = dot(hidden_ref[rows, :], grad_ref[...], LAST).astype(BF16)


def weight_terms(hidden, grad, blocks, rows):
    return pl.pallas_call(
        functools.partial(terms_kernel, blocks),
        out_shape=(jax.ShapeDtypeStruct((rows, grad.shape[0]), BF16),) * len(blocks),
        in_specs=[WHOLE] * 2,
        out_specs=(WHOLE,) * len(blocks),
        compiler_params=params(20),
        cost_estimate=NO_COST,
        name="weight_terms",
    )(grad, hidden)


def parts_of(pieces, size):
    return [(piece, start) for piece in pieces for start in range(0, piece.shape[0], size)]


def back_to_plain(starts_ref, query_ref, pair_ref, tokens, pieces, wide_ref, plain_ref):
    size = GROUP // 2
    for base, (query_rows, start), (pair_rows, pair_start) in zip(
        range(0, ALL, size),
        parts_of([piece for piece in pieces if piece.shape[1] == HALF], size),
        parts_of([piece for piece in pieces if piece.shape[1] != HALF], size),
        strict=True,
    ):
        part = dot(query_rows[start : start + size, :], query_ref[:, tokens])
        part = part + dot(pair_rows[pair_start : pair_start + size, :], pair_ref[:, tokens])
        wide_ref[base : base + size, :] = part
    for number in range(16):
        low, high = number * ROWS, (16 + number) * ROWS
        unit = wide_ref[unit_rows(starts_ref, number), :]
        plain_ref[low : low + ROWS, :] = unit[:ROWS]
        plain_ref[high : high + ROWS, :] = unit[ROWS : 2 * ROWS]


def row_chunks(size):
    return [slice(start, min(start + size, 32 * ROWS)) for start in range(0, 32 * ROWS, size)]


def back_other_kernel(starts_ref, query_ref, pair_ref, *refs):
    out_ref, wide_ref, plain_ref = refs[-3:]
    tokens = halves(query_ref.shape[1])[1]
    back_to_plain(starts_ref, query_ref, pair_ref, tokens, refs[:-3], wide_ref, plain_ref)
    for rows in row_chunks(112):
        out_ref[rows, :] = plain_ref[rows, :].astype(BF16)


def back_own_kernel(starts_ref, query_ref, pair_ref, received_ref, tokens_ref, mods_ref, *refs):
    out_ref, sums_ref, wide_ref, plain_ref = refs[-4:]
    tokens = halves(query_ref.shape[1])[0]
    back_to_plain(starts_ref, query_ref, pair_ref, tokens, refs[:-4], wide_ref, plain_ref)
    features, count = tokens_ref.shape
    total = jnp.zeros((1, count), F32)
    for rows in row_chunks(112):
        values = tokens_ref[rows, :].astype(F32)
        total = total + jnp.sum(values * values, axis=0, keepdims=True)
    inverse = lax.rsqrt(total * (1.0 / features) + 1e-06)
    mean = jnp.zeros((1, count), F32)
    for rows in row_chunks(112):
        normed = tokens_ref[rows, :].astype(F32) * inverse
        grad = plain_ref[rows, :] + received_ref[rows, :].astype(F32)
        product = grad * normed
        plain_ref[rows, :] = grad
        wide_ref[rows, :] = product
        product = product * (1.0 + mods_ref[rows, 1:2])
        mean = mean + jnp.sum(product, axis=0, keepdims=True)
    for rows in row_chunks(640):
        sums_ref[0:1, rows] = token_sum(plain_ref[rows, :])
        sums_ref[1:2, rows] = token_sum(wide_ref[rows, :])
    mean = mean * (1.0 / features)
    for rows in row_chunks(112):
        normed = tokens_ref[rows, :].astype(F32) * inverse
        grad = plain_ref[rows, :] * (1.0 + mods_ref[rows, 1:2])
        out_ref[rows, :] = (inverse * (grad - normed * mean)).astype(BF16)


def back_project(starts, grad_query, grad_pair, pieces, own=()):
    count, features = grad_query.shape[1] // 2, 32 * ROWS
    out = [jax.ShapeDtypeStruct((features, count), BF16)]
    if own:
        out.append(jax.ShapeDtypeStruct((2, features), F32))
    return pl.pallas_call(
        back_own_kernel if own else back_other_kernel,
        out_shape=out,
        in_specs=[pl.BlockSpec(memory_space=pltpu.SMEM)] + [WHOLE] * (2 + len(own) + len(pieces)),
        out_specs=[WHOLE] * len(out),
        scratch_shapes=[pltpu.VMEM((ALL, count), F32), pltpu.VMEM((features, count), F32)],
        compiler_params=params(34),
        cost_estimate=NO_COST,
        name="back_project",
    )(starts, grad_query, grad_pair, *own, *pieces)


def unit_starts(x, y, core):
    starts = []
    for at_y in range(4):
        for at_x in range(4):
            step_x, step_y = lax.rem(at_x - x + 4, 4), lax.rem(at_y - y + 4, 4)
            outer, inner = pick(core, step_x, step_y), pick(core, step_y, step_x)
            outer = jnp.where(outer == 2, 3, jnp.where(outer == 3, 2, outer))
            starts.append((outer * 4 + inner) * UNIT)
    return jnp.stack(starts).astype(jnp.int32)


def body(tokens, modulation, weight, cotangent):
    seq, dp = lax.axis_index("seq"), lax.axis_index("dp")
    x, y, z_lo = lax.rem(seq, 4), lax.rem(seq // 4, 4), seq // 16
    core = lax.rem(dp, 2)
    count, features = tokens.shape[1:]
    clip_length = count * lax.axis_size("seq")
    all_length = clip_length * lax.axis_size("dp")
    keep = jnp.where(core == 0, 1.0, 0.0).astype(F32).reshape(1)

    starts = unit_starts(x, y, core)
    half = GROUP // 2
    unit, (tokens, cotangent, modulation) = gather_units(
        weight, z_lo, core, (tokens, cotangent, modulation)
    )
    tokens_own = tokens[0].T
    tokens_other = send(tokens_own, "core")
    mods_own = modulation[0].T
    mods_other = send(modulation[0], "core").T
    grad_out = cotangent[0].T
    grad_out = jnp.concatenate(
        [head_half(grad_out, core, 0), send(head_half(grad_out, core, 0, other=True), "core")], axis=1
    )
    unit, tokens_other, mods_other, grad_out = together(unit, tokens_other, mods_other, grad_out)
    ahead, behind = send(unit, "middle", -1), send(unit, "middle", 1)
    ahead, behind, tokens_other = together(ahead, behind, tokens_other)
    far_first = send(ahead[: UNIT // 2], "middle", -1)
    far_second = send(behind[UNIT // 2 :], "middle", 1)
    group = jnp.concatenate([unit, ahead, far_first, far_second, behind])
    pair_group, query_group = group[:, : 2 * HALF], group[:, 2 * HALF :]
    pair_first, pair_second = pair_group[:half], pair_group[half:]

    ahead_first = send(pair_first, "last", -1)
    behind_second = send(pair_second, "last", 1)
    ahead_second = send(pair_second, "last", -1)
    behind_first = send(pair_first, "last", 1)
    hidden = make_hidden(starts, tokens_own, mods_own, tokens_other, mods_other)
    pair = project_near(hidden, (pair_first, pair_second), (0, 1))
    ahead_first, behind_second, ahead_second, behind_first, pair, query_group = together(
        ahead_first, behind_second, ahead_second, behind_first, pair, query_group
    )
    pair_far_first = send(ahead_first, "last", -1)
    pair_far_second = send(behind_second, "last", 1)
    pair_near = (ahead_first, ahead_second, behind_first, behind_second)
    pair = project_near(hidden, pair_near, (2, 3, 4, 5), (pair,))
    pair_far_first, pair_far_second, pair, query_group = together(
        pair_far_first, pair_far_second, pair, query_group
    )
    query_ahead = send(query_group, "last", -1)
    query_behind = send(query_group, "last", 1)
    pair, state = project_far(hidden, pair, pair_far_first, pair_far_second, True)

    parts = exchange(state, "last")
    *parts, query_ahead, query_behind = together(*parts, query_ahead, query_behind)
    state = ring_sum(state, parts)
    parts = exchange(state, "middle")
    query_far_first = send(query_ahead[:half], "last", -1)
    query_far_second = send(query_behind[half:], "last", 1)
    query = project_near(hidden, (query_group, query_ahead, query_behind), (0, 1, 2))
    *parts, query, query_far_first, query_far_second = together(
        *parts, query, query_far_first, query_far_second
    )
    state = ring_sum(state, parts)
    part = send(state, "z_lo")
    (query,) = project_far(hidden, query, query_far_first, query_far_second, False)
    part, query = together(part, query)
    state = state + part

    attention, grad_query, state_grad = make_middle(keep, query, grad_out, state)
    parts = exchange(state_grad.astype(BF16), "last")
    terms = weight_terms(hidden, grad_query, (6, 7, 2, 3, 4, 5, 0, 1), half)
    *parts, terms = together(*parts, terms)
    state_grad = ring_sum(state_grad, parts)
    parts = exchange(state_grad.astype(BF16), "middle")
    query_far = send(terms[0], "last", 1), send(terms[1], "last", -1)
    *parts, attention = together(*parts, attention)
    state_grad = ring_sum(state_grad, parts)
    part = send(state_grad.astype(BF16), "z_lo")
    other_attention = send(attention[:, count:], "core")
    query_sums = add(terms[2], query_far[0]), add(terms[5], query_far[1])
    query_ahead_term = jnp.concatenate([query_sums[0], terms[3]])
    query_behind_term = jnp.concatenate([terms[4], query_sums[1]])
    part, query_ahead_term, query_behind_term, other_attention = together(
        part, query_ahead_term, query_behind_term, other_attention
    )
    state_grad = state_grad + part.astype(F32)

    grad_pair = make_pair_grad(keep, pair, state_grad)
    soon = weight_terms(hidden, grad_pair, (6, 7, 3, 4), half)
    far_first = send(soon[0], "last", 1)
    far_second = send(soon[1], "last", -1)
    plain_ahead = send(soon[2], "last", 1)
    plain_behind = send(soon[3], "last", -1)
    pieces = (query_group, query_ahead, query_behind, query_far_first, query_far_second)
    pieces = (*pieces, pair_first, pair_second, *pair_near, pair_far_first, pair_far_second)
    grad_pair, other_attention, _ = together(grad_pair, other_attention, soon[0])
    (received,) = back_project(starts, grad_query, grad_pair, pieces)
    later = weight_terms(hidden, grad_pair, (2, 5, 0, 1), half)
    attention = head_join(attention[:, :count], other_attention, core, 0)
    far_first, far_second, plain_ahead, plain_behind, later, received, attention = together(
        far_first, far_second, plain_ahead, plain_behind, later, received, attention
    )
    received = send(received, "core")
    summed_ahead = send(add(later[0], far_first), "last", 1)
    summed_behind = send(add(later[1], far_second), "last", -1)
    query_ahead_term, query_behind_term, _ = together(
        query_ahead_term, query_behind_term, later[2]
    )
    query_from_behind = send(query_ahead_term, "last", 1)
    query_from_ahead = send(query_behind_term, "last", -1)
    own = (received, tokens_own, mods_own)
    grad_tokens, mod_grad = back_project(starts, grad_query, grad_pair, pieces, own)
    summed_ahead, summed_behind, query_from_behind, query_from_ahead, mod_grad = together(
        summed_ahead, summed_behind, query_from_behind, query_from_ahead, mod_grad
    )
    query_part = jnp.concatenate([terms[6], terms[7]]).astype(F32)
    query_part = query_part + query_from_behind.astype(F32) + query_from_ahead.astype(F32)
    pair_part = jnp.concatenate(
        [
            later[2].astype(F32) + summed_ahead.astype(F32) + plain_behind.astype(F32),
            later[3].astype(F32) + plain_ahead.astype(F32) + summed_behind.astype(F32),
        ]
    )
    group = jnp.concatenate([pair_part, query_part], axis=1).astype(BF16)
    own, ahead, far, behind = jnp.split(group, 4)
    far_first = send(far[: UNIT // 2], "middle", 1)
    far_second = send(far[UNIT // 2 :], "middle", -1)
    parts = exchange(mod_grad, "last")
    *parts, far_first, far_second = together(*parts, far_first, far_second)
    mod_grad = ring_sum(mod_grad, parts)
    ahead = jnp.concatenate([add(ahead[: UNIT // 2], far_first), ahead[UNIT // 2 :]])
    behind = jnp.concatenate([behind[: UNIT // 2], add(behind[UNIT // 2 :], far_second)])
    from_behind = send(ahead, "middle", 1)
    from_ahead = send(behind, "middle", -1)
    parts = exchange(mod_grad, "middle")
    *parts, from_behind, from_ahead = together(*parts, from_behind, from_ahead)
    mod_grad = ring_sum(mod_grad, parts)
    mod_grad = (mod_grad + send(mod_grad, "z_lo")) * (1.0 / math.sqrt(clip_length))
    unit = (own.astype(F32) + from_behind.astype(F32) + from_ahead.astype(F32)).astype(BF16)
    weight_grad = finish_weight(unit, z_lo, dp, core)
    weight_grad = weight_grad * (1.0 / math.sqrt(all_length))
    return (attention.T[None], grad_tokens.T[None], weight_grad, mod_grad[None])


def solution(mesh):
    return jax.shard_map(
        body,
        mesh=mesh,
        in_specs=(P("dp", "seq", None), P("dp", None, None), P("seq", "dp"), P("dp", "seq", None)),
        out_specs=(P("dp", "seq", None), P("dp", "seq", None), P("seq", "dp"), P("dp", None, None)),
        check_vma=False,
    )
```

```python
import functools
import math

import jax
import jax.numpy as jnp
from jax import lax
from jax.experimental import pallas as pl
from jax.experimental.pallas import tpu as pltpu
from jax.sharding import PartitionSpec as P

HDIM = 32
AXES = ("seq", "dp")
ROWS = 70
UNIT = 144
COLS = 840
HALF = 576
GROUP = 4 * UNIT
ALL = 16 * UNIT
LANES = 128
PACK = 72
NEAR = 3 * GROUP
F32, BF16 = jnp.float32, jnp.bfloat16
WHOLE = pl.BlockSpec(memory_space=pltpu.VMEM)
ANYWHERE = pl.BlockSpec(memory_space=pl.ANY)


def place(index):
    seq, dp = divmod(index, 4)
    z_lo, rest = divmod(seq, 16)
    y, x = divmod(rest, 4)
    z_hi, core = divmod(dp, 2)
    return x, y, z_hi * 2 + z_lo, core


def index_of(x, y, z, core):
    x, y, z = x % 4, y % 4, z % 4
    return ((z % 2) * 16 + y * 4 + x) * 4 + (z // 2) * 2 + core


def route(kind, offset):
    pairs = []
    for index in range(128):
        x, y, z, core = place(index)
        if kind == "z":
            target = index_of(x, y, z + offset, core)
        elif kind == "z_lo":
            target = index_of(x, y, z ^ 1, core)
        elif kind == "z_hi":
            target = index_of(x, y, z ^ 2, core)
        elif kind == "core":
            target = index_of(x, y, z, 1 - core)
        elif (kind == "last") == (core == 0):
            target = index_of(x + offset, y, z, core)
        else:
            target = index_of(x, y + offset, z, core)
        pairs.append((index, target))
    return pairs


def send(value, kind, offset=0):
    return lax.ppermute(value, AXES, route(kind, offset))


def together(*values):
    return lax.optimization_barrier(values)


def add(left, right):
    return (left.astype(F32) + right.astype(F32)).astype(BF16)


def exchange(value, kind):
    return send(value, kind, 2), send(value, kind, -1), send(value, kind, 1)


def ring_sum(value, parts):
    far, ahead, behind = (part.astype(F32) for part in parts)
    return (value + far) + (ahead + behind)


def pick(core, on_zero, on_one):
    return jnp.where(core == 0, on_zero, on_one)


def head_half(array, core, axis, other=False):
    size = array.shape[axis]
    low = lax.slice_in_dim(array, 0, HALF, axis=axis)
    high = lax.slice_in_dim(array, size - HALF, size, axis=axis)
    return pick(core, high, low) if other else pick(core, low, high)


def head_join(mine, other, core, axis):
    second = lax.slice_in_dim(pick(core, other, mine), HDIM, HALF, axis=axis)
    return jnp.concatenate([pick(core, mine, other), second], axis=axis)


def gather_units(weight, z_lo, core, extra):
    blocks, extra = together(lax.all_gather(weight, "dp"), extra)
    columns = jnp.concatenate([blocks[i] for i in range(4)], axis=1)
    third = 4 * COLS // 3
    query, keys, values = (
        head_half(columns[:, i * third : (i + 1) * third], core, 1) for i in range(3)
    )
    mine = jnp.concatenate([keys, values, query], axis=1)
    other = send(mine, "z_lo")
    unit = jnp.concatenate([pick(z_lo, mine, other), pick(z_lo, other, mine)])
    return jnp.pad(unit, ((0, UNIT - 2 * ROWS), (0, 0))), extra


def finish_weight(unit, z_lo, dp, core):
    first, second = unit[:ROWS], unit[ROWS : 2 * ROWS]
    mine = add(pick(z_lo, first, second), send(pick(z_lo, second, first), "z_lo"))
    zero = jnp.zeros((ROWS, HALF), BF16)
    columns = jnp.concatenate(
        [head_join(mine[:, i * HALF : (i + 1) * HALF], zero, core, 1) for i in (2, 0, 1)], axis=1
    )
    blocks = jnp.stack([columns[:, i * COLS : (i + 1) * COLS] for i in range(4)])

    def block(flip):
        return lax.dynamic_index_in_dim(blocks, dp ^ flip, 0, keepdims=False)

    by_core = send(jnp.stack([block(1), block(3)]), "core")
    mine = block(0).astype(F32) + by_core[0].astype(F32)
    return mine + send(add(block(2), by_core[1]), "z_hi").astype(F32)


def params(mebibytes):
    return pltpu.CompilerParams(vmem_limit_bytes=mebibytes * 1024 * 1024)


NO_COST = pl.CostEstimate(flops=0, bytes_accessed=0, transcendentals=0)


def split(value):
    high = value.astype(BF16)
    return high, (value - high.astype(F32)).astype(BF16)


def dot(left, right, dims=((1,), (0,))):
    return lax.dot_general(left, right, (dims, ((), ())), preferred_element_type=F32)


def dot_wide(left, right, dims=((1,), (0,))):
    left_high, left_low = split(left)
    right_high, right_low = split(right)
    return dot(left_high, right_high, dims) + (
        dot(left_low, right_high, dims) + dot(left_high, right_low, dims)
    )


def dot_left(left, right, dims=((1,), (0,))):
    high, low = split(left)
    return dot(high, right, dims) + dot(low, right, dims)


def dot_right(left, right, dims=((1,), (0,))):
    high, low = split(right)
    return dot(left, high, dims) + dot(left, low, dims)


def feature(values):
    lower = jnp.exp(jnp.minimum(values, 0.0))
    return jnp.where(values > 0, values + 1.0, lower), jnp.where(values > 0, 1.0, lower)


def same_head(size):
    row = lax.broadcasted_iota(jnp.int32, (size, size), 0) // HDIM
    return row == lax.broadcasted_iota(jnp.int32, (size, size), 1) // HDIM


def diagonal(product):
    width = product.shape[1]
    kept = jnp.where(same_head(width), product, 0.0)
    total = kept[:HDIM]
    for start in range(HDIM, width, HDIM):
        total = total + kept[start : start + HDIM]
    return total


def block_diagonal(blocks):
    width = blocks.shape[1]
    tiled = jnp.concatenate([blocks] * (width // HDIM), axis=0)
    return jnp.where(same_head(width), tiled, 0.0)


def column(row):
    width = row.shape[1]
    index = lax.broadcasted_iota(jnp.int32, (width, width), 0)
    same = index == lax.broadcasted_iota(jnp.int32, (width, width), 1)
    return jnp.sum(jnp.where(same, row, 0.0), axis=1, keepdims=True)


def token_sum(array):
    ones = jnp.ones((16, array.shape[1]), BF16)
    return dot_right(ones, array, ((1,), (1,)))[:1]


def groups():
    return [(start, min(LANES, HALF - start)) for start in range(0, HALF, LANES)]


MARK = jax.ShapeDtypeStruct((8, LANES), F32)
SCALARS = pl.BlockSpec(memory_space=pltpu.SMEM)


def unit_rows(starts_ref, number):
    return pl.ds(pl.multiple_of(starts_ref[number], 16), UNIT)


def hidden_kernel(starts_ref, *refs):
    out_ref, mark_ref, wide_ref = refs[-3:]
    mark_ref[...] = jnp.zeros_like(mark_ref)
    chunk = 112
    for clip in range(2):
        tokens_ref, mods_ref = refs[2 * clip : 2 * clip + 2]
        features, count = tokens_ref.shape
        total = jnp.zeros((1, count), F32)
        for start in range(0, features, chunk):
            values = tokens_ref[start : start + chunk, :].astype(F32)
            total = total + jnp.sum(values * values, axis=0, keepdims=True)
        inverse = lax.rsqrt(total * (1.0 / features) + 1e-06)
        for start in range(0, features, chunk):
            rows = slice(start, start + chunk)
            values = tokens_ref[rows, :].astype(F32) * inverse
            wide_ref[rows, :] = values * (1.0 + mods_ref[rows, 1:2]) + mods_ref[rows, 0:1]
        for number in range(16):
            low, high = number * ROWS, (16 + number) * ROWS
            parts = [
                wide_ref[low : low + ROWS, :],
                wide_ref[high : high + ROWS, :],
                jnp.zeros((UNIT - 2 * ROWS, count), F32),
            ]
            tokens = slice(clip * count, (clip + 1) * count)
            out_ref[unit_rows(starts_ref, number), tokens] = jnp.concatenate(parts).astype(BF16)


def make_hidden(starts, *arrays):
    features, count = arrays[0].shape
    return pl.pallas_call(
        hidden_kernel,
        out_shape=(jax.ShapeDtypeStruct((ALL, 2 * count), BF16), MARK),
        in_specs=[SCALARS] + [WHOLE] * 4,
        out_specs=(WHOLE,) * 2,
        scratch_shapes=[pltpu.VMEM((features, count), F32)],
        compiler_params=params(24),
        cost_estimate=NO_COST,
        name="hidden",
    )(starts, *arrays)


def chunks(width):
    size = 384 if width % 384 == 0 else 256
    return [slice(start, min(start + size, width)) for start in range(0, width, size)]


def halves(count):
    return [slice(0, count // 2), slice(count // 2, count)]


FIRST, LAST = ((0,), (0,)), ((1,), (1,))


def near_kernel(numbers, _, hidden_ref, *refs):
    out_ref, mark_ref = refs[-2:]
    mark_ref[...] = jnp.zeros_like(mark_ref)
    for rows in chunks(out_ref.shape[0]):
        for tokens in halves(out_ref.shape[1]):
            total = refs[len(numbers)][rows, tokens] if len(refs) > len(numbers) + 2 else 0.0
            for number, piece_ref in zip(numbers, refs, strict=False):
                depth = piece_ref.shape[0]
                part = hidden_ref[number * depth : (number + 1) * depth, tokens]
                total = total + dot(piece_ref[:, rows], part, FIRST)
            out_ref[rows, tokens] = total


def project_near(mark, hidden, pieces, numbers, before=()):
    width, count = pieces[0].shape[1], hidden.shape[1]
    return pl.pallas_call(
        functools.partial(near_kernel, numbers),
        out_shape=(jax.ShapeDtypeStruct((width, count), F32), MARK),
        in_specs=[WHOLE] * (2 + len(pieces) + len(before)),
        out_specs=(WHOLE,) * 2,
        compiler_params=params(24),
        cost_estimate=NO_COST,
        name="project_near",
    )(mark, hidden, *pieces, *before)


def far_kernel(_, hidden_ref, near_ref, first_ref, second_ref, out_ref, state_ref):
    half = GROUP // 2
    width, count = out_ref.shape
    for rows in chunks(width):
        for tokens in halves(count):
            total = near_ref[rows, tokens]
            total += dot(first_ref[:, rows], hidden_ref[NEAR : NEAR + half, tokens], FIRST)
            total += dot(second_ref[:, rows], hidden_ref[NEAR + half :, tokens], FIRST)
            out_ref[rows, tokens] = total.astype(BF16)
    state_ref[2 * HDIM :, :] = jnp.zeros((PACK - 2 * HDIM, HALF), F32)
    for start, size in groups():
        columns = slice(start, start + size)
        for clip, tokens in enumerate(halves(count)):
            keys, _ = feature(out_ref[columns, tokens].astype(F32))
            values = out_ref[HALF + start : HALF + start + size, tokens]
            product = dot_left(keys, values, LAST)
            state_ref[clip * HDIM : (clip + 1) * HDIM, columns] = diagonal(product)
            state_ref[2 * HDIM + clip : 2 * HDIM + clip + 1, columns] = token_sum(keys)


def project_far(mark, hidden, near, first, second):
    width, count = near.shape
    shapes = (
        jax.ShapeDtypeStruct((width, count), BF16),
        jax.ShapeDtypeStruct((PACK, HALF), F32),
    )
    return pl.pallas_call(
        far_kernel,
        out_shape=shapes,
        in_specs=[WHOLE] * 5,
        out_specs=(WHOLE,) * 2,
        compiler_params=params(24),
        cost_estimate=NO_COST,
        name="project_far",
    )(mark, hidden, near, first, second)


def query_kernel(hidden_ref, *refs):
    *refs, out_ref, mark_ref = refs
    mark_ref[...] = jnp.zeros_like(mark_ref)
    for rows in chunks(out_ref.shape[0]):
        for tokens in halves(out_ref.shape[1]):
            total, start = 0.0, 0
            for piece_ref in refs:
                depth = piece_ref.shape[0]
                part = hidden_ref[start : start + depth, tokens]
                total = total + dot(piece_ref[:, rows], part, FIRST)
                start += depth
            out_ref[rows, tokens] = total.astype(BF16)


def project_query(hidden, pieces):
    return pl.pallas_call(
        query_kernel,
        out_shape=(jax.ShapeDtypeStruct((pieces[0].shape[1], hidden.shape[1]), BF16), MARK),
        in_specs=[WHOLE] * (1 + len(pieces)),
        out_specs=(WHOLE,) * 2,
        compiler_params=params(16),
        cost_estimate=NO_COST,
        name="project_query",
    )(hidden, *pieces)


def once(start, width, keep):
    row = lax.broadcasted_iota(jnp.int32, (width, 1), 0) + start
    return jnp.where(row < HDIM, keep, 1.0)


def middle_kernel(
    _, keep_ref, query_ref, own_ref, other_ref, state_ref, *outs
):
    attention_ref, grad_query_ref, state_grad_ref = outs
    count = query_ref.shape[1] // 2
    state_grad_ref[2 * HDIM :, :] = jnp.zeros((PACK - 2 * HDIM, HALF), F32)
    keep = keep_ref[0]
    for start, width in groups():
        rows = slice(start, start + width)
        ones = same_head(width).astype(BF16)
        for clip in range(2):
            tokens = slice(clip * count, (clip + 1) * count)
            mine = slice(clip * HDIM, (clip + 1) * HDIM)
            sums = slice(2 * HDIM + clip, 2 * HDIM + clip + 1)
            state = block_diagonal(state_ref[mine, rows])
            total = state_ref[sums, rows]
            total_column = column(total)
            query, slope = feature(query_ref[rows, tokens].astype(F32))
            grad = (own_ref, other_ref)[clip][rows, :].astype(F32)
            numer = dot_wide(state, query, ((0,), (0,)))
            inverse = 1.0 / (dot_right(ones, query * total_column) + 1.0)
            quotient = numer * inverse
            attention_ref[rows, tokens] = quotient.astype(BF16)
            grad_numer = grad * inverse
            grad_denom = -dot_right(ones, grad * quotient) * inverse
            product = dot(query.astype(BF16), grad_numer.astype(BF16), LAST)
            state_grad_ref[mine, rows] = diagonal(product)
            state_grad_ref[sums, rows] = token_sum(query * grad_denom)
            back = dot_wide(state, grad_numer) + grad_denom * total_column
            back = slope * back * once(start, width, keep)
            grad_query_ref[rows, tokens] = back.astype(BF16)


def make_middle(mark, keep, query, grads, state):
    count = query.shape[1]
    return pl.pallas_call(
        middle_kernel,
        out_shape=(
            jax.ShapeDtypeStruct((HALF, count), BF16),
            jax.ShapeDtypeStruct((HALF, count), BF16),
            jax.ShapeDtypeStruct((PACK, HALF), F32),
        ),
        in_specs=[WHOLE, SCALARS] + [WHOLE] * 4,
        out_specs=(WHOLE,) * 3,
        compiler_params=params(24),
        cost_estimate=NO_COST,
        name="attention",
    )(mark, keep, query, *grads, state)


def pair_grad_kernel(_, keep_ref, pair_ref, state_grad_ref, out_ref):
    count = pair_ref.shape[1] // 2
    keep = keep_ref[0]
    for start, width in groups():
        rows = slice(start, start + width)
        value_rows = slice(HALF + start, HALF + start + width)
        factor = once(start, width, keep)
        for clip in range(2):
            tokens = slice(clip * count, (clip + 1) * count)
            sums = slice(2 * HDIM + clip, 2 * HDIM + clip + 1)
            state_grad = block_diagonal(state_grad_ref[clip * HDIM : (clip + 1) * HDIM, rows])
            total_grad = column(state_grad_ref[sums, rows])
            keys, slope = feature(pair_ref[rows, tokens].astype(F32))
            state_grad = state_grad.astype(BF16)
            grad_keys = dot(state_grad, pair_ref[value_rows, tokens]) + total_grad
            grad_values = dot(state_grad, keys.astype(BF16), FIRST)
            out_ref[rows, tokens] = (slope * grad_keys * factor).astype(BF16)
            out_ref[value_rows, tokens] = (grad_values * factor).astype(BF16)


def make_pair_grad(mark, keep, pair, state_grad):
    return pl.pallas_call(
        pair_grad_kernel,
        out_shape=jax.ShapeDtypeStruct(pair.shape, BF16),
        in_specs=[WHOLE, SCALARS] + [WHOLE] * 2,
        out_specs=WHOLE,
        compiler_params=params(24),
        cost_estimate=NO_COST,
        name="pair_grad",
    )(mark, keep, pair, state_grad)


def terms_kernel(outputs, _, grad_ref, hidden_ref, *outs):
    *outs, mark_ref = outs
    mark_ref[...] = jnp.zeros_like(mark_ref)
    size = GROUP // 2
    for blocks, out_ref in zip(outputs, outs, strict=True):
        for place, number in enumerate(blocks):
            part = dot(hidden_ref[number * size : (number + 1) * size, :], grad_ref[...], LAST)
            out_ref[place * size : (place + 1) * size, :] = part.astype(BF16)


def weight_terms(gate, hidden, grad, *outputs):
    shapes = [(len(blocks) * GROUP // 2, grad.shape[0]) for blocks in outputs]
    return pl.pallas_call(
        functools.partial(terms_kernel, outputs),
        out_shape=[*(jax.ShapeDtypeStruct(shape, BF16) for shape in shapes), MARK],
        in_specs=[SCALARS] + [WHOLE] * 2,
        out_specs=[WHOLE] * (len(outputs) + 1),
        compiler_params=params(20),
        cost_estimate=NO_COST,
        name="weight_terms",
    )(gate, grad, hidden)


def parts_of(pieces, size):
    return [(piece, start) for piece in pieces for start in range(0, piece.shape[0], size)]


def back_to_plain(starts_ref, query_ref, pair_ref, tokens, pieces, wide_ref, plain_ref):
    size = GROUP // 2
    for base, (query_rows, start), (pair_rows, pair_start) in zip(
        range(0, ALL, size),
        parts_of([piece for piece in pieces if piece.shape[1] == HALF], size),
        parts_of([piece for piece in pieces if piece.shape[1] != HALF], size),
        strict=True,
    ):
        part = dot(query_rows[start : start + size, :], query_ref[:, tokens])
        part = part + dot(pair_rows[pair_start : pair_start + size, :], pair_ref[:, tokens])
        wide_ref[base : base + size, :] = part
    for number in range(16):
        low, high = number * ROWS, (16 + number) * ROWS
        unit = wide_ref[unit_rows(starts_ref, number), :]
        plain_ref[low : low + ROWS, :] = unit[:ROWS]
        plain_ref[high : high + ROWS, :] = unit[ROWS : 2 * ROWS]


def row_chunks(size):
    return [slice(start, min(start + size, 32 * ROWS)) for start in range(0, 32 * ROWS, size)]


def back_kernel(clip, starts_ref, query_ref, pair_ref, *refs):
    out_ref, mark_ref, wide_ref, plain_ref = refs[-4:]
    mark_ref[...] = jnp.zeros_like(mark_ref)
    tokens = halves(query_ref.shape[1])[clip]
    back_to_plain(starts_ref, query_ref, pair_ref, tokens, refs[:-4], wide_ref, plain_ref)
    for rows in row_chunks(112):
        out_ref[rows, :] = plain_ref[rows, :].astype(BF16)


def back_project(starts, grad_query, grad_pair, pieces, clip):
    count, features = grad_query.shape[1] // 2, 32 * ROWS
    return pl.pallas_call(
        functools.partial(back_kernel, clip),
        out_shape=(jax.ShapeDtypeStruct((features, count), BF16), MARK),
        in_specs=[SCALARS] + [WHOLE] * (2 + len(pieces)),
        out_specs=(WHOLE,) * 2,
        scratch_shapes=[pltpu.VMEM((ALL, count), F32), pltpu.VMEM((features, count), F32)],
        compiler_params=params(34),
        cost_estimate=NO_COST,
        name="back_project",
    )(starts, grad_query, grad_pair, *pieces)


def tokens_kernel(*refs):
    mine_ref, received_ref, tokens_ref, mods_ref, out_ref, sums_ref, wide_ref, plain_ref = refs[3:]
    features, count = tokens_ref.shape
    total = jnp.zeros((1, count), F32)
    for rows in row_chunks(112):
        values = tokens_ref[rows, :].astype(F32)
        total = total + jnp.sum(values * values, axis=0, keepdims=True)
    inverse = lax.rsqrt(total * (1.0 / features) + 1e-06)
    mean = jnp.zeros((1, count), F32)
    for rows in row_chunks(112):
        normed = tokens_ref[rows, :].astype(F32) * inverse
        grad = mine_ref[rows, :].astype(F32) + received_ref[rows, :].astype(F32)
        product = grad * normed
        plain_ref[rows, :] = grad
        wide_ref[rows, :] = product
        product = product * (1.0 + mods_ref[rows, 1:2])
        mean = mean + jnp.sum(product, axis=0, keepdims=True)
    for rows in row_chunks(640):
        sums_ref[0:1, rows] = token_sum(plain_ref[rows, :])
        sums_ref[1:2, rows] = token_sum(wide_ref[rows, :])
    mean = mean * (1.0 / features)
    for rows in row_chunks(112):
        normed = tokens_ref[rows, :].astype(F32) * inverse
        grad = plain_ref[rows, :] * (1.0 + mods_ref[rows, 1:2])
        out_ref[rows, :] = (inverse * (grad - normed * mean)).astype(BF16)


def make_tokens(marks, mine, received, tokens, mods):
    features, count = tokens.shape
    return pl.pallas_call(
        tokens_kernel,
        out_shape=(
            jax.ShapeDtypeStruct((features, count), BF16),
            jax.ShapeDtypeStruct((2, features), F32),
        ),
        in_specs=[WHOLE] * 7,
        out_specs=(WHOLE,) * 2,
        scratch_shapes=[pltpu.VMEM((features, count), F32), pltpu.VMEM((features, count), F32)],
        compiler_params=params(24),
        cost_estimate=NO_COST,
        name="grad_tokens",
    )(*marks, mine, received, tokens, mods)


def unit_starts(x, y, core):
    starts = []
    for at_y in range(4):
        for at_x in range(4):
            step_x, step_y = lax.rem(at_x - x + 4, 4), lax.rem(at_y - y + 4, 4)
            outer, inner = pick(core, step_x, step_y), pick(core, step_y, step_x)
            outer = jnp.where(outer == 2, 3, jnp.where(outer == 3, 2, outer))
            starts.append((outer * 4 + inner) * UNIT)
    return jnp.stack(starts).astype(jnp.int32)


def body(tokens, modulation, weight, cotangent):
    seq, dp = lax.axis_index("seq"), lax.axis_index("dp")
    x, y, z_lo = lax.rem(seq, 4), lax.rem(seq // 4, 4), seq // 16
    core = lax.rem(dp, 2)
    count, features = tokens.shape[1:]
    clip_length = count * lax.axis_size("seq")
    all_length = clip_length * lax.axis_size("dp")
    keep = jnp.where(core == 0, 1.0, 0.0).astype(F32).reshape(1)

    starts = unit_starts(x, y, core)
    half = GROUP // 2
    unit, (tokens, cotangent, modulation) = gather_units(
        weight, z_lo, core, (tokens, cotangent, modulation)
    )
    tokens_own = tokens[0].T
    tokens_other = send(tokens_own, "core")
    mods_own = modulation[0].T
    mods_other = send(modulation[0], "core").T
    grad_out = cotangent[0].T
    grads = head_half(grad_out, core, 0), send(head_half(grad_out, core, 0, other=True), "core")
    unit, tokens_other, mods_other = together(unit, tokens_other, mods_other)
    first, second = unit[: UNIT // 2], unit[UNIT // 2 :]
    ahead_first, behind_second = send(first, "middle", -1), send(second, "middle", 1)
    ahead_second, behind_first = send(second, "middle", -1), send(first, "middle", 1)
    hidden, mark = make_hidden(starts, tokens_own, mods_own, tokens_other, mods_other)
    ahead_first, behind_second, ahead_second, behind_first, mark = together(
        ahead_first, behind_second, ahead_second, behind_first, mark
    )
    far_first = send(ahead_first, "middle", -1)
    far_second = send(behind_second, "middle", 1)
    group = jnp.concatenate(
        [unit, ahead_first, ahead_second, far_first, far_second, behind_first, behind_second]
    )
    pair_group, query_group = group[:, : 2 * HALF], group[:, 2 * HALF :]
    pair_first, pair_second = pair_group[:half], pair_group[half:]

    ahead_first = send(pair_first, "last", -1)
    behind_second = send(pair_second, "last", 1)
    ahead_second = send(pair_second, "last", -1)
    behind_first = send(pair_first, "last", 1)
    pair, mark = project_near(mark, hidden, (pair_first, pair_second), (0, 1))
    pair_near = (ahead_first, ahead_second, behind_first, behind_second)
    *pair_near, mark, query_group = together(*pair_near, mark, query_group)
    pair_far_first = send(pair_near[0], "last", -1)
    pair_far_second = send(pair_near[3], "last", 1)
    pair, mark = project_near(mark, hidden, pair_near, (2, 3, 4, 5), (pair,))
    query_ahead = send(query_group, "last", -1)
    query_behind = send(query_group, "last", 1)
    query_first, query_second, mark = together(query_ahead[:half], query_behind[half:], mark)
    query_far_first = send(query_first, "last", -1)
    query_far_second = send(query_second, "last", 1)
    pair, state = project_far(mark, hidden, pair, pair_far_first, pair_far_second)
    part = send(state, "z_lo")
    part, far_first, far_second = together(part, query_far_first, query_far_second)
    state = state + part
    far, ahead, behind = exchange(state, "last")
    query_pieces = (query_group, query_ahead, query_behind, far_first, far_second)
    query, mark = project_query(hidden, query_pieces)
    far, ahead, behind, mark = together(far, ahead, behind, mark)
    state = ring_sum(state, (far, ahead, behind))
    parts = exchange(state, "middle")
    state = ring_sum(state, parts)

    attention, grad_query, state_grad = make_middle(mark, keep, query, grads, state)
    parts = exchange(state_grad.astype(BF16), "last")
    far_first, far_second, _ = weight_terms(starts, hidden, grad_query, (6,), (7,))
    *parts, far_first, far_second, gate = together(*parts, far_first, far_second, starts)
    state_grad = ring_sum(state_grad, parts)
    parts = exchange(state_grad.astype(BF16), "middle")
    far_first, far_second = send(far_first, "last", 1), send(far_second, "last", -1)
    ahead, behind, own_query, mark = weight_terms(gate, hidden, grad_query, (2, 3), (4, 5), (0, 1))
    *parts, far_first, far_second, attention, mark = together(
        *parts, far_first, far_second, attention, mark
    )
    state_grad = ring_sum(state_grad, parts)
    part = send(state_grad.astype(BF16), "z_lo")
    other_attention = send(attention[:, count:], "core")
    ahead = jnp.concatenate([add(ahead[:half], far_first), ahead[half:]])
    behind = jnp.concatenate([behind[:half], add(behind[half:], far_second)])
    state_grad = state_grad + part.astype(F32)
    query_from_behind, query_from_ahead = send(ahead, "last", 1), send(behind, "last", -1)
    grad_pair = make_pair_grad(mark, keep, pair, state_grad)
    soon_ahead, soon_behind, _ = weight_terms(starts, hidden, grad_pair, (6, 3), (7, 4))
    soon_ahead, soon_behind, gate, other_attention, query_from_behind, query_from_ahead = together(
        soon_ahead, soon_behind, starts, other_attention, query_from_behind, query_from_ahead
    )
    from_behind, from_ahead = send(soon_ahead, "last", 1), send(soon_behind, "last", -1)
    pieces = (*query_pieces, pair_first, pair_second, *pair_near, pair_far_first, pair_far_second)
    received, mark_other = back_project(gate, grad_query, grad_pair, pieces, 1)
    grad_hidden, mark_own = back_project(gate, grad_query, grad_pair, pieces, 0)
    later_ahead, later_behind, own_first, own_second, mark = weight_terms(
        gate, hidden, grad_pair, (2,), (5,), (0,), (1,)
    )
    attention = head_join(attention[:, :count], other_attention, core, 0)
    from_behind, from_ahead, received, attention, *marks = together(
        from_behind, from_ahead, received, attention, mark, mark_other, mark_own
    )
    received = send(received, "core")
    plain_ahead, plain_behind = from_behind[half:], from_ahead[half:]
    from_behind = send(add(later_ahead, from_behind[:half]), "last", 1)
    from_ahead = send(add(later_behind, from_ahead[:half]), "last", -1)
    grad_tokens, mod_grad = make_tokens(marks, grad_hidden, received, tokens_own, mods_own)
    from_behind, from_ahead, mod_grad = together(from_behind, from_ahead, mod_grad)
    query_part = own_query.astype(F32) + (
        query_from_behind.astype(F32) + query_from_ahead.astype(F32)
    )
    pair_part = jnp.concatenate(
        [
            own_first.astype(F32) + from_behind.astype(F32) + plain_behind.astype(F32),
            own_second.astype(F32) + plain_ahead.astype(F32) + from_ahead.astype(F32),
        ]
    )
    group = jnp.concatenate([pair_part, query_part], axis=1).astype(BF16)
    own, ahead, far, behind = jnp.split(group, 4)
    far_first = send(far[: UNIT // 2], "middle", 1)
    far_second = send(far[UNIT // 2 :], "middle", -1)
    parts = exchange(mod_grad, "last")
    *parts, far_first, far_second = together(*parts, far_first, far_second)
    mod_grad = ring_sum(mod_grad, parts)
    ahead = jnp.concatenate([add(ahead[: UNIT // 2], far_first), ahead[UNIT // 2 :]])
    behind = jnp.concatenate([behind[: UNIT // 2], add(behind[UNIT // 2 :], far_second)])
    from_behind = send(ahead, "middle", 1)
    from_ahead = send(behind, "middle", -1)
    parts = exchange(mod_grad, "middle")
    *parts, from_behind, from_ahead = together(*parts, from_behind, from_ahead)
    mod_grad = ring_sum(mod_grad, parts)
    mod_grad = (mod_grad + send(mod_grad, "z_lo")) * (1.0 / math.sqrt(clip_length))
    unit = (own.astype(F32) + from_behind.astype(F32) + from_ahead.astype(F32)).astype(BF16)
    weight_grad = finish_weight(unit, z_lo, dp, core)
    weight_grad = weight_grad * (1.0 / math.sqrt(all_length))
    return (attention.T[None], grad_tokens.T[None], weight_grad, mod_grad[None])


def solution(mesh):
    return jax.shard_map(
        body,
        mesh=mesh,
        in_specs=(P("dp", "seq", None), P("dp", None, None), P("seq", "dp"), P("dp", "seq", None)),
        out_specs=(P("dp", "seq", None), P("dp", "seq", None), P("seq", "dp"), P("dp", None, None)),
        check_vma=False,
    )
```

```python
import functools
import math

import jax
import jax.numpy as jnp
from jax import lax
from jax.experimental import pallas as pl
from jax.experimental.pallas import tpu as pltpu
from jax.sharding import PartitionSpec as P

HDIM = 32
AXES = ("seq", "dp")
ROWS = 70
UNIT = 144
COLS = 840
HALF = 576
GROUP = 4 * UNIT
ALL = 16 * UNIT
LANES = 128
PACK = 72
NEAR = 3 * GROUP
F32, BF16 = jnp.float32, jnp.bfloat16
WHOLE = pl.BlockSpec(memory_space=pltpu.VMEM)
ANYWHERE = pl.BlockSpec(memory_space=pl.ANY)


def place(index):
    seq, dp = divmod(index, 4)
    z_lo, rest = divmod(seq, 16)
    y, x = divmod(rest, 4)
    z_hi, core = divmod(dp, 2)
    return x, y, z_hi * 2 + z_lo, core


def index_of(x, y, z, core):
    x, y, z = x % 4, y % 4, z % 4
    return ((z % 2) * 16 + y * 4 + x) * 4 + (z // 2) * 2 + core


def route(kind, offset):
    pairs = []
    for index in range(128):
        x, y, z, core = place(index)
        if kind == "z":
            target = index_of(x, y, z + offset, core)
        elif kind == "z_lo":
            target = index_of(x, y, z ^ 1, core)
        elif kind == "z_hi":
            target = index_of(x, y, z ^ 2, core)
        elif kind == "core":
            target = index_of(x, y, z, 1 - core)
        elif (kind == "last") == (core == 0):
            target = index_of(x + offset, y, z, core)
        else:
            target = index_of(x, y + offset, z, core)
        pairs.append((index, target))
    return pairs


def send(value, kind, offset=0):
    return lax.ppermute(value, AXES, route(kind, offset))


def together(*values):
    return lax.optimization_barrier(values)


def add(left, right):
    return (left.astype(F32) + right.astype(F32)).astype(BF16)


def exchange(value, kind):
    return send(value, kind, 2), send(value, kind, -1), send(value, kind, 1)


def ring_sum(value, parts):
    far, ahead, behind = (part.astype(F32) for part in parts)
    return (value + far) + (ahead + behind)


def pick(core, on_zero, on_one):
    return jnp.where(core == 0, on_zero, on_one)


def head_half(array, core, axis, other=False):
    size = array.shape[axis]
    low = lax.slice_in_dim(array, 0, HALF, axis=axis)
    high = lax.slice_in_dim(array, size - HALF, size, axis=axis)
    return pick(core, high, low) if other else pick(core, low, high)


def head_join(mine, other, core, axis):
    second = lax.slice_in_dim(pick(core, other, mine), HDIM, HALF, axis=axis)
    return jnp.concatenate([pick(core, mine, other), second], axis=axis)


def gather_units(weight, z_lo, core, extra):
    blocks, extra = together(lax.all_gather(weight, "dp"), extra)
    columns = jnp.concatenate([blocks[i] for i in range(4)], axis=1)
    third = 4 * COLS // 3
    query, keys, values = (
        head_half(columns[:, i * third : (i + 1) * third], core, 1) for i in range(3)
    )
    mine = jnp.concatenate([keys, values, query], axis=1)
    other = send(mine, "z_lo")
    unit = jnp.concatenate([pick(z_lo, mine, other), pick(z_lo, other, mine)])
    return jnp.pad(unit, ((0, UNIT - 2 * ROWS), (0, 0))), extra


def finish_weight(unit, z_lo, dp, core):
    first, second = unit[:ROWS], unit[ROWS : 2 * ROWS]
    mine = add(pick(z_lo, first, second), send(pick(z_lo, second, first), "z_lo"))
    zero = jnp.zeros((ROWS, HALF), BF16)
    columns = jnp.concatenate(
        [head_join(mine[:, i * HALF : (i + 1) * HALF], zero, core, 1) for i in (2, 0, 1)], axis=1
    )
    blocks = jnp.stack([columns[:, i * COLS : (i + 1) * COLS] for i in range(4)])

    def block(flip):
        return lax.dynamic_index_in_dim(blocks, dp ^ flip, 0, keepdims=False)

    by_core = send(jnp.stack([block(1), block(3)]), "core")
    mine = block(0).astype(F32) + by_core[0].astype(F32)
    return mine + send(add(block(2), by_core[1]), "z_hi").astype(F32)


def params(mebibytes):
    return pltpu.CompilerParams(vmem_limit_bytes=mebibytes * 1024 * 1024)


NO_COST = pl.CostEstimate(flops=0, bytes_accessed=0, transcendentals=0)


def split(value):
    high = value.astype(BF16)
    return high, (value - high.astype(F32)).astype(BF16)


def dot(left, right, dims=((1,), (0,))):
    return lax.dot_general(left, right, (dims, ((), ())), preferred_element_type=F32)


def dot_wide(left, right, dims=((1,), (0,))):
    left_high, left_low = split(left)
    right_high, right_low = split(right)
    return dot(left_high, right_high, dims) + (
        dot(left_low, right_high, dims) + dot(left_high, right_low, dims)
    )


def dot_left(left, right, dims=((1,), (0,))):
    high, low = split(left)
    return dot(high, right, dims) + dot(low, right, dims)


def dot_right(left, right, dims=((1,), (0,))):
    high, low = split(right)
    return dot(left, high, dims) + dot(left, low, dims)


def feature(values):
    lower = jnp.exp(jnp.minimum(values, 0.0))
    return jnp.where(values > 0, values + 1.0, lower), jnp.where(values > 0, 1.0, lower)


def same_head(size):
    row = lax.broadcasted_iota(jnp.int32, (size, size), 0) // HDIM
    return row == lax.broadcasted_iota(jnp.int32, (size, size), 1) // HDIM


def diagonal(product):
    width = product.shape[1]
    kept = jnp.where(same_head(width), product, 0.0)
    total = kept[:HDIM]
    for start in range(HDIM, width, HDIM):
        total = total + kept[start : start + HDIM]
    return total


def block_diagonal(blocks):
    width = blocks.shape[1]
    tiled = jnp.concatenate([blocks] * (width // HDIM), axis=0)
    return jnp.where(same_head(width), tiled, 0.0)


def column(row):
    width = row.shape[1]
    index = lax.broadcasted_iota(jnp.int32, (width, width), 0)
    same = index == lax.broadcasted_iota(jnp.int32, (width, width), 1)
    return jnp.sum(jnp.where(same, row, 0.0), axis=1, keepdims=True)


def head_sum(array):
    return jnp.sum(array.reshape(-1, HDIM, array.shape[1]), axis=1, keepdims=True)


def by_head(array, factors):
    return (array.reshape(-1, HDIM, array.shape[1]) * factors).reshape(array.shape)


def token_sum(array):
    parts = [array[:, start : start + LANES] for start in range(0, array.shape[1], LANES)]
    ones = jnp.ones((16, LANES), BF16)
    return dot_right(ones, sum(parts[1:], parts[0]), ((1,), (1,)))[:1]


def groups():
    return [(start, min(LANES, HALF - start)) for start in range(0, HALF, LANES)]


MARK = jax.ShapeDtypeStruct((8, LANES), F32)
SCALARS = pl.BlockSpec(memory_space=pltpu.SMEM)


def unit_rows(starts_ref, number):
    return pl.ds(pl.multiple_of(starts_ref[number], 16), UNIT)


def hidden_kernel(starts_ref, *refs):
    out_ref, mark_ref, wide_ref = refs[-3:]
    mark_ref[...] = jnp.zeros_like(mark_ref)
    chunk = 112
    for clip in range(2):
        tokens_ref, mods_ref = refs[2 * clip : 2 * clip + 2]
        features, count = tokens_ref.shape
        total = jnp.zeros((1, count), F32)
        for start in range(0, features, chunk):
            values = tokens_ref[start : start + chunk, :].astype(F32)
            total = total + jnp.sum(values * values, axis=0, keepdims=True)
        inverse = lax.rsqrt(total * (1.0 / features) + 1e-06)
        for start in range(0, features, chunk):
            rows = slice(start, start + chunk)
            values = tokens_ref[rows, :].astype(F32) * inverse
            wide_ref[rows, :] = values * (1.0 + mods_ref[rows, 1:2]) + mods_ref[rows, 0:1]
        for number in range(16):
            low, high = number * ROWS, (16 + number) * ROWS
            parts = [
                wide_ref[low : low + ROWS, :],
                wide_ref[high : high + ROWS, :],
                jnp.zeros((UNIT - 2 * ROWS, count), F32),
            ]
            tokens = slice(clip * count, (clip + 1) * count)
            out_ref[unit_rows(starts_ref, number), tokens] = jnp.concatenate(parts).astype(BF16)


def make_hidden(starts, *arrays):
    features, count = arrays[0].shape
    return pl.pallas_call(
        hidden_kernel,
        out_shape=(jax.ShapeDtypeStruct((ALL, 2 * count), BF16), MARK),
        in_specs=[SCALARS] + [WHOLE] * 4,
        out_specs=(WHOLE,) * 2,
        scratch_shapes=[pltpu.VMEM((features, count), F32)],
        compiler_params=params(24),
        cost_estimate=NO_COST,
        name="hidden",
    )(starts, *arrays)


def chunks(width):
    size = 384 if width % 384 == 0 else 256
    return [slice(start, min(start + size, width)) for start in range(0, width, size)]


def halves(count):
    return [slice(0, count // 2), slice(count // 2, count)]


FIRST, LAST = ((0,), (0,)), ((1,), (1,))


def near_kernel(numbers, _, hidden_ref, *refs):
    out_ref, mark_ref = refs[-2:]
    mark_ref[...] = jnp.zeros_like(mark_ref)
    for rows in chunks(out_ref.shape[0]):
        for tokens in halves(out_ref.shape[1]):
            total = refs[len(numbers)][rows, tokens] if len(refs) > len(numbers) + 2 else 0.0
            for number, piece_ref in zip(numbers, refs, strict=False):
                depth = piece_ref.shape[0]
                part = hidden_ref[number * depth : (number + 1) * depth, tokens]
                total = total + dot(piece_ref[:, rows], part, FIRST)
            out_ref[rows, tokens] = total


def project_near(mark, hidden, pieces, numbers, before=()):
    width, count = pieces[0].shape[1], hidden.shape[1]
    return pl.pallas_call(
        functools.partial(near_kernel, numbers),
        out_shape=(jax.ShapeDtypeStruct((width, count), F32), MARK),
        in_specs=[WHOLE] * (2 + len(pieces) + len(before)),
        out_specs=(WHOLE,) * 2,
        compiler_params=params(24),
        cost_estimate=NO_COST,
        name="project_near",
    )(mark, hidden, *pieces, *before)


def far_kernel(_, hidden_ref, near_ref, first_ref, second_ref, out_ref, state_ref):
    half = GROUP // 2
    width, count = out_ref.shape
    for rows in chunks(width):
        for tokens in halves(count):
            total = near_ref[rows, tokens]
            total += dot(first_ref[:, rows], hidden_ref[NEAR : NEAR + half, tokens], FIRST)
            total += dot(second_ref[:, rows], hidden_ref[NEAR + half :, tokens], FIRST)
            out_ref[rows, tokens] = total.astype(BF16)
    state_ref[2 * HDIM :, :] = jnp.zeros((PACK - 2 * HDIM, HALF), F32)
    for start, size in groups():
        columns = slice(start, start + size)
        for clip, tokens in enumerate(halves(count)):
            keys, _ = feature(out_ref[columns, tokens].astype(F32))
            values = out_ref[HALF + start : HALF + start + size, tokens]
            product = dot_left(keys, values, LAST)
            state_ref[clip * HDIM : (clip + 1) * HDIM, columns] = diagonal(product)
            state_ref[2 * HDIM + clip : 2 * HDIM + clip + 1, columns] = token_sum(keys)


def project_far(mark, hidden, near, first, second):
    width, count = near.shape
    shapes = (
        jax.ShapeDtypeStruct((width, count), BF16),
        jax.ShapeDtypeStruct((PACK, HALF), F32),
    )
    return pl.pallas_call(
        far_kernel,
        out_shape=shapes,
        in_specs=[WHOLE] * 5,
        out_specs=(WHOLE,) * 2,
        compiler_params=params(24),
        cost_estimate=NO_COST,
        name="project_far",
    )(mark, hidden, near, first, second)


def query_kernel(hidden_ref, *refs):
    *refs, out_ref, mark_ref = refs
    mark_ref[...] = jnp.zeros_like(mark_ref)
    for rows in chunks(out_ref.shape[0]):
        for tokens in halves(out_ref.shape[1]):
            total, start = 0.0, 0
            for piece_ref in refs:
                depth = piece_ref.shape[0]
                part = hidden_ref[start : start + depth, tokens]
                total = total + dot(piece_ref[:, rows], part, FIRST)
                start += depth
            out_ref[rows, tokens] = total.astype(BF16)


def project_query(hidden, pieces):
    return pl.pallas_call(
        query_kernel,
        out_shape=(jax.ShapeDtypeStruct((pieces[0].shape[1], hidden.shape[1]), BF16), MARK),
        in_specs=[WHOLE] * (1 + len(pieces)),
        out_specs=(WHOLE,) * 2,
        compiler_params=params(16),
        cost_estimate=NO_COST,
        name="project_query",
    )(hidden, *pieces)


def once(start, width, keep):
    row = lax.broadcasted_iota(jnp.int32, (width, 1), 0) + start
    return jnp.where(row < HDIM, keep, 1.0)


def middle_kernel(
    _, keep_ref, query_ref, own_ref, other_ref, state_ref, *outs
):
    attention_ref, grad_query_ref, state_grad_ref = outs
    count = query_ref.shape[1] // 2
    state_grad_ref[2 * HDIM :, :] = jnp.zeros((PACK - 2 * HDIM, HALF), F32)
    keep = keep_ref[0]
    for start, width in groups():
        rows = slice(start, start + width)
        for clip in range(2):
            tokens = slice(clip * count, (clip + 1) * count)
            mine = slice(clip * HDIM, (clip + 1) * HDIM)
            sums = slice(2 * HDIM + clip, 2 * HDIM + clip + 1)
            state = block_diagonal(state_ref[mine, rows])
            total = state_ref[sums, rows]
            total_column = column(total)
            query, slope = feature(query_ref[rows, tokens].astype(F32))
            grad = (own_ref, other_ref)[clip][rows, :].astype(F32)
            numer = dot_wide(state, query, ((0,), (0,)))
            inverse = 1.0 / (head_sum(query * total_column) + 1.0)
            quotient = by_head(numer, inverse)
            attention_ref[rows, tokens] = quotient.astype(BF16)
            grad_numer = by_head(grad, inverse)
            grad_denom = -head_sum(grad * quotient) * inverse
            product = dot(query.astype(BF16), grad_numer.astype(BF16), LAST)
            state_grad_ref[mine, rows] = diagonal(product)
            state_grad_ref[sums, rows] = token_sum(by_head(query, grad_denom))
            spread = by_head(jnp.broadcast_to(total_column, query.shape), grad_denom)
            back = dot_wide(state, grad_numer) + spread
            back = slope * back * once(start, width, keep)
            grad_query_ref[rows, tokens] = back.astype(BF16)


def make_middle(mark, keep, query, grads, state):
    count = query.shape[1]
    return pl.pallas_call(
        middle_kernel,
        out_shape=(
            jax.ShapeDtypeStruct((HALF, count), BF16),
            jax.ShapeDtypeStruct((HALF, count), BF16),
            jax.ShapeDtypeStruct((PACK, HALF), F32),
        ),
        in_specs=[WHOLE, SCALARS] + [WHOLE] * 4,
        out_specs=(WHOLE,) * 3,
        compiler_params=params(24),
        cost_estimate=NO_COST,
        name="attention",
    )(mark, keep, query, *grads, state)


def pair_grad_kernel(_, keep_ref, pair_ref, state_grad_ref, out_ref):
    count = pair_ref.shape[1] // 2
    keep = keep_ref[0]
    for start, width in groups():
        rows = slice(start, start + width)
        value_rows = slice(HALF + start, HALF + start + width)
        factor = once(start, width, keep)
        for clip in range(2):
            tokens = slice(clip * count, (clip + 1) * count)
            sums = slice(2 * HDIM + clip, 2 * HDIM + clip + 1)
            state_grad = block_diagonal(state_grad_ref[clip * HDIM : (clip + 1) * HDIM, rows])
            total_grad = column(state_grad_ref[sums, rows])
            keys, slope = feature(pair_ref[rows, tokens].astype(F32))
            state_grad = state_grad.astype(BF16)
            grad_keys = dot(state_grad, pair_ref[value_rows, tokens]) + total_grad
            grad_values = dot(state_grad, keys.astype(BF16), FIRST)
            out_ref[rows, tokens] = (slope * grad_keys * factor).astype(BF16)
            out_ref[value_rows, tokens] = (grad_values * factor).astype(BF16)


def make_pair_grad(mark, keep, pair, state_grad):
    return pl.pallas_call(
        pair_grad_kernel,
        out_shape=jax.ShapeDtypeStruct(pair.shape, BF16),
        in_specs=[WHOLE, SCALARS] + [WHOLE] * 2,
        out_specs=WHOLE,
        compiler_params=params(24),
        cost_estimate=NO_COST,
        name="pair_grad",
    )(mark, keep, pair, state_grad)


def terms_kernel(outputs, _, grad_ref, hidden_ref, *outs):
    *outs, mark_ref = outs
    mark_ref[...] = jnp.zeros_like(mark_ref)
    size = GROUP // 2
    for blocks, out_ref in zip(outputs, outs, strict=True):
        for place, number in enumerate(blocks):
            part = dot(hidden_ref[number * size : (number + 1) * size, :], grad_ref[...], LAST)
            out_ref[place * size : (place + 1) * size, :] = part.astype(BF16)


def weight_terms(gate, hidden, grad, *outputs):
    shapes = [(len(blocks) * GROUP // 2, grad.shape[0]) for blocks in outputs]
    return pl.pallas_call(
        functools.partial(terms_kernel, outputs),
        out_shape=[*(jax.ShapeDtypeStruct(shape, BF16) for shape in shapes), MARK],
        in_specs=[SCALARS] + [WHOLE] * 2,
        out_specs=[WHOLE] * (len(outputs) + 1),
        compiler_params=params(20),
        cost_estimate=NO_COST,
        name="weight_terms",
    )(gate, grad, hidden)


def parts_of(pieces, size):
    return [(piece, start) for piece in pieces for start in range(0, piece.shape[0], size)]


def back_to_plain(starts_ref, query_ref, pair_ref, tokens, pieces, wide_ref, plain_ref):
    size = GROUP // 2
    for base, (query_rows, start), (pair_rows, pair_start) in zip(
        range(0, ALL, size),
        parts_of([piece for piece in pieces if piece.shape[1] == HALF], size),
        parts_of([piece for piece in pieces if piece.shape[1] != HALF], size),
        strict=True,
    ):
        part = dot(query_rows[start : start + size, :], query_ref[:, tokens])
        part = part + dot(pair_rows[pair_start : pair_start + size, :], pair_ref[:, tokens])
        wide_ref[base : base + size, :] = part
    for number in range(16):
        low, high = number * ROWS, (16 + number) * ROWS
        unit = wide_ref[unit_rows(starts_ref, number), :]
        plain_ref[low : low + ROWS, :] = unit[:ROWS]
        plain_ref[high : high + ROWS, :] = unit[ROWS : 2 * ROWS]


def row_chunks(size):
    return [slice(start, min(start + size, 32 * ROWS)) for start in range(0, 32 * ROWS, size)]


def back_kernel(clip, starts_ref, query_ref, pair_ref, *refs):
    out_ref, mark_ref, wide_ref, plain_ref = refs[-4:]
    mark_ref[...] = jnp.zeros_like(mark_ref)
    tokens = halves(query_ref.shape[1])[clip]
    back_to_plain(starts_ref, query_ref, pair_ref, tokens, refs[:-4], wide_ref, plain_ref)
    for rows in row_chunks(112):
        out_ref[rows, :] = plain_ref[rows, :].astype(BF16)


def back_project(starts, grad_query, grad_pair, pieces, clip):
    count, features = grad_query.shape[1] // 2, 32 * ROWS
    return pl.pallas_call(
        functools.partial(back_kernel, clip),
        out_shape=(jax.ShapeDtypeStruct((features, count), BF16), MARK),
        in_specs=[SCALARS] + [WHOLE] * (2 + len(pieces)),
        out_specs=(WHOLE,) * 2,
        scratch_shapes=[pltpu.VMEM((ALL, count), F32), pltpu.VMEM((features, count), F32)],
        compiler_params=params(34),
        cost_estimate=NO_COST,
        name="back_project",
    )(starts, grad_query, grad_pair, *pieces)


def tokens_kernel(*refs):
    mine_ref, received_ref, tokens_ref, mods_ref, out_ref, sums_ref, wide_ref, plain_ref = refs[3:]
    features, count = tokens_ref.shape
    total = jnp.zeros((1, count), F32)
    for rows in row_chunks(112):
        values = tokens_ref[rows, :].astype(F32)
        total = total + jnp.sum(values * values, axis=0, keepdims=True)
    inverse = lax.rsqrt(total * (1.0 / features) + 1e-06)
    mean = jnp.zeros((1, count), F32)
    for rows in row_chunks(112):
        normed = tokens_ref[rows, :].astype(F32) * inverse
        grad = mine_ref[rows, :].astype(F32) + received_ref[rows, :].astype(F32)
        product = grad * normed
        plain_ref[rows, :] = grad
        wide_ref[rows, :] = product
        product = product * (1.0 + mods_ref[rows, 1:2])
        mean = mean + jnp.sum(product, axis=0, keepdims=True)
    for rows in row_chunks(640):
        sums_ref[0:1, rows] = token_sum(plain_ref[rows, :])
        sums_ref[1:2, rows] = token_sum(wide_ref[rows, :])
    mean = mean * (1.0 / features)
    for rows in row_chunks(112):
        normed = tokens_ref[rows, :].astype(F32) * inverse
        grad = plain_ref[rows, :] * (1.0 + mods_ref[rows, 1:2])
        out_ref[rows, :] = (inverse * (grad - normed * mean)).astype(BF16)


def make_tokens(marks, mine, received, tokens, mods):
    features, count = tokens.shape
    return pl.pallas_call(
        tokens_kernel,
        out_shape=(
            jax.ShapeDtypeStruct((features, count), BF16),
            jax.ShapeDtypeStruct((2, features), F32),
        ),
        in_specs=[WHOLE] * 7,
        out_specs=(WHOLE,) * 2,
        scratch_shapes=[pltpu.VMEM((features, count), F32), pltpu.VMEM((features, count), F32)],
        compiler_params=params(24),
        cost_estimate=NO_COST,
        name="grad_tokens",
    )(*marks, mine, received, tokens, mods)


def unit_starts(x, y, core):
    starts = []
    for at_y in range(4):
        for at_x in range(4):
            step_x, step_y = lax.rem(at_x - x + 4, 4), lax.rem(at_y - y + 4, 4)
            outer, inner = pick(core, step_x, step_y), pick(core, step_y, step_x)
            outer = jnp.where(outer == 2, 3, jnp.where(outer == 3, 2, outer))
            starts.append((outer * 4 + inner) * UNIT)
    return jnp.stack(starts).astype(jnp.int32)


def body(tokens, modulation, weight, cotangent):
    seq, dp = lax.axis_index("seq"), lax.axis_index("dp")
    x, y, z_lo = lax.rem(seq, 4), lax.rem(seq // 4, 4), seq // 16
    core = lax.rem(dp, 2)
    count, features = tokens.shape[1:]
    clip_length = count * lax.axis_size("seq")
    all_length = clip_length * lax.axis_size("dp")
    keep = jnp.where(core == 0, 1.0, 0.0).astype(F32).reshape(1)

    starts = unit_starts(x, y, core)
    half = GROUP // 2
    unit, (tokens, cotangent, modulation) = gather_units(
        weight, z_lo, core, (tokens, cotangent, modulation)
    )
    tokens_own = tokens[0].T
    tokens_other = send(tokens_own, "core")
    mods_own = modulation[0].T
    mods_other = send(modulation[0], "core").T
    grad_out = cotangent[0].T
    grads = head_half(grad_out, core, 0), send(head_half(grad_out, core, 0, other=True), "core")
    unit, tokens_other, mods_other = together(unit, tokens_other, mods_other)
    first, second = unit[: UNIT // 2], unit[UNIT // 2 :]
    ahead_first, behind_second = send(first, "middle", -1), send(second, "middle", 1)
    ahead_second, behind_first = send(second, "middle", -1), send(first, "middle", 1)
    hidden, mark = make_hidden(starts, tokens_own, mods_own, tokens_other, mods_other)
    ahead_first, behind_second, ahead_second, behind_first, mark = together(
        ahead_first, behind_second, ahead_second, behind_first, mark
    )
    far_first = send(ahead_first, "middle", -1)
    far_second = send(behind_second, "middle", 1)
    group = jnp.concatenate(
        [unit, ahead_first, ahead_second, far_first, far_second, behind_first, behind_second]
    )
    pair_group, query_group = group[:, : 2 * HALF], group[:, 2 * HALF :]
    pair_first, pair_second = pair_group[:half], pair_group[half:]

    ahead_first = send(pair_first, "last", -1)
    behind_second = send(pair_second, "last", 1)
    ahead_second = send(pair_second, "last", -1)
    behind_first = send(pair_first, "last", 1)
    pair, mark = project_near(mark, hidden, (pair_first, pair_second), (0, 1))
    pair_near = (ahead_first, ahead_second, behind_first, behind_second)
    *pair_near, mark, query_group = together(*pair_near, mark, query_group)
    pair_far_first = send(pair_near[0], "last", -1)
    pair_far_second = send(pair_near[3], "last", 1)
    pair, mark = project_near(mark, hidden, pair_near, (2, 3, 4, 5), (pair,))
    query_ahead = send(query_group, "last", -1)
    query_behind = send(query_group, "last", 1)
    query_first, query_second, mark = together(query_ahead[:half], query_behind[half:], mark)
    query_far_first = send(query_first, "last", -1)
    query_far_second = send(query_second, "last", 1)
    pair, state = project_far(mark, hidden, pair, pair_far_first, pair_far_second)
    part = send(state, "z_lo")
    part, far_first, far_second = together(part, query_far_first, query_far_second)
    state = state + part
    far, ahead, behind = exchange(state, "last")
    query_pieces = (query_group, query_ahead, query_behind, far_first, far_second)
    query, mark = project_query(hidden, query_pieces)
    far, ahead, behind, mark = together(far, ahead, behind, mark)
    state = ring_sum(state, (far, ahead, behind))
    parts = exchange(state, "middle")
    state = ring_sum(state, parts)

    attention, grad_query, state_grad = make_middle(mark, keep, query, grads, state)
    parts = exchange(state_grad.astype(BF16), "last")
    far_first, far_second, _ = weight_terms(starts, hidden, grad_query, (6,), (7,))
    *parts, far_first, far_second, gate = together(*parts, far_first, far_second, starts)
    state_grad = ring_sum(state_grad, parts)
    parts = exchange(state_grad.astype(BF16), "middle")
    far_first, far_second = send(far_first, "last", 1), send(far_second, "last", -1)
    ahead, behind, own_query, mark = weight_terms(gate, hidden, grad_query, (2, 3), (4, 5), (0, 1))
    *parts, far_first, far_second, attention, mark = together(
        *parts, far_first, far_second, attention, mark
    )
    state_grad = ring_sum(state_grad, parts)
    part = send(state_grad.astype(BF16), "z_lo")
    other_attention = send(attention[:, count:], "core")
    ahead = jnp.concatenate([add(ahead[:half], far_first), ahead[half:]])
    behind = jnp.concatenate([behind[:half], add(behind[half:], far_second)])
    state_grad = state_grad + part.astype(F32)
    query_from_behind, query_from_ahead = send(ahead, "last", 1), send(behind, "last", -1)
    grad_pair = make_pair_grad(mark, keep, pair, state_grad)
    soon_ahead, soon_behind, _ = weight_terms(starts, hidden, grad_pair, (6, 3), (7, 4))
    soon_ahead, soon_behind, gate, other_attention, query_from_behind, query_from_ahead = together(
        soon_ahead, soon_behind, starts, other_attention, query_from_behind, query_from_ahead
    )
    from_behind, from_ahead = send(soon_ahead, "last", 1), send(soon_behind, "last", -1)
    pieces = (*query_pieces, pair_first, pair_second, *pair_near, pair_far_first, pair_far_second)
    received, mark_other = back_project(gate, grad_query, grad_pair, pieces, 1)
    grad_hidden, mark_own = back_project(gate, grad_query, grad_pair, pieces, 0)
    later_ahead, later_behind, own_first, own_second, mark = weight_terms(
        gate, hidden, grad_pair, (2,), (5,), (0,), (1,)
    )
    attention = head_join(attention[:, :count], other_attention, core, 0)
    from_behind, from_ahead, received, attention, *marks = together(
        from_behind, from_ahead, received, attention, mark, mark_other, mark_own
    )
    received = send(received, "core")
    plain_ahead, plain_behind = from_behind[half:], from_ahead[half:]
    from_behind = send(add(later_ahead, from_behind[:half]), "last", 1)
    from_ahead = send(add(later_behind, from_ahead[:half]), "last", -1)
    grad_tokens, mod_grad = make_tokens(marks, grad_hidden, received, tokens_own, mods_own)
    from_behind, from_ahead, mod_grad = together(from_behind, from_ahead, mod_grad)
    query_part = own_query.astype(F32) + (
        query_from_behind.astype(F32) + query_from_ahead.astype(F32)
    )
    pair_part = jnp.concatenate(
        [
            own_first.astype(F32) + from_behind.astype(F32) + plain_behind.astype(F32),
            own_second.astype(F32) + plain_ahead.astype(F32) + from_ahead.astype(F32),
        ]
    )
    group = jnp.concatenate([pair_part, query_part], axis=1).astype(BF16)
    own, ahead, far, behind = jnp.split(group, 4)
    far_first = send(far[: UNIT // 2], "middle", 1)
    far_second = send(far[UNIT // 2 :], "middle", -1)
    parts = exchange(mod_grad, "last")
    *parts, far_first, far_second = together(*parts, far_first, far_second)
    mod_grad = ring_sum(mod_grad, parts)
    ahead = jnp.concatenate([add(ahead[: UNIT // 2], far_first), ahead[UNIT // 2 :]])
    behind = jnp.concatenate([behind[: UNIT // 2], add(behind[UNIT // 2 :], far_second)])
    from_behind = send(ahead, "middle", 1)
    from_ahead = send(behind, "middle", -1)
    parts = exchange(mod_grad, "middle")
    *parts, from_behind, from_ahead = together(*parts, from_behind, from_ahead)
    mod_grad = ring_sum(mod_grad, parts)
    mod_grad = (mod_grad + send(mod_grad, "z_lo")) * (1.0 / math.sqrt(clip_length))
    unit = (own.astype(F32) + from_behind.astype(F32) + from_ahead.astype(F32)).astype(BF16)
    weight_grad = finish_weight(unit, z_lo, dp, core)
    weight_grad = weight_grad * (1.0 / math.sqrt(all_length))
    return (attention.T[None], grad_tokens.T[None], weight_grad, mod_grad[None])


def solution(mesh):
    return jax.shard_map(
        body,
        mesh=mesh,
        in_specs=(P("dp", "seq", None), P("dp", None, None), P("seq", "dp"), P("dp", "seq", None)),
        out_specs=(P("dp", "seq", None), P("dp", "seq", None), P("seq", "dp"), P("dp", None, None)),
        check_vma=False,
    )
```

```python
import functools
import math

import jax
import jax.numpy as jnp
from jax import lax
from jax.experimental import pallas as pl
from jax.experimental.pallas import tpu as pltpu
from jax.sharding import PartitionSpec as P

HDIM = 32
AXES = ("seq", "dp")
ROWS = 70
UNIT = 144
COLS = 840
HALF = 576
GROUP = 4 * UNIT
ALL = 16 * UNIT
LANES = 128
PACK = 72
NEAR = 3 * GROUP
F32, BF16 = jnp.float32, jnp.bfloat16
WHOLE = pl.BlockSpec(memory_space=pltpu.VMEM)
ANYWHERE = pl.BlockSpec(memory_space=pl.ANY)


def place(index):
    seq, dp = divmod(index, 4)
    z_lo, rest = divmod(seq, 16)
    y, x = divmod(rest, 4)
    z_hi, core = divmod(dp, 2)
    return x, y, z_hi * 2 + z_lo, core


def index_of(x, y, z, core):
    x, y, z = x % 4, y % 4, z % 4
    return ((z % 2) * 16 + y * 4 + x) * 4 + (z // 2) * 2 + core


def route(kind, offset):
    pairs = []
    for index in range(128):
        x, y, z, core = place(index)
        if kind == "z":
            target = index_of(x, y, z + offset, core)
        elif kind == "z_lo":
            target = index_of(x, y, z ^ 1, core)
        elif kind == "z_hi":
            target = index_of(x, y, z ^ 2, core)
        elif kind == "core":
            target = index_of(x, y, z, 1 - core)
        elif (kind == "last") == (core == 0):
            target = index_of(x + offset, y, z, core)
        else:
            target = index_of(x, y + offset, z, core)
        pairs.append((index, target))
    return pairs


def send(value, kind, offset=0):
    return lax.ppermute(value, AXES, route(kind, offset))


def together(*values):
    return lax.optimization_barrier(values)


def add(left, right):
    return (left.astype(F32) + right.astype(F32)).astype(BF16)


def exchange(value, kind):
    return send(value, kind, 2), send(value, kind, -1), send(value, kind, 1)


def ring_sum(value, parts):
    far, ahead, behind = (part.astype(F32) for part in parts)
    return (value + far) + (ahead + behind)


def pick(core, on_zero, on_one):
    return jnp.where(core == 0, on_zero, on_one)


def head_half(array, core, axis, other=False):
    size = array.shape[axis]
    low = lax.slice_in_dim(array, 0, HALF, axis=axis)
    high = lax.slice_in_dim(array, size - HALF, size, axis=axis)
    return pick(core, high, low) if other else pick(core, low, high)


def head_join(mine, other, core, axis):
    second = lax.slice_in_dim(pick(core, other, mine), HDIM, HALF, axis=axis)
    return jnp.concatenate([pick(core, mine, other), second], axis=axis)


def gather_units(weight, z_lo, core, extra):
    blocks, extra = together(lax.all_gather(weight, "dp"), extra)
    columns = jnp.concatenate([blocks[i] for i in range(4)], axis=1)
    third = 4 * COLS // 3
    query, keys, values = (
        head_half(columns[:, i * third : (i + 1) * third], core, 1) for i in range(3)
    )
    mine = jnp.concatenate([keys, values, query], axis=1)
    other = send(mine, "z_lo")
    unit = jnp.concatenate([pick(z_lo, mine, other), pick(z_lo, other, mine)])
    return jnp.pad(unit, ((0, UNIT - 2 * ROWS), (0, 0))), extra


def finish_weight(unit, z_lo, dp, core):
    first, second = unit[:ROWS], unit[ROWS : 2 * ROWS]
    mine = add(pick(z_lo, first, second), send(pick(z_lo, second, first), "z_lo"))
    zero = jnp.zeros((ROWS, HALF), BF16)
    columns = jnp.concatenate(
        [head_join(mine[:, i * HALF : (i + 1) * HALF], zero, core, 1) for i in (2, 0, 1)], axis=1
    )
    blocks = jnp.stack([columns[:, i * COLS : (i + 1) * COLS] for i in range(4)])

    def block(flip):
        return lax.dynamic_index_in_dim(blocks, dp ^ flip, 0, keepdims=False)

    by_core = send(jnp.stack([block(1), block(3)]), "core")
    mine = block(0).astype(F32) + by_core[0].astype(F32)
    return mine + send(add(block(2), by_core[1]), "z_hi").astype(F32)


def params(mebibytes):
    return pltpu.CompilerParams(vmem_limit_bytes=mebibytes * 1024 * 1024)


NO_COST = pl.CostEstimate(flops=0, bytes_accessed=0, transcendentals=0)


def split(value):
    high = value.astype(BF16)
    return high, (value - high.astype(F32)).astype(BF16)


def dot(left, right, dims=((1,), (0,))):
    return lax.dot_general(left, right, (dims, ((), ())), preferred_element_type=F32)


def dot_wide(left, right, dims=((1,), (0,))):
    left_high, left_low = split(left)
    right_high, right_low = split(right)
    return dot(left_high, right_high, dims) + (
        dot(left_low, right_high, dims) + dot(left_high, right_low, dims)
    )


def dot_left(left, right, dims=((1,), (0,))):
    high, low = split(left)
    return dot(high, right, dims) + dot(low, right, dims)


def dot_right(left, right, dims=((1,), (0,))):
    high, low = split(right)
    return dot(left, high, dims) + dot(left, low, dims)


def feature(values):
    lower = jnp.exp(jnp.minimum(values, 0.0))
    return jnp.where(values > 0, values + 1.0, lower), jnp.where(values > 0, 1.0, lower)


def same_head(size):
    row = lax.broadcasted_iota(jnp.int32, (size, size), 0) // HDIM
    return row == lax.broadcasted_iota(jnp.int32, (size, size), 1) // HDIM


def diagonal(product):
    width = product.shape[1]
    kept = jnp.where(same_head(width), product, 0.0)
    total = kept[:HDIM]
    for start in range(HDIM, width, HDIM):
        total = total + kept[start : start + HDIM]
    return total


def block_diagonal(blocks):
    width = blocks.shape[1]
    tiled = jnp.concatenate([blocks] * (width // HDIM), axis=0)
    return jnp.where(same_head(width), tiled, 0.0)


def column(row):
    width = row.shape[1]
    index = lax.broadcasted_iota(jnp.int32, (width, width), 0)
    same = index == lax.broadcasted_iota(jnp.int32, (width, width), 1)
    return jnp.sum(jnp.where(same, row, 0.0), axis=1, keepdims=True)


def head_sum(array):
    return jnp.sum(array.reshape(-1, HDIM, array.shape[1]), axis=1, keepdims=True)


def by_head(array, factors):
    return (array.reshape(-1, HDIM, array.shape[1]) * factors).reshape(array.shape)


def token_sum(array):
    parts = [array[:, start : start + LANES] for start in range(0, array.shape[1], LANES)]
    ones = jnp.ones((16, LANES), BF16)
    return dot_right(ones, sum(parts[1:], parts[0]), ((1,), (1,)))[:1]


def groups():
    return [(start, min(LANES, HALF - start)) for start in range(0, HALF, LANES)]


MARK = jax.ShapeDtypeStruct((8, LANES), F32)
SCALARS = pl.BlockSpec(memory_space=pltpu.SMEM)


def unit_rows(starts_ref, number):
    return pl.ds(pl.multiple_of(starts_ref[number], 16), UNIT)


def hidden_kernel(starts_ref, *refs):
    out_ref, mark_ref, wide_ref = refs[-3:]
    mark_ref[...] = jnp.zeros_like(mark_ref)
    chunk = 112
    for clip in range(2):
        tokens_ref, mods_ref = refs[2 * clip : 2 * clip + 2]
        features, count = tokens_ref.shape
        total = jnp.zeros((1, count), F32)
        for start in range(0, features, chunk):
            values = tokens_ref[start : start + chunk, :].astype(F32)
            total = total + jnp.sum(values * values, axis=0, keepdims=True)
        inverse = lax.rsqrt(total * (1.0 / features) + 1e-06)
        for start in range(0, features, chunk):
            rows = slice(start, start + chunk)
            values = tokens_ref[rows, :].astype(F32) * inverse
            wide_ref[rows, :] = values * (1.0 + mods_ref[rows, 1:2]) + mods_ref[rows, 0:1]
        for number in range(16):
            low, high = number * ROWS, (16 + number) * ROWS
            parts = [
                wide_ref[low : low + ROWS, :],
                wide_ref[high : high + ROWS, :],
                jnp.zeros((UNIT - 2 * ROWS, count), F32),
            ]
            tokens = slice(clip * count, (clip + 1) * count)
            out_ref[unit_rows(starts_ref, number), tokens] = jnp.concatenate(parts).astype(BF16)


def make_hidden(starts, *arrays):
    features, count = arrays[0].shape
    return pl.pallas_call(
        hidden_kernel,
        out_shape=(jax.ShapeDtypeStruct((ALL, 2 * count), BF16), MARK),
        in_specs=[SCALARS] + [WHOLE] * 4,
        out_specs=(WHOLE,) * 2,
        scratch_shapes=[pltpu.VMEM((features, count), F32)],
        compiler_params=params(20),
        cost_estimate=NO_COST,
        name="hidden",
    )(starts, *arrays)


def chunks(width):
    size = 384 if width % 384 == 0 else 256
    return [slice(start, min(start + size, width)) for start in range(0, width, size)]


def halves(count):
    return [slice(0, count // 2), slice(count // 2, count)]


FIRST, LAST = ((0,), (0,)), ((1,), (1,))


def near_kernel(numbers, _, hidden_ref, *refs):
    out_ref, mark_ref = refs[-2:]
    mark_ref[...] = jnp.zeros_like(mark_ref)
    for rows in chunks(out_ref.shape[0]):
        for tokens in halves(out_ref.shape[1]):
            total = refs[len(numbers)][rows, tokens] if len(refs) > len(numbers) + 2 else 0.0
            for number, piece_ref in zip(numbers, refs, strict=False):
                depth = piece_ref.shape[0]
                part = hidden_ref[number * depth : (number + 1) * depth, tokens]
                total = total + dot(piece_ref[:, rows], part, FIRST)
            out_ref[rows, tokens] = total


def project_near(mark, hidden, pieces, numbers, before=()):
    width, count = pieces[0].shape[1], hidden.shape[1]
    return pl.pallas_call(
        functools.partial(near_kernel, numbers),
        out_shape=(jax.ShapeDtypeStruct((width, count), F32), MARK),
        in_specs=[WHOLE] * (2 + len(pieces) + len(before)),
        out_specs=(WHOLE,) * 2,
        compiler_params=params(22),
        cost_estimate=NO_COST,
        name="project_near",
    )(mark, hidden, *pieces, *before)


def far_kernel(_, hidden_ref, near_ref, first_ref, second_ref, out_ref, state_ref):
    half = GROUP // 2
    width, count = out_ref.shape
    for rows in chunks(width):
        for tokens in halves(count):
            total = near_ref[rows, tokens]
            total += dot(first_ref[:, rows], hidden_ref[NEAR : NEAR + half, tokens], FIRST)
            total += dot(second_ref[:, rows], hidden_ref[NEAR + half :, tokens], FIRST)
            out_ref[rows, tokens] = total.astype(BF16)
    state_ref[2 * HDIM :, :] = jnp.zeros((PACK - 2 * HDIM, HALF), F32)
    for start, size in groups():
        columns = slice(start, start + size)
        for clip, tokens in enumerate(halves(count)):
            keys, _ = feature(out_ref[columns, tokens].astype(F32))
            values = out_ref[HALF + start : HALF + start + size, tokens]
            product = dot_left(keys, values, LAST)
            state_ref[clip * HDIM : (clip + 1) * HDIM, columns] = diagonal(product)
            state_ref[2 * HDIM + clip : 2 * HDIM + clip + 1, columns] = token_sum(keys)


def project_far(mark, hidden, near, first, second):
    width, count = near.shape
    shapes = (
        jax.ShapeDtypeStruct((width, count), BF16),
        jax.ShapeDtypeStruct((PACK, HALF), F32),
    )
    return pl.pallas_call(
        far_kernel,
        out_shape=shapes,
        in_specs=[WHOLE] * 5,
        out_specs=(WHOLE,) * 2,
        compiler_params=params(18),
        cost_estimate=NO_COST,
        name="project_far",
    )(mark, hidden, near, first, second)


def query_kernel(hidden_ref, *refs):
    *refs, _, _, out_ref, mark_ref = refs
    mark_ref[...] = jnp.zeros_like(mark_ref)
    for rows in chunks(out_ref.shape[0]):
        for tokens in halves(out_ref.shape[1]):
            total, start = 0.0, 0
            for piece_ref in refs:
                depth = piece_ref.shape[0]
                part = hidden_ref[start : start + depth, tokens]
                total = total + dot(piece_ref[:, rows], part, FIRST)
                start += depth
            out_ref[rows, tokens] = total.astype(BF16)


def project_query(hidden, pieces, marks):
    return pl.pallas_call(
        query_kernel,
        out_shape=(jax.ShapeDtypeStruct((pieces[0].shape[1], hidden.shape[1]), BF16), MARK),
        in_specs=[WHOLE] * (3 + len(pieces)),
        out_specs=(WHOLE,) * 2,
        compiler_params=params(14),
        cost_estimate=NO_COST,
        name="project_query",
    )(hidden, *pieces, *marks)


def once(start, width, keep):
    row = lax.broadcasted_iota(jnp.int32, (width, 1), 0) + start
    return jnp.where(row < HDIM, keep, 1.0)


def middle_kernel(
    _, keep_ref, query_ref, own_ref, other_ref, state_ref, *outs
):
    attention_ref, grad_query_ref, state_grad_ref = outs
    count = query_ref.shape[1] // 2
    state_grad_ref[2 * HDIM :, :] = jnp.zeros((PACK - 2 * HDIM, HALF), F32)
    keep = keep_ref[0]
    for start, width in groups():
        rows = slice(start, start + width)
        for clip in range(2):
            tokens = slice(clip * count, (clip + 1) * count)
            mine = slice(clip * HDIM, (clip + 1) * HDIM)
            sums = slice(2 * HDIM + clip, 2 * HDIM + clip + 1)
            state = block_diagonal(state_ref[mine, rows])
            total = state_ref[sums, rows]
            total_column = column(total)
            query, slope = feature(query_ref[rows, tokens].astype(F32))
            grad = (own_ref, other_ref)[clip][rows, :].astype(F32)
            numer = dot_wide(state, query, ((0,), (0,)))
            inverse = 1.0 / (head_sum(query * total_column) + 1.0)
            quotient = by_head(numer, inverse)
            attention_ref[rows, tokens] = quotient.astype(BF16)
            grad_numer = by_head(grad, inverse)
            grad_denom = -head_sum(grad * quotient) * inverse
            product = dot(query.astype(BF16), grad_numer.astype(BF16), LAST)
            state_grad_ref[mine, rows] = diagonal(product)
            state_grad_ref[sums, rows] = token_sum(by_head(query, grad_denom))
            spread = by_head(jnp.broadcast_to(total_column, query.shape), grad_denom)
            back = dot_wide(state, grad_numer) + spread
            back = slope * back * once(start, width, keep)
            grad_query_ref[rows, tokens] = back.astype(BF16)


def make_middle(mark, keep, query, grads, state):
    count = query.shape[1]
    return pl.pallas_call(
        middle_kernel,
        out_shape=(
            jax.ShapeDtypeStruct((HALF, count), BF16),
            jax.ShapeDtypeStruct((HALF, count), BF16),
            jax.ShapeDtypeStruct((PACK, HALF), F32),
        ),
        in_specs=[WHOLE, SCALARS] + [WHOLE] * 4,
        out_specs=(WHOLE,) * 3,
        compiler_params=params(12),
        cost_estimate=NO_COST,
        name="attention",
    )(mark, keep, query, *grads, state)


def pair_grad_kernel(_, keep_ref, pair_ref, state_grad_ref, out_ref):
    count = pair_ref.shape[1] // 2
    keep = keep_ref[0]
    for start, width in groups():
        rows = slice(start, start + width)
        value_rows = slice(HALF + start, HALF + start + width)
        factor = once(start, width, keep)
        for clip in range(2):
            tokens = slice(clip * count, (clip + 1) * count)
            sums = slice(2 * HDIM + clip, 2 * HDIM + clip + 1)
            state_grad = block_diagonal(state_grad_ref[clip * HDIM : (clip + 1) * HDIM, rows])
            total_grad = column(state_grad_ref[sums, rows])
            keys, slope = feature(pair_ref[rows, tokens].astype(F32))
            state_grad = state_grad.astype(BF16)
            grad_keys = dot(state_grad, pair_ref[value_rows, tokens]) + total_grad
            grad_values = dot(state_grad, keys.astype(BF16), FIRST)
            out_ref[rows, tokens] = (slope * grad_keys * factor).astype(BF16)
            out_ref[value_rows, tokens] = (grad_values * factor).astype(BF16)


def make_pair_grad(mark, keep, pair, state_grad):
    return pl.pallas_call(
        pair_grad_kernel,
        out_shape=jax.ShapeDtypeStruct(pair.shape, BF16),
        in_specs=[WHOLE, SCALARS] + [WHOLE] * 2,
        out_specs=WHOLE,
        compiler_params=params(12),
        cost_estimate=NO_COST,
        name="pair_grad",
    )(mark, keep, pair, state_grad)


def terms_kernel(outputs, _, grad_ref, hidden_ref, *outs):
    *outs, mark_ref = outs
    mark_ref[...] = jnp.zeros_like(mark_ref)
    size = GROUP // 2
    for blocks, out_ref in zip(outputs, outs, strict=True):
        for place, number in enumerate(blocks):
            part = dot(hidden_ref[number * size : (number + 1) * size, :], grad_ref[...], LAST)
            out_ref[place * size : (place + 1) * size, :] = part.astype(BF16)


def weight_terms(gate, hidden, grad, *outputs):
    shapes = [(len(blocks) * GROUP // 2, grad.shape[0]) for blocks in outputs]
    return pl.pallas_call(
        functools.partial(terms_kernel, outputs),
        out_shape=[*(jax.ShapeDtypeStruct(shape, BF16) for shape in shapes), MARK],
        in_specs=[SCALARS] + [WHOLE] * 2,
        out_specs=[WHOLE] * (len(outputs) + 1),
        compiler_params=params(14),
        cost_estimate=NO_COST,
        name="weight_terms",
    )(gate, grad, hidden)


def parts_of(pieces, size):
    return [(piece, start) for piece in pieces for start in range(0, piece.shape[0], size)]


def back_to_plain(starts_ref, query_ref, pair_ref, tokens, pieces, wide_ref, plain_ref):
    size = GROUP // 2
    for base, (query_rows, start), (pair_rows, pair_start) in zip(
        range(0, ALL, size),
        parts_of([piece for piece in pieces if piece.shape[1] == HALF], size),
        parts_of([piece for piece in pieces if piece.shape[1] != HALF], size),
        strict=True,
    ):
        part = dot(query_rows[start : start + size, :], query_ref[:, tokens])
        part = part + dot(pair_rows[pair_start : pair_start + size, :], pair_ref[:, tokens])
        wide_ref[base : base + size, :] = part
    for number in range(16):
        low, high = number * ROWS, (16 + number) * ROWS
        unit = wide_ref[unit_rows(starts_ref, number), :]
        plain_ref[low : low + ROWS, :] = unit[:ROWS]
        plain_ref[high : high + ROWS, :] = unit[ROWS : 2 * ROWS]


def row_chunks(size):
    return [slice(start, min(start + size, 32 * ROWS)) for start in range(0, 32 * ROWS, size)]


def back_kernel(clip, starts_ref, query_ref, pair_ref, *refs):
    out_ref, mark_ref, wide_ref, plain_ref = refs[-4:]
    mark_ref[...] = jnp.zeros_like(mark_ref)
    tokens = halves(query_ref.shape[1])[clip]
    back_to_plain(starts_ref, query_ref, pair_ref, tokens, refs[:-4], wide_ref, plain_ref)
    for rows in row_chunks(112):
        out_ref[rows, :] = plain_ref[rows, :].astype(BF16)


def back_project(starts, grad_query, grad_pair, pieces, clip):
    count, features = grad_query.shape[1] // 2, 32 * ROWS
    return pl.pallas_call(
        functools.partial(back_kernel, clip),
        out_shape=(jax.ShapeDtypeStruct((features, count), BF16), MARK),
        in_specs=[SCALARS] + [WHOLE] * (2 + len(pieces)),
        out_specs=(WHOLE,) * 2,
        scratch_shapes=[pltpu.VMEM((ALL, count), F32), pltpu.VMEM((features, count), F32)],
        compiler_params=params(28),
        cost_estimate=NO_COST,
        name="back_project",
    )(starts, grad_query, grad_pair, *pieces)


def tokens_kernel(*refs):
    mine_ref, received_ref, tokens_ref, mods_ref, out_ref, sums_ref, wide_ref, plain_ref = refs[3:]
    features, count = tokens_ref.shape
    total = jnp.zeros((1, count), F32)
    for rows in row_chunks(112):
        values = tokens_ref[rows, :].astype(F32)
        total = total + jnp.sum(values * values, axis=0, keepdims=True)
    inverse = lax.rsqrt(total * (1.0 / features) + 1e-06)
    mean = jnp.zeros((1, count), F32)
    for rows in row_chunks(112):
        normed = tokens_ref[rows, :].astype(F32) * inverse
        grad = mine_ref[rows, :].astype(F32) + received_ref[rows, :].astype(F32)
        product = grad * normed
        plain_ref[rows, :] = grad
        wide_ref[rows, :] = product
        product = product * (1.0 + mods_ref[rows, 1:2])
        mean = mean + jnp.sum(product, axis=0, keepdims=True)
    for rows in row_chunks(640):
        sums_ref[0:1, rows] = token_sum(plain_ref[rows, :])
        sums_ref[1:2, rows] = token_sum(wide_ref[rows, :])
    mean = mean * (1.0 / features)
    for rows in row_chunks(112):
        normed = tokens_ref[rows, :].astype(F32) * inverse
        grad = plain_ref[rows, :] * (1.0 + mods_ref[rows, 1:2])
        out_ref[rows, :] = (inverse * (grad - normed * mean)).astype(BF16)


def make_tokens(marks, mine, received, tokens, mods):
    features, count = tokens.shape
    return pl.pallas_call(
        tokens_kernel,
        out_shape=(
            jax.ShapeDtypeStruct((features, count), BF16),
            jax.ShapeDtypeStruct((2, features), F32),
        ),
        in_specs=[WHOLE] * 7,
        out_specs=(WHOLE,) * 2,
        scratch_shapes=[pltpu.VMEM((features, count), F32), pltpu.VMEM((features, count), F32)],
        compiler_params=params(24),
        cost_estimate=NO_COST,
        name="grad_tokens",
    )(*marks, mine, received, tokens, mods)


def unit_starts(x, y, core):
    starts = []
    for at_y in range(4):
        for at_x in range(4):
            step_x, step_y = lax.rem(at_x - x + 4, 4), lax.rem(at_y - y + 4, 4)
            outer, inner = pick(core, step_x, step_y), pick(core, step_y, step_x)
            outer = jnp.where(outer == 2, 3, jnp.where(outer == 3, 2, outer))
            starts.append((outer * 4 + inner) * UNIT)
    return jnp.stack(starts).astype(jnp.int32)


def body(tokens, modulation, weight, cotangent):
    seq, dp = lax.axis_index("seq"), lax.axis_index("dp")
    x, y, z_lo = lax.rem(seq, 4), lax.rem(seq // 4, 4), seq // 16
    core = lax.rem(dp, 2)
    count, features = tokens.shape[1:]
    clip_length = count * lax.axis_size("seq")
    all_length = clip_length * lax.axis_size("dp")
    keep = jnp.where(core == 0, 1.0, 0.0).astype(F32).reshape(1)

    starts = unit_starts(x, y, core)
    half = GROUP // 2
    unit, (tokens, cotangent, modulation) = gather_units(
        weight, z_lo, core, (tokens, cotangent, modulation)
    )
    tokens_own = tokens[0].T
    tokens_other = send(tokens_own, "core")
    mods_own = modulation[0].T
    mods_other = send(modulation[0], "core").T
    grad_out = cotangent[0].T
    grads = head_half(grad_out, core, 0), send(head_half(grad_out, core, 0, other=True), "core")
    unit, tokens_other, mods_other = together(unit, tokens_other, mods_other)
    first, second = unit[: UNIT // 2], unit[UNIT // 2 :]
    ahead_first, behind_second = send(first, "middle", -1), send(second, "middle", 1)
    ahead_second, behind_first = send(second, "middle", -1), send(first, "middle", 1)
    hidden, mark = make_hidden(starts, tokens_own, mods_own, tokens_other, mods_other)
    ahead_first, behind_second, ahead_second, behind_first, mark = together(
        ahead_first, behind_second, ahead_second, behind_first, mark
    )
    far_first = send(ahead_first, "middle", -1)
    far_second = send(behind_second, "middle", 1)
    group = jnp.concatenate(
        [unit, ahead_first, ahead_second, far_first, far_second, behind_first, behind_second]
    )
    pair_group, query_group = group[:, : 2 * HALF], group[:, 2 * HALF :]
    pair_first, pair_second = pair_group[:half], pair_group[half:]

    ahead_first = send(pair_first, "last", -1)
    behind_second = send(pair_second, "last", 1)
    ahead_second = send(pair_second, "last", -1)
    behind_first = send(pair_first, "last", 1)
    pair, mark = project_near(mark, hidden, (pair_first, pair_second), (0, 1))
    pair_near = (ahead_first, ahead_second, behind_first, behind_second)
    *pair_near, mark = together(*pair_near, mark)
    pair_far_first = send(pair_near[0], "last", -1)
    pair_far_second = send(pair_near[3], "last", 1)
    pair, mark = project_near(mark, hidden, pair_near, (2, 3, 4, 5), (pair,))
    query_group, mark = together(query_group, mark)
    query_ahead = send(query_group, "last", -1)
    query_behind = send(query_group, "last", 1)
    pair, state = project_far(mark, hidden, pair, pair_far_first, pair_far_second)
    part = send(state, "z_lo")
    part, query_first, query_second = together(part, query_ahead[:half], query_behind[half:])
    state = state + part
    parts = exchange(state, "last")
    far_first, far_second = send(query_first, "last", -1), send(query_second, "last", 1)
    marks = far_first[:16, :LANES], far_second[:16, :LANES]
    *parts, mark_first, mark_second = together(*parts, *marks)
    state = ring_sum(state, parts)
    parts = exchange(state, "middle")
    query_pieces = (query_group, query_ahead, query_behind, far_first, far_second)
    query, mark = project_query(hidden, query_pieces, (mark_first, mark_second))
    *parts, mark = together(*parts, mark)
    state = ring_sum(state, parts)

    attention, grad_query, state_grad = make_middle(mark, keep, query, grads, state)
    parts = exchange(state_grad.astype(BF16), "last")
    far_first, far_second, _ = weight_terms(starts, hidden, grad_query, (6,), (7,))
    *parts, far_first, far_second, gate = together(*parts, far_first, far_second, starts)
    state_grad = ring_sum(state_grad, parts)
    parts = exchange(state_grad.astype(BF16), "middle")
    far_first, far_second = send(far_first, "last", 1), send(far_second, "last", -1)
    ahead, behind, own_query, mark = weight_terms(gate, hidden, grad_query, (2, 3), (4, 5), (0, 1))
    *parts, far_first, far_second, attention, mark = together(
        *parts, far_first, far_second, attention, mark
    )
    state_grad = ring_sum(state_grad, parts)
    part = send(state_grad.astype(BF16), "z_lo")
    other_attention = send(attention[:, count:], "core")
    ahead = jnp.concatenate([add(ahead[:half], far_first), ahead[half:]])
    behind = jnp.concatenate([behind[:half], add(behind[half:], far_second)])
    state_grad = state_grad + part.astype(F32)
    query_from_behind, query_from_ahead = send(ahead, "last", 1), send(behind, "last", -1)
    grad_pair = make_pair_grad(mark, keep, pair, state_grad)
    soon_ahead, soon_behind, _ = weight_terms(starts, hidden, grad_pair, (6, 3), (7, 4))
    soon_ahead, soon_behind, gate, other_attention, query_from_behind, query_from_ahead = together(
        soon_ahead, soon_behind, starts, other_attention, query_from_behind, query_from_ahead
    )
    from_behind, from_ahead = send(soon_ahead, "last", 1), send(soon_behind, "last", -1)
    pieces = (*query_pieces, pair_first, pair_second, *pair_near, pair_far_first, pair_far_second)
    received, mark_other = back_project(gate, grad_query, grad_pair, pieces, 1)
    grad_hidden, mark_own = back_project(gate, grad_query, grad_pair, pieces, 0)
    later_ahead, later_behind, own_first, own_second, mark = weight_terms(
        gate, hidden, grad_pair, (2,), (5,), (0,), (1,)
    )
    attention = head_join(attention[:, :count], other_attention, core, 0)
    from_behind, from_ahead, received, attention, *marks = together(
        from_behind, from_ahead, received, attention, mark, mark_other, mark_own
    )
    received = send(received, "core")
    plain_ahead, plain_behind = from_behind[half:], from_ahead[half:]
    from_behind = send(add(later_ahead, from_behind[:half]), "last", 1)
    from_ahead = send(add(later_behind, from_ahead[:half]), "last", -1)
    grad_tokens, mod_grad = make_tokens(marks, grad_hidden, received, tokens_own, mods_own)
    from_behind, from_ahead, mod_grad = together(from_behind, from_ahead, mod_grad)
    query_part = own_query.astype(F32) + (
        query_from_behind.astype(F32) + query_from_ahead.astype(F32)
    )
    pair_part = jnp.concatenate(
        [
            own_first.astype(F32) + from_behind.astype(F32) + plain_behind.astype(F32),
            own_second.astype(F32) + plain_ahead.astype(F32) + from_ahead.astype(F32),
        ]
    )
    group = jnp.concatenate([pair_part, query_part], axis=1).astype(BF16)
    own, ahead, far, behind = jnp.split(group, 4)
    far_first = send(far[: UNIT // 2], "middle", 1)
    far_second = send(far[UNIT // 2 :], "middle", -1)
    parts = exchange(mod_grad, "last")
    *parts, far_first, far_second = together(*parts, far_first, far_second)
    mod_grad = ring_sum(mod_grad, parts)
    ahead = jnp.concatenate([add(ahead[: UNIT // 2], far_first), ahead[UNIT // 2 :]])
    behind = jnp.concatenate([behind[: UNIT // 2], add(behind[UNIT // 2 :], far_second)])
    from_behind = send(ahead, "middle", 1)
    from_ahead = send(behind, "middle", -1)
    parts = exchange(mod_grad, "middle")
    *parts, from_behind, from_ahead = together(*parts, from_behind, from_ahead)
    mod_grad = ring_sum(mod_grad, parts)
    mod_grad = (mod_grad + send(mod_grad, "z_lo")) * (1.0 / math.sqrt(clip_length))
    unit = (own.astype(F32) + from_behind.astype(F32) + from_ahead.astype(F32)).astype(BF16)
    weight_grad = finish_weight(unit, z_lo, dp, core)
    weight_grad = weight_grad * (1.0 / math.sqrt(all_length))
    return (attention.T[None], grad_tokens.T[None], weight_grad, mod_grad[None])


def solution(mesh):
    return jax.shard_map(
        body,
        mesh=mesh,
        in_specs=(P("dp", "seq", None), P("dp", None, None), P("seq", "dp"), P("dp", "seq", None)),
        out_specs=(P("dp", "seq", None), P("dp", "seq", None), P("seq", "dp"), P("dp", None, None)),
        check_vma=False,
    )
```

```python
import functools
import math

import jax
import jax.numpy as jnp
from jax import lax
from jax.experimental import pallas as pl
from jax.experimental.pallas import tpu as pltpu
from jax.sharding import PartitionSpec as P

HDIM = 32
AXES = ("seq", "dp")
ROWS = 70
UNIT = 144
COLS = 840
HALF = 576
GROUP = 4 * UNIT
ALL = 16 * UNIT
LANES = 128
PACK = 72
NEAR = 3 * GROUP
F32, BF16 = jnp.float32, jnp.bfloat16
WHOLE = pl.BlockSpec(memory_space=pltpu.VMEM)
ANYWHERE = pl.BlockSpec(memory_space=pl.ANY)


def place(index):
    seq, dp = divmod(index, 4)
    z_lo, rest = divmod(seq, 16)
    y, x = divmod(rest, 4)
    z_hi, core = divmod(dp, 2)
    return x, y, z_hi * 2 + z_lo, core


def index_of(x, y, z, core):
    x, y, z = x % 4, y % 4, z % 4
    return ((z % 2) * 16 + y * 4 + x) * 4 + (z // 2) * 2 + core


def route(kind, offset):
    pairs = []
    for index in range(128):
        x, y, z, core = place(index)
        if kind == "z":
            target = index_of(x, y, z + offset, core)
        elif kind == "z_lo":
            target = index_of(x, y, z ^ 1, core)
        elif kind == "z_hi":
            target = index_of(x, y, z ^ 2, core)
        elif kind == "core":
            target = index_of(x, y, z, 1 - core)
        elif (kind == "last") == (core == 0):
            target = index_of(x + offset, y, z, core)
        else:
            target = index_of(x, y + offset, z, core)
        pairs.append((index, target))
    return pairs


def send(value, kind, offset=0):
    return lax.ppermute(value, AXES, route(kind, offset))


def together(*values):
    return lax.optimization_barrier(values)


def add(left, right):
    return (left.astype(F32) + right.astype(F32)).astype(BF16)


def exchange(value, kind):
    return send(value, kind, 2), send(value, kind, -1), send(value, kind, 1)


def ring_sum(value, parts):
    far, ahead, behind = (part.astype(F32) for part in parts)
    return (value + far) + (ahead + behind)


def pick(core, on_zero, on_one):
    return jnp.where(core == 0, on_zero, on_one)


def head_half(array, core, axis, other=False):
    size = array.shape[axis]
    low = lax.slice_in_dim(array, 0, HALF, axis=axis)
    high = lax.slice_in_dim(array, size - HALF, size, axis=axis)
    return pick(core, high, low) if other else pick(core, low, high)


def head_join(mine, other, core, axis):
    second = lax.slice_in_dim(pick(core, other, mine), HDIM, HALF, axis=axis)
    return jnp.concatenate([pick(core, mine, other), second], axis=axis)


def gather_units(weight, z_lo, core, extra):
    blocks, extra = together(lax.all_gather(weight, "dp"), extra)
    columns = jnp.concatenate([blocks[i] for i in range(4)], axis=1)
    third = 4 * COLS // 3
    query, keys, values = (
        head_half(columns[:, i * third : (i + 1) * third], core, 1) for i in range(3)
    )
    mine = jnp.concatenate([keys, values, query], axis=1)
    other = send(mine, "z_lo")
    unit = jnp.concatenate([pick(z_lo, mine, other), pick(z_lo, other, mine)])
    return jnp.pad(unit, ((0, UNIT - 2 * ROWS), (0, 0))), extra


def finish_weight(unit, z_lo, dp, core):
    first, second = unit[:ROWS], unit[ROWS : 2 * ROWS]
    mine = add(pick(z_lo, first, second), send(pick(z_lo, second, first), "z_lo"))
    zero = jnp.zeros((ROWS, HALF), BF16)
    columns = jnp.concatenate(
        [head_join(mine[:, i * HALF : (i + 1) * HALF], zero, core, 1) for i in (2, 0, 1)], axis=1
    )
    blocks = jnp.stack([columns[:, i * COLS : (i + 1) * COLS] for i in range(4)])

    def block(flip):
        return lax.dynamic_index_in_dim(blocks, dp ^ flip, 0, keepdims=False)

    by_core = send(jnp.stack([block(1), block(3)]), "core")
    mine = block(0).astype(F32) + by_core[0].astype(F32)
    return mine + send(add(block(2), by_core[1]), "z_hi").astype(F32)


def params(mebibytes):
    return pltpu.CompilerParams(vmem_limit_bytes=mebibytes * 1024 * 1024)


NO_COST = pl.CostEstimate(flops=0, bytes_accessed=0, transcendentals=0)


def split(value):
    high = value.astype(BF16)
    return high, (value - high.astype(F32)).astype(BF16)


def dot(left, right, dims=((1,), (0,))):
    return lax.dot_general(left, right, (dims, ((), ())), preferred_element_type=F32)


def dot_wide(left, right, dims=((1,), (0,))):
    left_high, left_low = split(left)
    right_high, right_low = split(right)
    (left_axis,), (right_axis,) = dims
    left_twice = jnp.concatenate([left_high, left_high], axis=left_axis)
    right_both = jnp.concatenate([right_high, right_low], axis=right_axis)
    return dot(left_twice, right_both, dims) + dot(left_low, right_high, dims)


def dot_left(left, right, dims=((1,), (0,))):
    high, low = split(left)
    return dot(high, right, dims) + dot(low, right, dims)


def dot_right(left, right, dims=((1,), (0,))):
    high, low = split(right)
    return dot(left, high, dims) + dot(left, low, dims)


def feature(values):
    lower = jnp.exp(jnp.minimum(values, 0.0))
    return jnp.where(values > 0, values + 1.0, lower), jnp.where(values > 0, 1.0, lower)


def same_head(size):
    row = lax.broadcasted_iota(jnp.int32, (size, size), 0) // HDIM
    return row == lax.broadcasted_iota(jnp.int32, (size, size), 1) // HDIM


def diagonal(product):
    width = product.shape[1]
    kept = jnp.where(same_head(width), product, 0.0)
    total = kept[:HDIM]
    for start in range(HDIM, width, HDIM):
        total = total + kept[start : start + HDIM]
    return total


def block_diagonal(blocks):
    width = blocks.shape[1]
    tiled = jnp.concatenate([blocks] * (width // HDIM), axis=0)
    return jnp.where(same_head(width), tiled, 0.0)


def column(row):
    width = row.shape[1]
    index = lax.broadcasted_iota(jnp.int32, (width, width), 0)
    same = index == lax.broadcasted_iota(jnp.int32, (width, width), 1)
    return jnp.sum(jnp.where(same, row, 0.0), axis=1, keepdims=True)


def head_sum(array):
    return jnp.sum(array.reshape(-1, HDIM, array.shape[1]), axis=1, keepdims=True)


def by_head(array, factors):
    return (array.reshape(-1, HDIM, array.shape[1]) * factors).reshape(array.shape)


def token_sum(array):
    parts = [array[:, start : start + LANES] for start in range(0, array.shape[1], LANES)]
    ones = jnp.ones((16, LANES), BF16)
    return dot_right(ones, sum(parts[1:], parts[0]), ((1,), (1,)))[:1]


def groups():
    return [(start, min(LANES, HALF - start)) for start in range(0, HALF, LANES)]


MARK = jax.ShapeDtypeStruct((8, LANES), F32)
SCALARS = pl.BlockSpec(memory_space=pltpu.SMEM)


def unit_rows(starts_ref, number):
    return pl.ds(pl.multiple_of(starts_ref[number], 16), UNIT)


def hidden_kernel(starts_ref, *refs):
    out_ref, mark_ref, wide_ref = refs[-3:]
    mark_ref[...] = jnp.zeros_like(mark_ref)
    chunk = 112
    for clip in range(2):
        tokens_ref, mods_ref = refs[2 * clip : 2 * clip + 2]
        features, count = tokens_ref.shape
        total = jnp.zeros((1, count), F32)
        for start in range(0, features, chunk):
            values = tokens_ref[start : start + chunk, :].astype(F32)
            total = total + jnp.sum(values * values, axis=0, keepdims=True)
        inverse = lax.rsqrt(total * (1.0 / features) + 1e-06)
        for start in range(0, features, chunk):
            rows = slice(start, start + chunk)
            values = tokens_ref[rows, :].astype(F32) * inverse
            wide_ref[rows, :] = values * (1.0 + mods_ref[rows, 1:2]) + mods_ref[rows, 0:1]
        for number in range(16):
            low, high = number * ROWS, (16 + number) * ROWS
            parts = [
                wide_ref[low : low + ROWS, :],
                wide_ref[high : high + ROWS, :],
                jnp.zeros((UNIT - 2 * ROWS, count), F32),
            ]
            tokens = slice(clip * count, (clip + 1) * count)
            out_ref[unit_rows(starts_ref, number), tokens] = jnp.concatenate(parts).astype(BF16)


def make_hidden(starts, *arrays):
    features, count = arrays[0].shape
    return pl.pallas_call(
        hidden_kernel,
        out_shape=(jax.ShapeDtypeStruct((ALL, 2 * count), BF16), MARK),
        in_specs=[SCALARS] + [WHOLE] * 4,
        out_specs=(WHOLE,) * 2,
        scratch_shapes=[pltpu.VMEM((features, count), F32)],
        compiler_params=params(20),
        cost_estimate=NO_COST,
        name="hidden",
    )(starts, *arrays)


def chunks(width):
    size = 384 if width % 384 == 0 else 256
    return [slice(start, min(start + size, width)) for start in range(0, width, size)]


def halves(count):
    return [slice(0, count // 2), slice(count // 2, count)]


FIRST, LAST = ((0,), (0,)), ((1,), (1,))


def near_kernel(numbers, _, hidden_ref, *refs):
    out_ref, mark_ref = refs[-2:]
    mark_ref[...] = jnp.zeros_like(mark_ref)
    for rows in chunks(out_ref.shape[0]):
        for tokens in halves(out_ref.shape[1]):
            total = refs[len(numbers)][rows, tokens] if len(refs) > len(numbers) + 2 else 0.0
            for number, piece_ref in zip(numbers, refs, strict=False):
                depth = piece_ref.shape[0]
                part = hidden_ref[number * depth : (number + 1) * depth, tokens]
                total = total + dot(piece_ref[:, rows], part, FIRST)
            out_ref[rows, tokens] = total


def project_near(mark, hidden, pieces, numbers, before=()):
    width, count = pieces[0].shape[1], hidden.shape[1]
    return pl.pallas_call(
        functools.partial(near_kernel, numbers),
        out_shape=(jax.ShapeDtypeStruct((width, count), F32), MARK),
        in_specs=[WHOLE] * (2 + len(pieces) + len(before)),
        out_specs=(WHOLE,) * 2,
        compiler_params=params(22),
        cost_estimate=NO_COST,
        name="project_near",
    )(mark, hidden, *pieces, *before)


def far_kernel(_, hidden_ref, near_ref, first_ref, second_ref, out_ref, state_ref):
    half = GROUP // 2
    width, count = out_ref.shape
    for rows in chunks(width):
        for tokens in halves(count):
            total = near_ref[rows, tokens]
            total += dot(first_ref[:, rows], hidden_ref[NEAR : NEAR + half, tokens], FIRST)
            total += dot(second_ref[:, rows], hidden_ref[NEAR + half :, tokens], FIRST)
            out_ref[rows, tokens] = total.astype(BF16)
    state_ref[2 * HDIM :, :] = jnp.zeros((PACK - 2 * HDIM, HALF), F32)
    for start, size in groups():
        columns = slice(start, start + size)
        for clip, tokens in enumerate(halves(count)):
            keys, _ = feature(out_ref[columns, tokens].astype(F32))
            values = out_ref[HALF + start : HALF + start + size, tokens]
            product = dot_left(keys, values, LAST)
            state_ref[clip * HDIM : (clip + 1) * HDIM, columns] = diagonal(product)
            state_ref[2 * HDIM + clip : 2 * HDIM + clip + 1, columns] = token_sum(keys)


def project_far(mark, hidden, near, first, second):
    width, count = near.shape
    shapes = (
        jax.ShapeDtypeStruct((width, count), BF16),
        jax.ShapeDtypeStruct((PACK, HALF), F32),
    )
    return pl.pallas_call(
        far_kernel,
        out_shape=shapes,
        in_specs=[WHOLE] * 5,
        out_specs=(WHOLE,) * 2,
        compiler_params=params(18),
        cost_estimate=NO_COST,
        name="project_far",
    )(mark, hidden, near, first, second)


def query_kernel(hidden_ref, *refs):
    *refs, _, _, out_ref, mark_ref = refs
    mark_ref[...] = jnp.zeros_like(mark_ref)
    for rows in chunks(out_ref.shape[0]):
        for tokens in halves(out_ref.shape[1]):
            total, start = 0.0, 0
            for piece_ref in refs:
                depth = piece_ref.shape[0]
                part = hidden_ref[start : start + depth, tokens]
                total = total + dot(piece_ref[:, rows], part, FIRST)
                start += depth
            out_ref[rows, tokens] = total.astype(BF16)


def project_query(hidden, pieces, marks):
    return pl.pallas_call(
        query_kernel,
        out_shape=(jax.ShapeDtypeStruct((pieces[0].shape[1], hidden.shape[1]), BF16), MARK),
        in_specs=[WHOLE] * (3 + len(pieces)),
        out_specs=(WHOLE,) * 2,
        compiler_params=params(14),
        cost_estimate=NO_COST,
        name="project_query",
    )(hidden, *pieces, *marks)


def once(start, width, keep):
    row = lax.broadcasted_iota(jnp.int32, (width, 1), 0) + start
    return jnp.where(row < HDIM, keep, 1.0)


def middle_kernel(
    _, keep_ref, query_ref, own_ref, other_ref, state_ref, *outs
):
    attention_ref, grad_query_ref, state_grad_ref = outs
    count = query_ref.shape[1] // 2
    state_grad_ref[2 * HDIM :, :] = jnp.zeros((PACK - 2 * HDIM, HALF), F32)
    keep = keep_ref[0]
    for start, width in groups():
        rows = slice(start, start + width)
        for clip in range(2):
            tokens = slice(clip * count, (clip + 1) * count)
            mine = slice(clip * HDIM, (clip + 1) * HDIM)
            sums = slice(2 * HDIM + clip, 2 * HDIM + clip + 1)
            state = block_diagonal(state_ref[mine, rows])
            total = state_ref[sums, rows]
            total_column = column(total)
            query, slope = feature(query_ref[rows, tokens].astype(F32))
            grad = (own_ref, other_ref)[clip][rows, :].astype(F32)
            numer = dot_wide(state, query, ((0,), (0,)))
            inverse = 1.0 / (head_sum(query * total_column) + 1.0)
            quotient = by_head(numer, inverse)
            attention_ref[rows, tokens] = quotient.astype(BF16)
            grad_numer = by_head(grad, inverse)
            grad_denom = -head_sum(grad * quotient) * inverse
            product = dot(query.astype(BF16), grad_numer.astype(BF16), LAST)
            state_grad_ref[mine, rows] = diagonal(product)
            state_grad_ref[sums, rows] = token_sum(by_head(query, grad_denom))
            spread = by_head(jnp.broadcast_to(total_column, query.shape), grad_denom)
            back = dot_wide(state, grad_numer) + spread
            back = slope * back * once(start, width, keep)
            grad_query_ref[rows, tokens] = back.astype(BF16)


def make_middle(mark, keep, query, grads, state):
    count = query.shape[1]
    return pl.pallas_call(
        middle_kernel,
        out_shape=(
            jax.ShapeDtypeStruct((HALF, count), BF16),
            jax.ShapeDtypeStruct((HALF, count), BF16),
            jax.ShapeDtypeStruct((PACK, HALF), F32),
        ),
        in_specs=[WHOLE, SCALARS] + [WHOLE] * 4,
        out_specs=(WHOLE,) * 3,
        compiler_params=params(12),
        cost_estimate=NO_COST,
        name="attention",
    )(mark, keep, query, *grads, state)


def pair_grad_kernel(_, keep_ref, pair_ref, state_grad_ref, out_ref):
    count = pair_ref.shape[1] // 2
    keep = keep_ref[0]
    for start, width in groups():
        rows = slice(start, start + width)
        value_rows = slice(HALF + start, HALF + start + width)
        factor = once(start, width, keep)
        for clip in range(2):
            tokens = slice(clip * count, (clip + 1) * count)
            sums = slice(2 * HDIM + clip, 2 * HDIM + clip + 1)
            state_grad = block_diagonal(state_grad_ref[clip * HDIM : (clip + 1) * HDIM, rows])
            total_grad = column(state_grad_ref[sums, rows])
            keys, slope = feature(pair_ref[rows, tokens].astype(F32))
            state_grad = state_grad.astype(BF16)
            grad_keys = dot(state_grad, pair_ref[value_rows, tokens]) + total_grad
            grad_values = dot(state_grad, keys.astype(BF16), FIRST)
            out_ref[rows, tokens] = (slope * grad_keys * factor).astype(BF16)
            out_ref[value_rows, tokens] = (grad_values * factor).astype(BF16)


def make_pair_grad(mark, keep, pair, state_grad):
    return pl.pallas_call(
        pair_grad_kernel,
        out_shape=jax.ShapeDtypeStruct(pair.shape, BF16),
        in_specs=[WHOLE, SCALARS] + [WHOLE] * 2,
        out_specs=WHOLE,
        compiler_params=params(12),
        cost_estimate=NO_COST,
        name="pair_grad",
    )(mark, keep, pair, state_grad)


def terms_kernel(outputs, _, grad_ref, hidden_ref, *outs):
    *outs, mark_ref = outs
    mark_ref[...] = jnp.zeros_like(mark_ref)
    size = GROUP // 2
    for blocks, out_ref in zip(outputs, outs, strict=True):
        for place, number in enumerate(blocks):
            part = dot(hidden_ref[number * size : (number + 1) * size, :], grad_ref[...], LAST)
            out_ref[place * size : (place + 1) * size, :] = part.astype(BF16)


def weight_terms(gate, hidden, grad, *outputs):
    shapes = [(len(blocks) * GROUP // 2, grad.shape[0]) for blocks in outputs]
    return pl.pallas_call(
        functools.partial(terms_kernel, outputs),
        out_shape=[*(jax.ShapeDtypeStruct(shape, BF16) for shape in shapes), MARK],
        in_specs=[SCALARS] + [WHOLE] * 2,
        out_specs=[WHOLE] * (len(outputs) + 1),
        compiler_params=params(14),
        cost_estimate=NO_COST,
        name="weight_terms",
    )(gate, grad, hidden)


def parts_of(pieces, size):
    return [(piece, start) for piece in pieces for start in range(0, piece.shape[0], size)]


def back_to_plain(starts_ref, query_ref, pair_ref, tokens, pieces, wide_ref, plain_ref):
    size = GROUP // 2
    for base, (query_rows, start), (pair_rows, pair_start) in zip(
        range(0, ALL, size),
        parts_of([piece for piece in pieces if piece.shape[1] == HALF], size),
        parts_of([piece for piece in pieces if piece.shape[1] != HALF], size),
        strict=True,
    ):
        part = dot(query_rows[start : start + size, :], query_ref[:, tokens])
        part = part + dot(pair_rows[pair_start : pair_start + size, :], pair_ref[:, tokens])
        wide_ref[base : base + size, :] = part
    for number in range(16):
        low, high = number * ROWS, (16 + number) * ROWS
        unit = wide_ref[unit_rows(starts_ref, number), :]
        plain_ref[low : low + ROWS, :] = unit[:ROWS]
        plain_ref[high : high + ROWS, :] = unit[ROWS : 2 * ROWS]


def row_chunks(size):
    return [slice(start, min(start + size, 32 * ROWS)) for start in range(0, 32 * ROWS, size)]


def back_kernel(clip, starts_ref, query_ref, pair_ref, *refs):
    out_ref, mark_ref, wide_ref, plain_ref = refs[-4:]
    mark_ref[...] = jnp.zeros_like(mark_ref)
    tokens = halves(query_ref.shape[1])[clip]
    back_to_plain(starts_ref, query_ref, pair_ref, tokens, refs[:-4], wide_ref, plain_ref)
    for rows in row_chunks(112):
        out_ref[rows, :] = plain_ref[rows, :].astype(BF16)


def back_project(starts, grad_query, grad_pair, pieces, clip):
    count, features = grad_query.shape[1] // 2, 32 * ROWS
    return pl.pallas_call(
        functools.partial(back_kernel, clip),
        out_shape=(jax.ShapeDtypeStruct((features, count), BF16), MARK),
        in_specs=[SCALARS] + [WHOLE] * (2 + len(pieces)),
        out_specs=(WHOLE,) * 2,
        scratch_shapes=[pltpu.VMEM((ALL, count), F32), pltpu.VMEM((features, count), F32)],
        compiler_params=params(28),
        cost_estimate=NO_COST,
        name="back_project",
    )(starts, grad_query, grad_pair, *pieces)


def tokens_kernel(*refs):
    mine_ref, received_ref, tokens_ref, mods_ref, out_ref, sums_ref, wide_ref, plain_ref = refs[3:]
    features, count = tokens_ref.shape
    total = jnp.zeros((1, count), F32)
    for rows in row_chunks(112):
        values = tokens_ref[rows, :].astype(F32)
        total = total + jnp.sum(values * values, axis=0, keepdims=True)
    inverse = lax.rsqrt(total * (1.0 / features) + 1e-06)
    mean = jnp.zeros((1, count), F32)
    for rows in row_chunks(112):
        normed = tokens_ref[rows, :].astype(F32) * inverse
        grad = mine_ref[rows, :].astype(F32) + received_ref[rows, :].astype(F32)
        product = grad * normed
        plain_ref[rows, :] = grad
        wide_ref[rows, :] = product
        product = product * (1.0 + mods_ref[rows, 1:2])
        mean = mean + jnp.sum(product, axis=0, keepdims=True)
    for rows in row_chunks(640):
        sums_ref[0:1, rows] = token_sum(plain_ref[rows, :])
        sums_ref[1:2, rows] = token_sum(wide_ref[rows, :])
    mean = mean * (1.0 / features)
    for rows in row_chunks(112):
        normed = tokens_ref[rows, :].astype(F32) * inverse
        grad = plain_ref[rows, :] * (1.0 + mods_ref[rows, 1:2])
        out_ref[rows, :] = (inverse * (grad - normed * mean)).astype(BF16)


def make_tokens(marks, mine, received, tokens, mods):
    features, count = tokens.shape
    return pl.pallas_call(
        tokens_kernel,
        out_shape=(
            jax.ShapeDtypeStruct((features, count), BF16),
            jax.ShapeDtypeStruct((2, features), F32),
        ),
        in_specs=[WHOLE] * 7,
        out_specs=(WHOLE,) * 2,
        scratch_shapes=[pltpu.VMEM((features, count), F32), pltpu.VMEM((features, count), F32)],
        compiler_params=params(24),
        cost_estimate=NO_COST,
        name="grad_tokens",
    )(*marks, mine, received, tokens, mods)


def unit_starts(x, y, core):
    starts = []
    for at_y in range(4):
        for at_x in range(4):
            step_x, step_y = lax.rem(at_x - x + 4, 4), lax.rem(at_y - y + 4, 4)
            outer, inner = pick(core, step_x, step_y), pick(core, step_y, step_x)
            outer = jnp.where(outer == 2, 3, jnp.where(outer == 3, 2, outer))
            starts.append((outer * 4 + inner) * UNIT)
    return jnp.stack(starts).astype(jnp.int32)


def body(tokens, modulation, weight, cotangent):
    seq, dp = lax.axis_index("seq"), lax.axis_index("dp")
    x, y, z_lo = lax.rem(seq, 4), lax.rem(seq // 4, 4), seq // 16
    core = lax.rem(dp, 2)
    count, features = tokens.shape[1:]
    clip_length = count * lax.axis_size("seq")
    all_length = clip_length * lax.axis_size("dp")
    keep = jnp.where(core == 0, 1.0, 0.0).astype(F32).reshape(1)

    starts = unit_starts(x, y, core)
    half = GROUP // 2
    unit, (tokens, cotangent, modulation) = gather_units(
        weight, z_lo, core, (tokens, cotangent, modulation)
    )
    tokens_own = tokens[0].T
    tokens_other = send(tokens_own, "core")
    mods_own = modulation[0].T
    mods_other = send(modulation[0], "core").T
    grad_out = cotangent[0].T
    grads = head_half(grad_out, core, 0), send(head_half(grad_out, core, 0, other=True), "core")
    unit, tokens_other, mods_other = together(unit, tokens_other, mods_other)
    first, second = unit[: UNIT // 2], unit[UNIT // 2 :]
    ahead_first, behind_second = send(first, "middle", -1), send(second, "middle", 1)
    ahead_second, behind_first = send(second, "middle", -1), send(first, "middle", 1)
    hidden, mark = make_hidden(starts, tokens_own, mods_own, tokens_other, mods_other)
    ahead_first, behind_second, ahead_second, behind_first, mark = together(
        ahead_first, behind_second, ahead_second, behind_first, mark
    )
    far_first = send(ahead_first, "middle", -1)
    far_second = send(behind_second, "middle", 1)
    group = jnp.concatenate(
        [unit, ahead_first, ahead_second, far_first, far_second, behind_first, behind_second]
    )
    pair_group, query_group = group[:, : 2 * HALF], group[:, 2 * HALF :]
    pair_first, pair_second = pair_group[:half], pair_group[half:]

    ahead_first = send(pair_first, "last", -1)
    behind_second = send(pair_second, "last", 1)
    ahead_second = send(pair_second, "last", -1)
    behind_first = send(pair_first, "last", 1)
    pair, mark = project_near(mark, hidden, (pair_first, pair_second), (0, 1))
    pair_near = (ahead_first, ahead_second, behind_first, behind_second)
    *pair_near, mark = together(*pair_near, mark)
    pair_far_first = send(pair_near[0], "last", -1)
    pair_far_second = send(pair_near[3], "last", 1)
    pair, mark = project_near(mark, hidden, pair_near, (2, 3, 4, 5), (pair,))
    query_group, mark = together(query_group, mark)
    query_ahead = send(query_group, "last", -1)
    query_behind = send(query_group, "last", 1)
    pair, state = project_far(mark, hidden, pair, pair_far_first, pair_far_second)
    part = send(state, "z_lo")
    part, query_first, query_second = together(part, query_ahead[:half], query_behind[half:])
    state = state + part
    parts = exchange(state, "last")
    far_first, far_second = send(query_first, "last", -1), send(query_second, "last", 1)
    marks = far_first[:16, :LANES], far_second[:16, :LANES]
    *parts, mark_first, mark_second = together(*parts, *marks)
    state = ring_sum(state, parts)
    parts = exchange(state, "middle")
    query_pieces = (query_group, query_ahead, query_behind, far_first, far_second)
    query, mark = project_query(hidden, query_pieces, (mark_first, mark_second))
    *parts, mark = together(*parts, mark)
    state = ring_sum(state, parts)

    attention, grad_query, state_grad = make_middle(mark, keep, query, grads, state)
    parts = exchange(state_grad.astype(BF16), "last")
    far_first, far_second, _ = weight_terms(starts, hidden, grad_query, (6,), (7,))
    *parts, far_first, far_second, gate = together(*parts, far_first, far_second, starts)
    state_grad = ring_sum(state_grad, parts)
    parts = exchange(state_grad.astype(BF16), "middle")
    far_first, far_second = send(far_first, "last", 1), send(far_second, "last", -1)
    ahead, behind, own_query, mark = weight_terms(gate, hidden, grad_query, (2, 3), (4, 5), (0, 1))
    *parts, far_first, far_second, attention, mark = together(
        *parts, far_first, far_second, attention, mark
    )
    state_grad = ring_sum(state_grad, parts)
    part = send(state_grad.astype(BF16), "z_lo")
    other_attention = send(attention[:, count:], "core")
    ahead = jnp.concatenate([add(ahead[:half], far_first), ahead[half:]])
    behind = jnp.concatenate([behind[:half], add(behind[half:], far_second)])
    state_grad = state_grad + part.astype(F32)
    query_from_behind, query_from_ahead = send(ahead, "last", 1), send(behind, "last", -1)
    grad_pair = make_pair_grad(mark, keep, pair, state_grad)
    soon_ahead, soon_behind, _ = weight_terms(starts, hidden, grad_pair, (6, 3), (7, 4))
    soon_ahead, soon_behind, gate, other_attention, query_from_behind, query_from_ahead = together(
        soon_ahead, soon_behind, starts, other_attention, query_from_behind, query_from_ahead
    )
    from_behind, from_ahead = send(soon_ahead, "last", 1), send(soon_behind, "last", -1)
    pieces = (*query_pieces, pair_first, pair_second, *pair_near, pair_far_first, pair_far_second)
    received, mark_other = back_project(gate, grad_query, grad_pair, pieces, 1)
    grad_hidden, mark_own = back_project(gate, grad_query, grad_pair, pieces, 0)
    later_ahead, later_behind, own_first, own_second, mark = weight_terms(
        gate, hidden, grad_pair, (2,), (5,), (0,), (1,)
    )
    attention = head_join(attention[:, :count], other_attention, core, 0)
    from_behind, from_ahead, received, attention, *marks = together(
        from_behind, from_ahead, received, attention, mark, mark_other, mark_own
    )
    received = send(received, "core")
    plain_ahead, plain_behind = from_behind[half:], from_ahead[half:]
    from_behind = send(add(later_ahead, from_behind[:half]), "last", 1)
    from_ahead = send(add(later_behind, from_ahead[:half]), "last", -1)
    grad_tokens, mod_grad = make_tokens(marks, grad_hidden, received, tokens_own, mods_own)
    from_behind, from_ahead, mod_grad = together(from_behind, from_ahead, mod_grad)
    query_part = own_query.astype(F32) + (
        query_from_behind.astype(F32) + query_from_ahead.astype(F32)
    )
    pair_part = jnp.concatenate(
        [
            own_first.astype(F32) + from_behind.astype(F32) + plain_behind.astype(F32),
            own_second.astype(F32) + plain_ahead.astype(F32) + from_ahead.astype(F32),
        ]
    )
    group = jnp.concatenate([pair_part, query_part], axis=1).astype(BF16)
    own, ahead, far, behind = jnp.split(group, 4)
    far_first = send(far[: UNIT // 2], "middle", 1)
    far_second = send(far[UNIT // 2 :], "middle", -1)
    parts = exchange(mod_grad, "last")
    *parts, far_first, far_second = together(*parts, far_first, far_second)
    mod_grad = ring_sum(mod_grad, parts)
    ahead = jnp.concatenate([add(ahead[: UNIT // 2], far_first), ahead[UNIT // 2 :]])
    behind = jnp.concatenate([behind[: UNIT // 2], add(behind[UNIT // 2 :], far_second)])
    from_behind = send(ahead, "middle", 1)
    from_ahead = send(behind, "middle", -1)
    parts = exchange(mod_grad, "middle")
    *parts, from_behind, from_ahead = together(*parts, from_behind, from_ahead)
    mod_grad = ring_sum(mod_grad, parts)
    mod_grad = (mod_grad + send(mod_grad, "z_lo")) * (1.0 / math.sqrt(clip_length))
    unit = (own.astype(F32) + from_behind.astype(F32) + from_ahead.astype(F32)).astype(BF16)
    weight_grad = finish_weight(unit, z_lo, dp, core)
    weight_grad = weight_grad * (1.0 / math.sqrt(all_length))
    return (attention.T[None], grad_tokens.T[None], weight_grad, mod_grad[None])


def solution(mesh):
    return jax.shard_map(
        body,
        mesh=mesh,
        in_specs=(P("dp", "seq", None), P("dp", None, None), P("seq", "dp"), P("dp", "seq", None)),
        out_specs=(P("dp", "seq", None), P("dp", "seq", None), P("seq", "dp"), P("dp", None, None)),
        check_vma=False,
    )
```
